128 devices in a mesh: seq: 32 (over y, z_lo, x), batch: 4 (over z_hi, core).
Axes of the slice: x: 4, y: 4, z: 4 (z_hi: 2, z_lo: 2; z = z_hi * 2 + z_lo), core: 2. Of those that a mesh axis runs over, the one named last changes fastest.
Arguments:
- tokens: bfloat16 [4, 8192, 768], P('batch', 'seq'), may hold values from -6 to 6
- token_pos: int32 [4, 8192], P('batch', 'seq'), may hold values from 0 to 4095, as said below
- token_pass: int32 [4, 8192], P('batch', 'seq'), may hold values from 0 to 4, as said below
- token_count: int32 [4, 8192], P('batch', 'seq'), may hold values from 2 to 5, as said below
- w_qkv: bfloat16 [768, 2304], replicated, may hold values from -0.21875 to 0.21875
- w_out: bfloat16 [768, 768], replicated, may hold values from -0.875 to 0.875
- w_up: bfloat16 [768, 3072], replicated, may hold values from -0.21875 to 0.21875
- w_down: bfloat16 [3072, 768], replicated, may hold values from -0.109375 to 0.109375
- gain_attn: float32 [768], replicated, may hold values from 0.5 to 1.5
- gain_mlp: float32 [768], replicated, may hold values from 0.5 to 1.5
- pass_table: float32 [5, 768], replicated, may hold values from -3 to 3
- cotangent: bfloat16 [4, 8192, 768], P('batch', 'seq'), may hold values from -6 to 6
Outputs:
- mixed: bfloat16 [4, 8192, 768], P('batch', 'seq')
- grad_tokens: float32 [4, 8192, 768], P('batch', 'seq')
- grad_qkv: float32 [768, 2304], replicated
- grad_out: float32 [768, 768], replicated
- grad_up: float32 [768, 3072], replicated
- grad_down: float32 [3072, 768], replicated
- grad_gain_attn: float32 [768], replicated
- grad_gain_mlp: float32 [768], replicated
- grad_pass_table: float32 [5, 768], replicated
The draws below stay inside these ranges and needn't reach their ends.
Inputs may be any that keep to these rules, and one draw needn't show every extreme that they name: `token_pos`: A stream holds three documents end to end; the middle one begins on the first 256 tokens and ends in the last 256. Inside a document of c passes, the token at position p and pass r stands p * c + r places after its first token; only a document's last position may hold fewer than c passes. `token_pass`: the pass number of a token in its document. `token_count`: equal for all tokens of one document; every stream has a document of 2 and one of 5 passes.
All inputs are finite; a program needn't handle non-finite values.
Results may differ from the reference program's by a relative error of at most 0.018.
Values may be sent and summed in bfloat16 or wider, within the bound.
No kernel may reach another device: no remote copies, remote signals or barrier semaphores. Data moves between devices by JAX's collectives and lax.ppermute only.
A program may use at most 320 MiB of HBM per device.

```python
import math
import jax
import jax.numpy as jnp
from jax import lax

D = 768
FF = 3072
HEADS = 12
HEAD_DIM = 64
PASSES = 5
TOK_DEV = 256
STREAM = 8192
STREAMS = 4


def doc_layout(key):
    stream_keys = jax.random.split(key, STREAMS)

    def single_stream(stream_key):
        parts = jax.random.split(stream_key, 4)
        swapped = jax.random.randint(parts[0], (), 0, 2)
        count_first = 2 + 3 * swapped
        count_last = 5 - 3 * swapped
        count_mid = jax.random.randint(parts[1], (), 2, 6)
        base_first = 1 + jax.random.randint(parts[2], (), 0, max(TOK_DEV // 10, 1))
        len_first = base_first * count_first
        len_last = 5 + jax.random.randint(parts[3], (), 0, max(TOK_DEV // 3, 1))
        len_mid = STREAM - len_first - len_last
        places = jnp.arange(STREAM, dtype=jnp.int32)
        in_second = places >= len_first
        in_third = places >= len_first + len_mid
        doc_start = jnp.where(in_third, len_first + len_mid, jnp.where(in_second, len_first, 0))
        doc_count = jnp.where(in_third, count_last, jnp.where(in_second, count_mid, count_first))
        offset = places - doc_start
        return ((offset // doc_count).astype(jnp.int32), (offset % doc_count).astype(jnp.int32), doc_count.astype(jnp.int32))
    return jax.vmap(single_stream)(stream_keys)


def draw_token_pos(key, part):
    shared = doc_layout(key)
    return shared[0]


def draw_token_pass(key, part):
    shared = doc_layout(key)
    return shared[1]


def draw_token_count(key, part):
    shared = doc_layout(key)
    return shared[2]


def level_of(own_key, shape, shards, smallest, high):
    loudness, own = 1.0, jax.random.fold_in(own_key, 6)
    for axis_at, blocks in shards:
        heights = jnp.exp(jax.random.uniform(jax.random.fold_in(own, axis_at), (blocks,), jnp.float32, smallest / len(shards), high / len(shards)))
        loudness = loudness * jnp.repeat(heights, shape[axis_at] // blocks).reshape([-1 if axis == axis_at else 1 for axis in range(len(shape))])
    return loudness


def centred(rng, extent, deviation, most, shards=(), held_as=jnp.bfloat16):
    factor_of = level_of(rng, extent, shards, -0.22, 0.18) if shards else 1.0
    entries = jax.random.normal(rng, extent, jnp.float32) * deviation * factor_of
    return jnp.minimum(jnp.maximum(entries, -most), most).astype(held_as)


def setup_inputs(seed: int = 0) -> dict:
    keys = jax.random.split(jax.random.key(seed), 13)
    tokens = centred(keys[0], (STREAMS, STREAM, D), 1.0, 6.0, ((0, 4), (1, 32)))
    token_pos = draw_token_pos(jax.random.fold_in(keys[12], 71), 0)
    token_pass = draw_token_pass(jax.random.fold_in(keys[12], 71), 0)
    token_count = draw_token_count(jax.random.fold_in(keys[12], 71), 0)
    w_qkv = centred(keys[4], (D, 3 * D), D ** -0.5, 0.21875)
    w_out = centred(keys[5], (D, D), (D // 16) ** -0.5, 0.875)
    w_up = centred(keys[6], (D, FF), D ** -0.5, 0.21875)
    w_down = centred(keys[7], (FF, D), FF ** -0.5, 0.109375)
    gain_attn = jnp.clip(1.0 + 0.1 * jax.random.normal(keys[8], (D,), jnp.float32), 0.5, 1.5)
    gain_mlp = jnp.clip(1.0 + 0.1 * jax.random.normal(keys[9], (D,), jnp.float32), 0.5, 1.5)
    pass_table = centred(keys[10], (PASSES, D), 0.5, 3.0, (), jnp.float32)
    cotangent = centred(keys[11], (STREAMS, STREAM, D), 1.0, 6.0, ((0, 4), (1, 32)))
    return dict(tokens=tokens, token_pos=token_pos, token_pass=token_pass, token_count=token_count, w_qkv=w_qkv, w_out=w_out, w_up=w_up, w_down=w_down, gain_attn=gain_attn, gain_mlp=gain_mlp, pass_table=pass_table, cotangent=cotangent)


@jax.custom_vjp
def low(v):
    return lax.optimization_barrier(v.astype(jnp.bfloat16)).astype(jnp.float32)

@jax.custom_vjp
def low_back(v):
    return v

def low_keep(v):
    return (low(v), None)

def low_pass(kept, grad):
    return (grad,)

def back_keep(v):
    return (v, None)

def back_low(kept, grad):
    return (low(grad),)
low.defvjp(low_keep, low_pass)
low_back.defvjp(back_keep, back_low)

def norm_rows(values, gain):
    row_mean = lax.optimization_barrier(jnp.mean(values, axis=-1, keepdims=True))
    centered = values - row_mean
    variance = lax.optimization_barrier(jnp.mean(centered * centered, axis=-1, keepdims=True))
    return centered * lax.rsqrt(variance + 1e-05) * gain

def attend(queries, keys_all, values_all, first_keys):
    length = queries.shape[0]
    row_block = math.gcd(length, 512)
    block_count = length // row_block
    keys_at = jnp.arange(length, dtype=jnp.int32)
    scale = HEAD_DIM ** (-0.5)
    precise = lax.Precision.HIGHEST

    def one_block(inputs):
        query_rows, first_rows, block_start = inputs
        rows_at = block_start + jnp.arange(row_block, dtype=jnp.int32)
        raw_scores = jnp.einsum('qhe,khe->hqk', query_rows, keys_all, precision=precise)
        scores = low_back(raw_scores) * scale
        allowed = (keys_at[None, :] >= first_rows[:, None]) & (keys_at[None, :] <= rows_at[:, None])
        masked = jnp.where(allowed[None], scores, -1e+30)
        row_top = lax.optimization_barrier(jnp.max(masked, axis=-1, keepdims=True))
        weights = jnp.where(allowed[None], jnp.exp(masked - row_top), 0.0)
        row_total = lax.optimization_barrier(jnp.sum(weights, axis=-1))
        summed = jnp.einsum('hqk,khe->qhe', low(weights), values_all, precision=precise)
        return summed / jnp.transpose(row_total)[:, :, None]
    blocks = (queries.reshape(block_count, row_block, HEADS, HEAD_DIM), first_keys.reshape(block_count, row_block), jnp.arange(block_count, dtype=jnp.int32) * row_block)
    result = lax.map(jax.checkpoint(one_block), blocks)
    return result.reshape(length, D)

def block(stream_in, first_keys, w_qkv, w_out, w_up, w_down, gain_attn, gain_mlp):
    length = stream_in.shape[0]
    precise = lax.Precision.HIGHEST
    normed = low(norm_rows(stream_in, gain_attn))
    projected = jnp.dot(normed, w_qkv, precision=precise)
    queries = low(low_back(projected[:, :D])).reshape(length, HEADS, HEAD_DIM)
    keys_all = low(low_back(projected[:, D:2 * D])).reshape(length, HEADS, HEAD_DIM)
    values_all = low(low_back(projected[:, 2 * D:])).reshape(length, HEADS, HEAD_DIM)
    attended = low(low_back(attend(queries, keys_all, values_all, first_keys)))
    resid_mid = stream_in + low_back(jnp.dot(attended, w_out, precision=precise))
    hidden = jnp.dot(low(norm_rows(resid_mid, gain_mlp)), w_up, precision=precise)
    activated = low(jax.nn.gelu(low_back(hidden), approximate=True))
    return resid_mid + low_back(jnp.dot(activated, w_down, precision=precise))

def forward(tokens, w_qkv, w_out, w_up, w_down, gain_attn, gain_mlp, pass_table, first_key, token_pass):

    def per_stream(inputs):
        stream_in, first_keys, passes = inputs
        first_out = block(stream_in, first_keys, w_qkv, w_out, w_up, w_down, gain_attn, gain_mlp)
        pass_onehot = (passes[:, None] == jnp.arange(PASSES, dtype=jnp.int32)[None, :]).astype(first_out.dtype)
        second_in = first_out + jnp.dot(pass_onehot, pass_table, precision=lax.Precision.HIGHEST)
        return block(second_in, first_keys, w_qkv, w_out, w_up, w_down, gain_attn, gain_mlp)
    return lax.map(per_stream, (tokens, first_key, token_pass))

def reference(tokens, token_pos, token_pass, token_count, w_qkv, w_out, w_up, w_down, gain_attn, gain_mlp, pass_table, cotangent):
    places = jnp.arange(tokens.shape[1], dtype=jnp.int32)[None, :]
    first_key = (places - (token_pos * token_count + token_pass)).astype(jnp.int32)

    def wrapped(tokens_in, qkv_in, out_in, up_in, down_in, gain_one, gain_two, table_in):
        return forward(tokens_in, qkv_in, out_in, up_in, down_in, gain_one, gain_two, table_in, first_key, token_pass)
    result, pullback = jax.vjp(wrapped, tokens.astype(jnp.float32), w_qkv.astype(jnp.float32), w_out.astype(jnp.float32), w_up.astype(jnp.float32), w_down.astype(jnp.float32), gain_attn.astype(jnp.float32), gain_mlp.astype(jnp.float32), pass_table.astype(jnp.float32))
    gradients = pullback(cotangent.astype(jnp.float32))
    return (result.astype(jnp.bfloat16), gradients[0], gradients[1], gradients[2], gradients[3], gradients[4], gradients[5], gradients[6], gradients[7])
```

```python
import functools

import jax
import jax.numpy as jnp
from jax import lax
from jax.experimental import pallas as pl
from jax.experimental.pallas import tpu as pltpu
from jax.sharding import PartitionSpec as P

HEADS = 12
HEAD_DIM = 64
PASSES = 5
SEQ = 32
ROWS = 256
HALF = 128
SLOT = ROWS + 64 + 16
WIDTH = 768
FF = 3072
FF_BLOCK = 512
EPS = 1e-5
LOG2E = 1.4426950408889634
LOW = -1e30
F32 = jnp.float32
BF16 = jnp.bfloat16

WORK = [3 * (e // 4) + e % 4 if e % 4 < 3 else None for e in range(SEQ)]
SLOT_OF = {w: e for e, w in enumerate(WORK) if w is not None}


def dot(left, right):
    return jnp.dot(left, right, preferred_element_type=F32)


def contract_rows(left, right):
    return lax.dot_general(left, right, (((0,), (0,)), ((), ())), preferred_element_type=F32)


def times_transposed(left, right):
    return lax.dot_general(left, right, (((1,), (1,)), ((), ())), preferred_element_type=F32)


def standardise(values):
    centered = values - jnp.mean(values, axis=-1, keepdims=True)
    inverse = lax.rsqrt(jnp.mean(centered * centered, axis=-1, keepdims=True) + EPS)
    return centered * inverse, inverse


def standardise_back(grad, gain, values):
    normal, inverse = standardise(values)
    scaled = grad * gain
    along = jnp.mean(scaled * normal, axis=-1, keepdims=True)
    grad_values = inverse * (scaled - jnp.mean(scaled, axis=-1, keepdims=True) - normal * along)
    return grad_values, jnp.sum(grad * normal, axis=0, keepdims=True)


GELU_A = 0.7978845608028654
GELU_B = 0.044715


def gelu(value):
    return 0.5 * value * (1.0 + jnp.tanh(GELU_A * (value + GELU_B * value * value * value)))


def gelu_slope(value):
    square = value * value
    bent = jnp.tanh(GELU_A * value * (1.0 + GELU_B * square))
    inner = GELU_A * (1.0 + 3.0 * GELU_B * square)
    return 0.5 * (1.0 + bent) + 0.5 * value * (1.0 - bent * bent) * inner


def slot_of(head, block, odd):
    this, other = SLOT_OF[2 * head + block], SLOT_OF[2 * head + 1 - block]
    return jnp.where(odd == 1, other, this)


class Held:
    def __init__(self, source, target, sem):
        self.target = target
        self.copy = pltpu.make_async_copy(source, target, sem)
        self.copy.start()
        self.waited = False

    def ready(self):
        if not self.waited:
            self.copy.wait()
            self.waited = True
        return self.target

    def __getitem__(self, at):
        return self.ready()[at]


class Kept:
    def __init__(self, source, target, sem):
        self.source = source
        self.copy = pltpu.make_async_copy(source, target, sem)
        self.started = False

    def __getitem__(self, at):
        return self.source[at]

    def __setitem__(self, at, value):
        self.source[at] = value

    def flush(self):
        self.copy.start()
        self.started = True

    def finish(self):
        if not self.started:
            self.flush()
        self.copy.wait()


def project(stream, gain, w_qkv, odd, third, slots, normed_out):
    normed = (standardise(stream)[0] * gain).astype(BF16)
    normed_out[...] = normed
    low_lanes = lax.broadcasted_iota(jnp.int32, (ROWS, 128), 1) < 64
    for pair in range(HEADS // 2):
        at = 128 * pair
        queries = dot(normed, w_qkv[:, at : at + 128]) * HEAD_DIM**-0.5
        keys = dot(normed, w_qkv[:, WIDTH + at : WIDTH + at + 128])
        values = dot(normed, w_qkv[:, 2 * WIDTH + at : 2 * WIDTH + at + 128])
        queries_t = queries.T.astype(BF16)
        first = jnp.where(low_lanes, keys, pltpu.roll(values, 64, 1)).astype(BF16)
        second = jnp.where(low_lanes, pltpu.roll(keys, 64, 1), values).astype(BF16)
        for j, both in enumerate((first, second)):
            head = 2 * pair + j
            for block in range(2):
                to = slot_of(head, block, odd)
                slots[to, 0:ROWS, :] = both
                slots[to, ROWS : ROWS + 64, :] = queries_t[
                    64 * j : 64 * j + 64, block * HALF : (block + 1) * HALF
                ]
                slots[to, ROWS + 64 : SLOT, :] = jnp.broadcast_to(third, (16, 128)).astype(BF16)


def gather_heads(recv, odd, row, target):
    for head in range(HEADS):
        for block in range(2):
            target[64 * head : 64 * head + 64, block * HALF : (block + 1) * HALF] = recv[
                slot_of(head, block, odd), row : row + 64, :
            ]


def scatter_heads(features, odd, slots):
    for head in range(HEADS):
        for block in range(2):
            slots[slot_of(head, block, odd)] = features[
                64 * head : 64 * head + 64, block * HALF : (block + 1) * HALF
            ]


def mix(recv, stream, odd, gain, weights, features, acc, att_out, mid_out, normed_out, hidden_out, act_out):
    gather_heads(recv, odd, 0, features)
    attended = features[...].T
    att_out[...] = attended
    mid = stream + dot(attended, weights[0][...])
    mid_out[...] = mid
    normed_out[...] = (standardise(mid)[0] * gain).astype(BF16)
    acc[...] = mid
    up, down = weights[1].ready(), weights[2].ready()

    def step(c, _):
        here = pl.ds(pl.multiple_of(c * FF_BLOCK, FF_BLOCK), FF_BLOCK)
        hidden = dot(normed_out[...], up[:, here])
        hidden_out[:, here] = hidden
        active = gelu(hidden).astype(BF16)
        act_out[:, here] = active
        acc[...] += dot(active, down[here, :])
        return 0

    lax.fori_loop(0, FF // FF_BLOCK, step, 0)


def mix_back(grad, odd, gain, mid, hidden, weights, acc, dz_out, dh_out, dy_out, dmid_out, gain_out, slots):
    out, up, down = weights
    up, down = up.ready(), down.ready()
    dz_out[...] = grad.astype(BF16)
    acc[...] = jnp.zeros(acc.shape, F32)

    def step(c, _):
        here = pl.ds(pl.multiple_of(c * FF_BLOCK, FF_BLOCK), FF_BLOCK)
        grad_act = times_transposed(dz_out[...], down[here, :])
        low = (gelu_slope(hidden[:, here]) * grad_act).astype(BF16)
        dh_out[:, here] = low
        acc[...] += times_transposed(low, up[:, here])
        return 0

    lax.fori_loop(0, FF // FF_BLOCK, step, 0)
    grad_mid, grad_gain = standardise_back(acc[...], gain, mid[...])
    gain_out[...] = grad_gain
    grad_mid = grad_mid + grad
    dmid_out[...] = grad_mid
    for done in (dh_out, dmid_out, dz_out):
        if isinstance(done, Kept):
            done.flush()
    low = grad_mid.astype(BF16)
    dy_out[...] = low
    scatter_heads(times_transposed(low, out[...]).T.astype(BF16), odd, slots)


def project_back(recv, odd, gain, stream, grad_mid, w_qkv, features, dproj_out, gain_out):
    gather_heads(recv, odd, ROWS, features)
    dproj_out[:, 0:WIDTH] = features[...].T
    low_lanes = lax.broadcasted_iota(jnp.int32, (ROWS, 128), 1) < 64
    for pair in range(HEADS // 2):
        at = 128 * pair
        both = []
        for head in (2 * pair, 2 * pair + 1):
            one, two = recv[SLOT_OF[2 * head], 0:ROWS, :], recv[SLOT_OF[2 * head + 1], 0:ROWS, :]
            both.append(one.astype(F32) + two.astype(F32))
        keys = jnp.where(low_lanes, both[0], pltpu.roll(both[1], 64, 1)).astype(BF16)
        values = jnp.where(low_lanes, pltpu.roll(both[0], 64, 1), both[1]).astype(BF16)
        dproj_out[:, WIDTH + at : WIDTH + at + 128] = keys
        dproj_out[:, 2 * WIDTH + at : 2 * WIDTH + at + 128] = values
    grad_normed = times_transposed(dproj_out[...], w_qkv[...])
    grad_stream, grad_gain = standardise_back(grad_normed, gain, stream[...].astype(F32))
    gain_out[...] = grad_gain
    return grad_stream + grad_mid[...]


def enter_kernel(info, gain_attn, ins, outs):
    tokens, w_qkv = ins
    slots, normed = outs
    project(tokens[...].astype(F32), gain_attn[...], w_qkv, info[3], info[4].astype(F32), slots, normed)


def turn_kernel(info, passes, table, gain_attn, gain_mlp, ins, outs, features, acc):
    recv, tokens, w_out, w_up, w_down, w_qkv = ins
    slots, normed, second, att, mid, mid_normed, hidden, act = outs
    odd = info[3]
    mix(recv, tokens[...].astype(F32), odd, gain_mlp[...], (w_out, w_up, w_down), features, acc, att, mid, mid_normed, hidden, act)
    for out in (att, mid, mid_normed, hidden, act):
        out.flush()
    stream = acc[...]
    for row in range(PASSES):
        stream = stream + jnp.where(passes[...] == row, table[row : row + 1, :], 0.0)
    second[...] = stream
    second.flush()
    project(stream, gain_attn[...], w_qkv, odd, info[4].astype(F32), slots, normed)


def crest_kernel(info, gain_mlp, ins, outs, features, acc, mid, hidden, dz):
    recv, stream, w_out, w_up, w_down, cotangent = ins
    slots, mixed, att, mid_normed, act, dh, dy, dmid, gain_out = outs
    odd = info[3]
    gain = gain_mlp[...]
    mix(recv, stream[...], odd, gain, (w_out, w_up, w_down), features, acc, att, mid, mid_normed, hidden, act)
    mixed[...] = acc[...].astype(BF16)
    for out in (att, mid_normed, act, mixed):
        out.flush()
    mix_back(cotangent[...].astype(F32), odd, gain, mid, hidden, (w_out, w_up, w_down), acc, dz, dh, dy, dmid, gain_out, slots)


def return_kernel(info, passes, gain_attn, gain_mlp, ins, outs, features, acc):
    recv, w_qkv, stream, grad_mid, w_down, hidden, w_up, mid, w_out = ins
    slots, dproj, gain_attn_out, table_out, dz, dh, dy, dmid, gain_mlp_out = outs
    odd = info[3]
    grad = project_back(recv, odd, gain_attn[...], stream, grad_mid, w_qkv, features, dproj, gain_attn_out)
    dproj.flush()
    for row in range(PASSES):
        table_out[row : row + 1, :] = jnp.sum(jnp.where(passes[...] == row, grad, 0.0), axis=0, keepdims=True)
    table_out[PASSES:8, :] = jnp.zeros((8 - PASSES, WIDTH), F32)
    mix_back(grad, odd, gain_mlp[...], mid, hidden.ready(), (w_out, w_up, w_down), acc, dz, dh, dy, dmid, gain_mlp_out, slots)


def leave_kernel(info, gain_attn, ins, outs, features):
    recv, w_qkv, tokens, grad_mid = ins
    grad_tokens, dproj, gain_out = outs
    grad_tokens[...] = project_back(recv, info[3], gain_attn[...], tokens, grad_mid, w_qkv, features, dproj, gain_out)


def shape(*dims, dtype=BF16):
    return jax.ShapeDtypeStruct(dims, dtype)


def in_vmem(kernel, name, info, small, arrays, outs, scratch, flops):
    vmem = pl.BlockSpec(memory_space=pltpu.VMEM)
    hbm = pl.BlockSpec(memory_space=pl.ANY)
    ins, count = len(arrays), len(arrays) + len(outs)

    def body(info, *refs):
        few, refs = refs[: len(small)], refs[len(small) :]
        far, near, sems, rest = refs[:count], refs[count : 2 * count], refs[2 * count], refs[2 * count + 1 :]
        held = [Held(far[i], near[i], sems.at[i]) for i in range(ins)]
        kept = [Kept(near[i], far[i], sems.at[i]) for i in range(ins, count)]
        kernel(info, *few, held, kept, *rest)
        for one in kept:
            if not one.started:
                one.flush()
        for one in held:
            one.ready()
        for one in kept:
            one.finish()

    return pl.pallas_call(
        body,
        out_shape=tuple(outs),
        in_specs=[pl.BlockSpec(memory_space=pltpu.SMEM)] + [vmem] * len(small) + [hbm] * ins,
        out_specs=(hbm,) * len(outs),
        scratch_shapes=[pltpu.VMEM(x.shape, x.dtype) for x in (*arrays, *outs)]
        + [pltpu.SemaphoreType.DMA((count,))]
        + scratch,
        compiler_params=pltpu.CompilerParams(vmem_limit_bytes=56 << 20),
        cost_estimate=pl.CostEstimate(flops=int(flops), bytes_accessed=16 << 20, transcendentals=1 << 20),
        name=name,
    )(info, *small, *arrays)


EARLY = 21504
LATE = 7680
CORE = 5


def grads_kernel(info, small, ins, outs):
    mid_one, dh_one, mid_two, dh_two, act_one, dz_one, act_two, dz_two, att_one, dy_one, att_two, dy_two = ins
    core = info[CORE]

    def left(one, two):
        return jnp.concatenate([one, two], axis=0).T

    def put(half, row, rows, value):
        for to, out in enumerate(outs):

            @pl.when((half ^ core) == to)
            def _():
                for i in range(value.shape[1] // 128):
                    out[pl.ds(row + i * rows, value.shape[0]), :] = value[:, 128 * i : 128 * i + 128]

    mid = left(mid_one[...], mid_two[...])
    dh_one.ready(), dh_two.ready()

    def up(c, _):
        here = pl.ds(pl.multiple_of(c * 512, 512), 512)
        right = jnp.concatenate([dh_one[:, here], dh_two[:, here]], axis=0)
        result = dot(mid, right).astype(BF16)
        row = pl.multiple_of(c * 1536, 512)
        put(0, row, 384, result[:384])
        put(1, row, 384, result[384:])
        return 0

    lax.fori_loop(0, 6, up, 0)
    dz = jnp.concatenate([dz_one[...], dz_two[...]], axis=0)
    act_one.ready(), act_two.ready()

    def down(c, _):
        here = pl.ds(pl.multiple_of(c * 512, 512), 512)
        result = dot(left(act_one[:, here], act_two[:, here]), dz).astype(BF16)
        put(c // 3, pl.multiple_of(9216 + (c % 3) * 512, 512), 1536, result)
        return 0

    lax.fori_loop(0, 6, down, 0)
    dy = jnp.concatenate([dy_one[...], dy_two[...]], axis=0)
    result = dot(left(att_one[...], att_two[...]), dy).astype(BF16)
    put(0, 18432, 384, result[:384])
    put(1, 18432, 384, result[384:])
    for out in outs:
        out[20736:20784, :] = small[...].astype(BF16)


def grad_qkv_kernel(info, ins, outs):
    normed, dproj = ins
    left = normed[...].T
    dproj.ready()

    def step(c, _):
        result = dot(left, dproj[:, pl.ds(pl.multiple_of(c * 384, 384), 384)])
        for i in range(3):
            outs[0][3 * c + i] = result[:, 128 * i : 128 * i + 128]
        return 0

    lax.fori_loop(0, 6, step, 0)


def grad_qkv_both_kernel(info, gains, ins, outs):
    normed, dproj, before = ins
    left = normed[...].T
    dproj.ready(), before.ready()
    core = info[CORE]

    def step(c, _):
        result = dot(left, dproj[:, pl.ds(pl.multiple_of(c * 384, 384), 384)])
        for to, out in enumerate(outs):

            @pl.when(core == to)
            def _():
                for i in range(3):
                    part = (result[:384, 128 * i : 128 * i + 128] + before[3 * c + i, :384, :]).astype(BF16)
                    out[pl.ds(pl.multiple_of((3 * c + i) * 384, 384), 384), :] = part

            @pl.when(core != to)
            def _():
                for i in range(3):
                    part = (result[384:, 128 * i : 128 * i + 128] + before[3 * c + i, 384:, :]).astype(BF16)
                    out[pl.ds(pl.multiple_of((3 * c + i) * 384, 384), 384), :] = part

        return 0

    lax.fori_loop(0, 6, step, 0)
    for out in outs:
        out[6912:6928, :] = gains[...].astype(BF16)


def widen_kernel(core, mine, other, out):
    half = pl.program_id(0) // 3

    def put(ref):
        for i in range(ref.shape[0]):
            out[:, 128 * i : 128 * i + 128] = ref[i].astype(F32)

    @pl.when(half == core[0])
    def _():
        put(mine)

    @pl.when(half != core[0])
    def _():
        put(other)


def widen(core, mine, other, columns, height, first):
    def place(own):
        def index(i, core):
            low = core[0] == (0 if own else 1)
            part = jnp.where(low, jnp.minimum(i, 2), jnp.maximum(i - 3, 0))
            return (first // columns, part, 0)

        return pl.BlockSpec((columns, height // 3, 128), index)

    return pl.pallas_call(
        widen_kernel,
        out_shape=shape(2 * height, columns * 128, dtype=F32),
        grid_spec=pltpu.PrefetchScalarGridSpec(
            num_scalar_prefetch=1,
            grid=(6,),
            in_specs=[place(True), place(False)],
            out_specs=pl.BlockSpec((height // 3, columns * 128), lambda i, core: (i, 0)),
        ),
        compiler_params=pltpu.CompilerParams(vmem_limit_bytes=20 << 20),
        name="widen",
    )(core, mine.reshape(-1, height, 128), other.reshape(-1, height, 128))


def swap(value, bit):
    return lax.ppermute(value, "batch", [(i, i ^ bit) for i in range(4)])


def exchange(slots):
    return lax.all_to_all(slots, "seq", 0, 0)


def sum_cores(partial):
    mine, other = partial
    return (mine.astype(F32) + swap(other, 1).astype(F32)).astype(BF16)


def deal(half):
    return exchange(half.reshape(SEQ, half.shape[0] // SEQ, 128))


def sum_chips(blocks):
    block = jnp.sum(blocks.astype(F32), axis=0).astype(BF16)
    return (block.astype(F32) + swap(block, 2).astype(F32)).astype(BF16)


def spread(block):
    whole = exchange(jnp.broadcast_to(block[None], (SEQ, *block.shape))).reshape(-1, 128)
    return whole, swap(whole, 1)


def positions(half, first_row, count):
    at = lax.broadcasted_iota(jnp.int32, (1, count), 1)
    block = at // HALF
    return first_row + block * ROWS + ((half + block) % 2) * HALF + at % HALF


def third_keys(recv, count):
    last = recv[SEQ - 1, ROWS + 64 : SLOT, :].astype(F32)[0:1].astype(jnp.int32)
    row = last + (SEQ - 1) * ROWS
    return jnp.concatenate([row] * (count // 128), axis=1)


def first_keys(at, second, third):
    return jnp.where(at < second, 0, jnp.where(at < third, second, third))


def attend_kernel(info, recv_far, out_low_far, out_f_far, lse_far, kv_t_far, q_t_far, recv, out_low, out_f, lse, kv_t, q_t, sems, top, acc, *, devs):
    tile_rows = devs * HALF
    span = devs * ROWS
    active, half, second = info[0], info[1], info[2]

    @pl.when(active == 1)
    def _():
        parts = [
            Held(recv_far.at[8 * i : 8 * i + 8], recv.at[8 * i : 8 * i + 8], sems.at[i]) for i in range(4)
        ]
        fars = (kv_t_far, q_t_far, out_low_far, out_f_far, lse_far)
        kept = [
            Kept(near, far, sems.at[4 + i])
            for i, (near, far) in enumerate(zip((kv_t, q_t, out_low, out_f, lse), fars))
        ]
        ones = (lax.broadcasted_iota(jnp.int32, (16, ROWS), 0) == 0).astype(BF16)
        for d in range(SEQ):
            parts[d // 8].ready()
            keys = slice(d * ROWS, (d + 1) * ROWS)
            kv_t[0:128, keys] = recv[d, 0:ROWS, :].T
            kv_t[128:144, keys] = ones
            q_t[0:64, d * HALF : (d + 1) * HALF] = recv[d, ROWS : ROWS + 64, :]
        q_t[64:128, :] = jnp.zeros((64, SEQ * HALF), BF16)
        kept[0].flush()
        kept[1].flush()

        third = third_keys(recv, tile_rows)

        def one_tile(t, _):
            start = t * span
            columns = pl.ds(pl.multiple_of(t * tile_rows, tile_rows), tile_rows)
            at = positions(half, start, tile_rows)
            first = first_keys(at, second, third)
            top[...] = jnp.full((1, tile_rows), LOW, F32)
            acc[...] = jnp.zeros((80, tile_rows), F32)
            queries = q_t[:, columns]

            def update(scores, key_rows, left):
                here = slice(left, tile_rows)
                old_top = top[:, here]
                new_top = jnp.maximum(old_top, jnp.max(scores, axis=0, keepdims=True))
                weights = jnp.exp2(scores - new_top).astype(BF16)
                shrink = jnp.exp2(old_top - new_top)
                acc[:, here] = acc[:, here] * shrink + dot(kv_t[64:144, key_rows], weights)
                top[:, here] = new_top

            def whole(j, masked):
                key_start = pl.multiple_of(j * 1024, 1024)
                kv = recv[pl.ds(j * 4, 4), 0:ROWS, :].reshape(1024, 128)
                scores = dot(kv, queries) * LOG2E
                if masked:
                    key_at = lax.broadcasted_iota(jnp.int32, (1024, 1), 0)
                    scores = jnp.where(key_at >= second, scores, LOW)
                update(scores, pl.ds(key_start, 1024), 0)

            @pl.when(t > 0)
            def _():
                whole(0, True)

            def step(j, _):
                whole(j, False)
                return 0

            lax.fori_loop(1, t * (span // 1024), step, 0)
            fresh = first >= start
            top[...] = jnp.where(fresh, LOW, top[...])
            acc[...] = jnp.where(fresh, 0.0, acc[...])
            for i in range(devs // 2):
                left = 256 * i
                key_start = pl.multiple_of(start + 512 * i, 512)
                kv = recv[pl.ds(t * devs + 2 * i, 2), 0:ROWS, :].reshape(512, 128)
                scores = dot(kv, queries[:, left:]) * LOG2E
                key_at = key_start + lax.broadcasted_iota(jnp.int32, (512, 1), 0)
                allowed = (key_at >= first[:, left:]) & (key_at <= at[:, left:])
                update(jnp.where(allowed, scores, LOW), pl.ds(key_start, 512), left)
            total = acc[64:65, :]
            result = acc[0:64, :] / total
            out_f[:, columns] = result
            lse[:, columns] = top[...] + jnp.log2(total)
            low = result.astype(BF16)
            for i in range(devs):
                out_low[t * devs + i] = low[:, i * HALF : (i + 1) * HALF]
            return 0

        lax.fori_loop(0, SEQ // devs, one_tile, 0)
        for one in kept[2:]:
            one.flush()
        for one in kept:
            one.finish()


def attend(info, recv):
    devs = 8
    pairs = 17.8e6
    out_low, *rest = pl.pallas_call(
        functools.partial(attend_kernel, devs=devs),
        out_shape=(
            jax.ShapeDtypeStruct((SEQ, 64, HALF), BF16),
            jax.ShapeDtypeStruct((64, SEQ * HALF), F32),
            jax.ShapeDtypeStruct((1, SEQ * HALF), F32),
            jax.ShapeDtypeStruct((144, SEQ * ROWS), BF16),
            jax.ShapeDtypeStruct((128, SEQ * HALF), BF16),
        ),
        in_specs=[
            pl.BlockSpec(memory_space=pltpu.SMEM),
            pl.BlockSpec(memory_space=pl.ANY),
        ],
        out_specs=tuple(pl.BlockSpec(memory_space=pl.ANY) for _ in range(5)),
        scratch_shapes=[
            pltpu.VMEM((SEQ, SLOT, 128), BF16),
            pltpu.VMEM((SEQ, 64, HALF), BF16),
            pltpu.VMEM((64, SEQ * HALF), F32),
            pltpu.VMEM((1, SEQ * HALF), F32),
            pltpu.VMEM((144, SEQ * ROWS), BF16),
            pltpu.VMEM((128, SEQ * HALF), BF16),
            pltpu.SemaphoreType.DMA((9,)),
            pltpu.VMEM((1, devs * HALF), F32),
            pltpu.VMEM((80, devs * HALF), F32),
        ],
        compiler_params=pltpu.CompilerParams(vmem_limit_bytes=56 << 20),
        cost_estimate=pl.CostEstimate(
            flops=int(pairs * 1024), bytes_accessed=8 << 20, transcendentals=int(pairs)
        ),
        name="attend",
    )(info, recv)
    out_f, lse, kv_t, q_t = rest
    return out_low, recv, kv_t, q_t, out_f, lse


def attend_back_kernel(info, recv_far, kv_t_far, q_t_far, out_f_far, lse_far, grad_out_far, send_far, recv, kv_t, q_t, out_f, lse, grad_out, send, sems, grad_kv, do_t, grad_q, *, devs):
    tile_rows = devs * HALF
    span = devs * ROWS
    active, half, second = info[0], info[1], info[2]

    @pl.when(active == 1)
    def _():
        fars = (grad_out_far, recv_far, q_t_far, out_f_far, lse_far, kv_t_far)
        nears = (grad_out, recv, q_t, out_f, lse, kv_t)
        held = [Held(far, near, sems.at[i]) for i, (far, near) in enumerate(zip(fars, nears))]
        grad_kv[...] = jnp.zeros(grad_kv.shape, F32)
        held[0].ready()
        for d in range(SEQ):
            do_t[64:128, d * HALF : (d + 1) * HALF] = grad_out[d]
        do_t[0:64, :] = jnp.zeros((64, SEQ * HALF), BF16)
        for one in held:
            one.ready()

        third = third_keys(recv, tile_rows)

        def one_tile(t, _):
            start = t * span
            columns = pl.ds(pl.multiple_of(t * tile_rows, tile_rows), tile_rows)
            at = positions(half, start, tile_rows)
            first = first_keys(at, second, third)
            queries = q_t[:, columns]
            grads = do_t[:, columns]
            query_rows = queries.T
            grad_rows = grads.T
            delta = jnp.sum(
                grads[64:128, :].astype(F32) * out_f[:, columns], axis=0, keepdims=True
            )
            own_lse = lse[:, columns]
            far_lse = jnp.where(first >= start, -LOW, own_lse)
            grad_q[...] = jnp.zeros((64, tile_rows), F32)

            def update(kv, key_rows, left, row_lse, mask):
                here = slice(left, tile_rows)
                scores = dot(kv, queries[:, here]) * LOG2E
                probs = jnp.exp2(scores - row_lse[:, here])
                if mask is not None:
                    probs = jnp.where(mask, probs, 0.0)
                grad_probs = dot(kv, grads[:, here])
                grad_scores = (probs * (grad_probs - delta[:, here])).astype(BF16)
                grad_kv[key_rows, :] += dot(grad_scores, query_rows[here, :]) + dot(
                    probs.astype(BF16), grad_rows[here, :]
                )
                grad_q[:, here] += dot(kv_t[0:64, key_rows], grad_scores)

            def whole(j, masked):
                key_start = pl.multiple_of(j * 1024, 1024)
                kv = recv[pl.ds(j * 4, 4), 0:ROWS, :].reshape(1024, 128)
                mask = None
                if masked:
                    mask = lax.broadcasted_iota(jnp.int32, (1024, 1), 0) >= second
                update(kv, pl.ds(key_start, 1024), 0, far_lse, mask)

            @pl.when(t > 0)
            def _():
                whole(0, True)

            def step(j, _):
                whole(j, False)
                return 0

            lax.fori_loop(1, t * (span // 1024), step, 0)
            for i in range(devs // 2):
                left = 256 * i
                key_start = pl.multiple_of(start + 512 * i, 512)
                kv = recv[pl.ds(t * devs + 2 * i, 2), 0:ROWS, :].reshape(512, 128)
                key_at = key_start + lax.broadcasted_iota(jnp.int32, (512, 1), 0)
                allowed = (key_at >= first[:, left:]) & (key_at <= at[:, left:])
                update(kv, pl.ds(key_start, 512), left, own_lse, allowed)
            low = (grad_q[...] * HEAD_DIM**-0.5).astype(BF16)
            for i in range(devs):
                send[t * devs + i, ROWS:, :] = low[:, i * HALF : (i + 1) * HALF]
            return 0

        lax.fori_loop(0, SEQ // devs, one_tile, 0)
        for d in range(SEQ):
            send[d, 0:ROWS, :] = grad_kv[d * ROWS : (d + 1) * ROWS, :].astype(BF16)
        out = Kept(send, send_far, sems.at[6])
        out.finish()


def attend_back(info, recv, kv_t, q_t, out_f, lse, grad_out):
    devs = 4
    pairs = 17.8e6
    return pl.pallas_call(
        functools.partial(attend_back_kernel, devs=devs),
        out_shape=jax.ShapeDtypeStruct((SEQ, ROWS + 64, HALF), BF16),
        in_specs=[pl.BlockSpec(memory_space=pltpu.SMEM)]
        + [pl.BlockSpec(memory_space=pl.ANY)] * 6,
        out_specs=pl.BlockSpec(memory_space=pl.ANY),
        scratch_shapes=[
            pltpu.VMEM((SEQ, SLOT, 128), BF16),
            pltpu.VMEM((144, SEQ * ROWS), BF16),
            pltpu.VMEM((128, SEQ * HALF), BF16),
            pltpu.VMEM((64, SEQ * HALF), F32),
            pltpu.VMEM((1, SEQ * HALF), F32),
            pltpu.VMEM((SEQ, 64, HALF), BF16),
            pltpu.VMEM((SEQ, ROWS + 64, HALF), BF16),
            pltpu.SemaphoreType.DMA((7,)),
            pltpu.VMEM((SEQ * ROWS, 128), F32),
            pltpu.VMEM((128, SEQ * HALF), BF16),
            pltpu.VMEM((64, devs * HALF), F32),
        ],
        compiler_params=pltpu.CompilerParams(vmem_limit_bytes=56 << 20),
        cost_estimate=pl.CostEstimate(
            flops=int(pairs * 1024), bytes_accessed=8 << 20, transcendentals=int(pairs)
        ),
        name="attend_back",
    )(info, recv, kv_t, q_t, out_f, lse, grad_out)


def on_device(
    tokens,
    token_pos,
    token_pass,
    token_count,
    w_qkv,
    w_out,
    w_up,
    w_down,
    gain_attn,
    gain_mlp,
    pass_table,
    cotangent,
):
    here = lax.axis_index("seq")
    offset = token_pos[0] * token_count[0] + token_pass[0]
    first_token = here * ROWS - offset[0]
    last_token = here * ROWS + ROWS - 1 - offset[ROWS - 1]
    second = jnp.where(here == 0, last_token, first_token)
    third = last_token - (SEQ - 1) * ROWS
    third = jnp.where((third < 0) | (third > ROWS), ROWS, third)
    group, place = here // 4, here % 4
    active = (place < 3).astype(jnp.int32)
    core = lax.axis_index("batch") % 2
    info = jnp.stack([active, (3 * group + place) % 2, second, here % 2, third, core])
    passes = token_pass[0][:, None]
    table = jnp.pad(pass_table, ((0, 8 - PASSES), (0, 0)))
    gain_a, gain_m = gain_attn[None], gain_mlp[None]
    stream_one = tokens[0]
    features = pltpu.VMEM((WIDTH, ROWS), BF16)
    acc = pltpu.VMEM((ROWS, WIDTH), F32)
    square = shape(ROWS, WIDTH)
    wide = shape(ROWS, WIDTH, dtype=F32)
    row = shape(1, WIDTH, dtype=F32)
    sent = shape(SEQ, SLOT, 128)
    sent_back = shape(SEQ, 64, 128)

    slots, normed_one = in_vmem(
        enter_kernel, "enter", info, (gain_a,), (stream_one, w_qkv), (sent, square), [], 1e9
    )
    saved_one = attend(info, exchange(slots))
    slots, normed_two, stream_two, att_one, mid_one, midn_one, hidden_one, act_one = in_vmem(
        turn_kernel,
        "turn",
        info,
        (passes, table, gain_a, gain_m),
        (exchange(saved_one[0]), stream_one, w_out, w_up, w_down, w_qkv),
        (sent, square, wide, square, wide, square, shape(ROWS, FF, dtype=F32), shape(ROWS, FF)),
        [features, acc],
        3.6e9,
    )
    saved_two = attend(info, exchange(slots))
    slots, mixed, att_two, midn_two, act_two, dh_two, dy_two, dmid_two, gain_m_two = in_vmem(
        crest_kernel,
        "crest",
        info,
        (gain_m,),
        (exchange(saved_two[0]), stream_two, w_out, w_up, w_down, cotangent[0]),
        (sent_back, square, square, square, shape(ROWS, FF), shape(ROWS, FF), square, wide, row),
        [features, acc, acc, pltpu.VMEM((ROWS, FF), F32), pltpu.VMEM((ROWS, WIDTH), BF16)],
        5e9,
    )
    back = exchange(slots)
    recv = exchange(attend_back(info, *saved_two[1:], back))
    slots, dproj_two, gain_a_two, grad_table, dz_one, dh_one, dy_one, dmid_one, gain_m_one = in_vmem(
        return_kernel,
        "return",
        info,
        (passes, gain_a, gain_m),
        (recv, w_qkv, stream_two, dmid_two, w_down, hidden_one, w_up, mid_one, w_out),
        (
            sent_back,
            shape(ROWS, 3 * WIDTH),
            row,
            shape(8, WIDTH, dtype=F32),
            square,
            shape(ROWS, FF),
            square,
            wide,
            row,
        ),
        [features, acc],
        5e9,
    )
    back = exchange(slots)
    small = jnp.concatenate(
        [grad_table[:PASSES], gain_a_two, gain_m_one + gain_m_two, jnp.zeros((1, WIDTH), F32)]
    ).reshape(48, 128)
    early = in_vmem(
        grads_kernel,
        "grads",
        info,
        (small,),
        (midn_one, dh_one, midn_two, dh_two, act_one, dz_one, act_two, cotangent[0], att_one, dy_one, att_two, dy_two),
        (shape(EARLY, 128),) * 2,
        [],
        5.4e10,
    )
    early = sum_cores(early)
    back, early = lax.optimization_barrier((back, early))
    sent_one = attend_back(info, *saved_one[1:], back)
    sent_one, early = lax.optimization_barrier((sent_one, deal(early)))
    recv = exchange(sent_one)
    early = sum_chips(early)
    grad_tokens, dproj_one, gain_a_one = in_vmem(
        leave_kernel,
        "leave",
        info,
        (gain_a,),
        (recv, w_qkv, stream_one, dmid_one),
        (wide, shape(ROWS, 3 * WIDTH), row),
        [features],
        1e9,
    )
    (grad_two,) = in_vmem(
        grad_qkv_kernel,
        "grad_qkv_two",
        info,
        (),
        (normed_two, dproj_two),
        (shape(18, WIDTH, 128, dtype=F32),),
        [],
        9e8,
    )
    late = in_vmem(
        grad_qkv_both_kernel,
        "grad_qkv",
        info,
        (jnp.pad(gain_a_one.reshape(6, 128), ((0, 10), (0, 0))),),
        (normed_one, dproj_one, grad_two),
        (shape(LATE, 128),) * 2,
        [],
        9e8,
    )
    core = info[CORE : CORE + 1]
    early = spread(early)
    grad_down = widen(core, *early, 6, 1536, 6)
    grad_up = widen(core, *early, 24, 384, 0)
    grad_out = widen(core, *early, 6, 384, 48)
    late = sum_chips(deal(sum_cores(late)))
    late, grad_down, grad_up, grad_out = lax.optimization_barrier((late, grad_down, grad_up, grad_out))
    late = spread(late)
    tail = early[0][20736:20784].reshape(8, WIDTH).astype(F32)
    gain_a_sum = late[0][6912:6918].reshape(WIDTH).astype(F32)
    return (
        mixed[None],
        grad_tokens[None],
        widen(core, *late, 18, 384, 0),
        grad_out,
        grad_up,
        grad_down,
        tail[PASSES] + gain_a_sum,
        tail[PASSES + 1],
        tail[:PASSES],
    )


def solution(mesh):
    return jax.shard_map(
        on_device,
        mesh=mesh,
        in_specs=(
            P("batch", "seq", None),
            P("batch", "seq"),
            P("batch", "seq"),
            P("batch", "seq"),
            P(),
            P(),
            P(),
            P(),
            P(),
            P(),
            P(),
            P("batch", "seq", None),
        ),
        out_specs=(
            P("batch", "seq", None),
            P("batch", "seq", None),
            P(),
            P(),
            P(),
            P(),
            P(),
            P(),
            P(),
        ),
        check_vma=False,
    )
```

```python
import functools

import jax
import jax.numpy as jnp
from jax import lax
from jax.experimental import pallas as pl
from jax.experimental.pallas import tpu as pltpu
from jax.sharding import PartitionSpec as P

HEADS = 12
HEAD_DIM = 64
PASSES = 5
SEQ = 32
ROWS = 256
HALF = 128
SLOT = ROWS + 64 + 16
WIDTH = 768
FF = 3072
FF_BLOCK = 512
EPS = 1e-5
LOG2E = 1.4426950408889634
LOW = -1e30
SMALL = 60.0
F32 = jnp.float32
BF16 = jnp.bfloat16

WORK = [3 * (e // 4) + e % 4 if e % 4 < 3 else None for e in range(SEQ)]
SLOT_OF = {w: e for e, w in enumerate(WORK) if w is not None}


def dot(left, right):
    return jnp.dot(left, right, preferred_element_type=F32)


def contract_rows(left, right):
    return lax.dot_general(left, right, (((0,), (0,)), ((), ())), preferred_element_type=F32)


def times_transposed(left, right):
    return lax.dot_general(left, right, (((1,), (1,)), ((), ())), preferred_element_type=F32)


def standardise(values):
    centered = values - jnp.mean(values, axis=-1, keepdims=True)
    inverse = lax.rsqrt(jnp.mean(centered * centered, axis=-1, keepdims=True) + EPS)
    return centered * inverse, inverse


def standardise_back(grad, gain, values):
    normal, inverse = standardise(values)
    scaled = grad * gain
    along = jnp.mean(scaled * normal, axis=-1, keepdims=True)
    grad_values = inverse * (scaled - jnp.mean(scaled, axis=-1, keepdims=True) - normal * along)
    return grad_values, jnp.sum(grad * normal, axis=0, keepdims=True)


GELU_A = 0.7978845608028654
GELU_B = 0.044715


def gelu(value):
    return 0.5 * value * (1.0 + jnp.tanh(GELU_A * (value + GELU_B * value * value * value)))


def gelu_slope(value):
    square = value * value
    bent = jnp.tanh(GELU_A * value * (1.0 + GELU_B * square))
    inner = GELU_A * (1.0 + 3.0 * GELU_B * square)
    return 0.5 * (1.0 + bent) + 0.5 * value * (1.0 - bent * bent) * inner


def slot_of(head, block, odd):
    this, other = SLOT_OF[2 * head + block], SLOT_OF[2 * head + 1 - block]
    return jnp.where(odd == 1, other, this)


class Held:
    def __init__(self, source, target, sem):
        self.target = target
        self.copy = pltpu.make_async_copy(source, target, sem)
        self.copy.start()
        self.waited = False

    def ready(self):
        if not self.waited:
            self.copy.wait()
            self.waited = True
        return self.target

    def __getitem__(self, at):
        return self.ready()[at]


class Kept:
    def __init__(self, source, target, sem):
        self.source = source
        self.copy = pltpu.make_async_copy(source, target, sem)
        self.started = False

    def __getitem__(self, at):
        return self.source[at]

    def __setitem__(self, at, value):
        self.source[at] = value

    def flush(self):
        self.copy.start()
        self.started = True

    def finish(self):
        if not self.started:
            self.flush()
        self.copy.wait()


def project(stream, gain, w_qkv, odd, third, slots, normed_out):
    normed = (standardise(stream)[0] * gain).astype(BF16)
    normed_out[...] = normed
    low_lanes = lax.broadcasted_iota(jnp.int32, (ROWS, 128), 1) < 64
    for pair in range(HEADS // 2):
        at = 128 * pair
        queries = dot(normed, w_qkv[:, at : at + 128]) * HEAD_DIM**-0.5
        keys = dot(normed, w_qkv[:, WIDTH + at : WIDTH + at + 128])
        values = dot(normed, w_qkv[:, 2 * WIDTH + at : 2 * WIDTH + at + 128])
        queries_t = queries.T.astype(BF16)
        first = jnp.where(low_lanes, keys, pltpu.roll(values, 64, 1)).astype(BF16)
        second = jnp.where(low_lanes, pltpu.roll(keys, 64, 1), values).astype(BF16)
        for j, both in enumerate((first, second)):
            head = 2 * pair + j
            for block in range(2):
                to = slot_of(head, block, odd)
                slots[to, 0:ROWS, :] = both
                slots[to, ROWS : ROWS + 64, :] = queries_t[
                    64 * j : 64 * j + 64, block * HALF : (block + 1) * HALF
                ]
                slots[to, ROWS + 64 : SLOT, :] = jnp.broadcast_to(third, (16, 128)).astype(BF16)


def gather_heads(recv, odd, row, target):
    for head in range(HEADS):
        for block in range(2):
            target[64 * head : 64 * head + 64, block * HALF : (block + 1) * HALF] = recv[
                slot_of(head, block, odd), row : row + 64, :
            ]


def scatter_heads(features, odd, slots):
    for head in range(HEADS):
        for block in range(2):
            slots[slot_of(head, block, odd)] = features[
                64 * head : 64 * head + 64, block * HALF : (block + 1) * HALF
            ]


def mix(recv, stream, odd, gain, weights, features, acc, att_out, mid_out, normed_out, hidden_out, act_out):
    gather_heads(recv, odd, 0, features)
    attended = features[...].T
    att_out[...] = attended
    mid = stream + dot(attended, weights[0][...])
    mid_out[...] = mid
    normed_out[...] = (standardise(mid)[0] * gain).astype(BF16)
    acc[...] = mid
    up, down = weights[1].ready(), weights[2].ready()

    def step(c, _):
        here = pl.ds(pl.multiple_of(c * FF_BLOCK, FF_BLOCK), FF_BLOCK)
        hidden = dot(normed_out[...], up[:, here])
        hidden_out[:, here] = hidden
        active = gelu(hidden).astype(BF16)
        act_out[:, here] = active
        acc[...] += dot(active, down[here, :])
        return 0

    lax.fori_loop(0, FF // FF_BLOCK, step, 0)


def mix_back(grad, odd, gain, mid, hidden, weights, acc, dz_out, dh_out, dy_out, dmid_out, gain_out, slots):
    out, up, down = weights
    up, down = up.ready(), down.ready()
    dz_out[...] = grad.astype(BF16)
    acc[...] = jnp.zeros(acc.shape, F32)

    def step(c, _):
        here = pl.ds(pl.multiple_of(c * FF_BLOCK, FF_BLOCK), FF_BLOCK)
        grad_act = times_transposed(dz_out[...], down[here, :])
        low = (gelu_slope(hidden[:, here]) * grad_act).astype(BF16)
        dh_out[:, here] = low
        acc[...] += times_transposed(low, up[:, here])
        return 0

    lax.fori_loop(0, FF // FF_BLOCK, step, 0)
    grad_mid, grad_gain = standardise_back(acc[...], gain, mid[...])
    gain_out[...] = grad_gain
    grad_mid = grad_mid + grad
    dmid_out[...] = grad_mid
    for done in (dh_out, dmid_out, dz_out):
        if isinstance(done, Kept):
            done.flush()
    low = grad_mid.astype(BF16)
    dy_out[...] = low
    scatter_heads(times_transposed(low, out[...]).T.astype(BF16), odd, slots)


def project_back(recv, odd, gain, stream, grad_mid, w_qkv, features, dproj_out, gain_out):
    gather_heads(recv, odd, ROWS, features)
    dproj_out[:, 0:WIDTH] = features[...].T
    low_lanes = lax.broadcasted_iota(jnp.int32, (ROWS, 128), 1) < 64
    for pair in range(HEADS // 2):
        at = 128 * pair
        both = []
        for head in (2 * pair, 2 * pair + 1):
            one, two = recv[SLOT_OF[2 * head], 0:ROWS, :], recv[SLOT_OF[2 * head + 1], 0:ROWS, :]
            both.append(one.astype(F32) + two.astype(F32))
        keys = jnp.where(low_lanes, both[0], pltpu.roll(both[1], 64, 1)).astype(BF16)
        values = jnp.where(low_lanes, pltpu.roll(both[0], 64, 1), both[1]).astype(BF16)
        dproj_out[:, WIDTH + at : WIDTH + at + 128] = keys
        dproj_out[:, 2 * WIDTH + at : 2 * WIDTH + at + 128] = values
    grad_normed = times_transposed(dproj_out[...], w_qkv[...])
    grad_stream, grad_gain = standardise_back(grad_normed, gain, stream[...].astype(F32))
    gain_out[...] = grad_gain
    return grad_stream + grad_mid[...]


def enter_kernel(info, gain_attn, ins, outs):
    tokens, w_qkv = ins
    slots, normed = outs
    project(tokens[...].astype(F32), gain_attn[...], w_qkv, info[3], info[4].astype(F32), slots, normed)


def turn_kernel(info, passes, table, gain_attn, gain_mlp, ins, outs, features, acc):
    recv, tokens, w_out, w_up, w_down, w_qkv = ins
    slots, normed, second, att, mid, mid_normed, hidden, act = outs
    odd = info[3]
    mix(recv, tokens[...].astype(F32), odd, gain_mlp[...], (w_out, w_up, w_down), features, acc, att, mid, mid_normed, hidden, act)
    for out in (att, mid, mid_normed, hidden, act):
        out.flush()
    stream = acc[...]
    for row in range(PASSES):
        stream = stream + jnp.where(passes[...] == row, table[row : row + 1, :], 0.0)
    second[...] = stream
    second.flush()
    project(stream, gain_attn[...], w_qkv, odd, info[4].astype(F32), slots, normed)


def crest_kernel(info, gain_mlp, ins, outs, features, acc, mid, hidden, dz):
    recv, stream, w_out, w_up, w_down, cotangent = ins
    slots, mixed, att, mid_normed, act, dh, dy, dmid, gain_out = outs
    odd = info[3]
    gain = gain_mlp[...]
    mix(recv, stream[...], odd, gain, (w_out, w_up, w_down), features, acc, att, mid, mid_normed, hidden, act)
    mixed[...] = acc[...].astype(BF16)
    for out in (att, mid_normed, act, mixed):
        out.flush()
    mix_back(cotangent[...].astype(F32), odd, gain, mid, hidden, (w_out, w_up, w_down), acc, dz, dh, dy, dmid, gain_out, slots)


def return_kernel(info, passes, gain_attn, gain_mlp, ins, outs, features, acc):
    recv, w_qkv, stream, grad_mid, w_down, hidden, w_up, mid, w_out = ins
    slots, dproj, gain_attn_out, table_out, dz, dh, dy, dmid, gain_mlp_out = outs
    odd = info[3]
    grad = project_back(recv, odd, gain_attn[...], stream, grad_mid, w_qkv, features, dproj, gain_attn_out)
    dproj.flush()
    for row in range(PASSES):
        table_out[row : row + 1, :] = jnp.sum(jnp.where(passes[...] == row, grad, 0.0), axis=0, keepdims=True)
    table_out[PASSES:8, :] = jnp.zeros((8 - PASSES, WIDTH), F32)
    mix_back(grad, odd, gain_mlp[...], mid, hidden.ready(), (w_out, w_up, w_down), acc, dz, dh, dy, dmid, gain_mlp_out, slots)


def leave_kernel(info, gain_attn, ins, outs, features):
    recv, w_qkv, tokens, grad_mid = ins
    grad_tokens, dproj, gain_out = outs
    grad_tokens[...] = project_back(recv, info[3], gain_attn[...], tokens, grad_mid, w_qkv, features, dproj, gain_out)


def shape(*dims, dtype=BF16):
    return jax.ShapeDtypeStruct(dims, dtype)


def in_vmem(kernel, name, info, small, arrays, outs, scratch, flops):
    vmem = pl.BlockSpec(memory_space=pltpu.VMEM)
    hbm = pl.BlockSpec(memory_space=pl.ANY)
    ins, count = len(arrays), len(arrays) + len(outs)

    def body(info, *refs):
        few, refs = refs[: len(small)], refs[len(small) :]
        far, near, sems, rest = refs[:count], refs[count : 2 * count], refs[2 * count], refs[2 * count + 1 :]
        held = [Held(far[i], near[i], sems.at[i]) for i in range(ins)]
        kept = [Kept(near[i], far[i], sems.at[i]) for i in range(ins, count)]
        kernel(info, *few, held, kept, *rest)
        for one in kept:
            if not one.started:
                one.flush()
        for one in held:
            one.ready()
        for one in kept:
            one.finish()

    return pl.pallas_call(
        body,
        out_shape=tuple(outs),
        in_specs=[pl.BlockSpec(memory_space=pltpu.SMEM)] + [vmem] * len(small) + [hbm] * ins,
        out_specs=(hbm,) * len(outs),
        scratch_shapes=[pltpu.VMEM(x.shape, x.dtype) for x in (*arrays, *outs)]
        + [pltpu.SemaphoreType.DMA((count,))]
        + scratch,
        compiler_params=pltpu.CompilerParams(vmem_limit_bytes=56 << 20),
        cost_estimate=pl.CostEstimate(flops=int(flops), bytes_accessed=16 << 20, transcendentals=1 << 20),
        name=name,
    )(info, *small, *arrays)


LATE = 7680
CORE = 5


def grads_kernel(info, small, ins, outs):
    dh_one, mid_one, dh_two, mid_two, act_one, dz_one, act_two, dz_two, att_one, dy_one, att_two, dy_two = ins
    up, down, out = outs

    def left(one, two):
        return jnp.concatenate([one, two], axis=0).T

    mid = left(mid_one[...], mid_two[...])
    dh_one.ready(), dh_two.ready()

    def step_up(c, _):
        here = pl.ds(pl.multiple_of(c * 512, 512), 512)
        up[:, here] = dot(mid, jnp.concatenate([dh_one[:, here], dh_two[:, here]], axis=0)).astype(BF16)
        return 0

    lax.fori_loop(0, 6, step_up, 0)
    up.flush()
    dz = jnp.concatenate([dz_one[...], dz_two[...]], axis=0)
    act_one.ready(), act_two.ready()

    def step_down(c, _):
        here = pl.ds(pl.multiple_of(c * 512, 512), 512)
        down[here, :] = dot(left(act_one[:, here], act_two[:, here]), dz).astype(BF16)
        return 0

    lax.fori_loop(0, 6, step_down, 0)
    down.flush()
    dy = jnp.concatenate([dy_one[...], dy_two[...]], axis=0)
    out[0:WIDTH, :] = dot(left(att_one[...], att_two[...]), dy).astype(BF16)
    out[WIDTH:, :] = small[...].astype(BF16)


def grad_qkv_kernel(info, ins, outs):
    normed, dproj = ins
    left = normed[...].T
    dproj.ready()

    def step(c, _):
        result = dot(left, dproj[:, pl.ds(pl.multiple_of(c * 384, 384), 384)])
        for i in range(3):
            outs[0][3 * c + i] = result[:, 128 * i : 128 * i + 128]
        return 0

    lax.fori_loop(0, 6, step, 0)


def grad_qkv_both_kernel(info, gains, ins, outs):
    normed, dproj, before = ins
    left = normed[...].T
    dproj.ready(), before.ready()
    core = info[CORE]

    def step(c, _):
        result = dot(left, dproj[:, pl.ds(pl.multiple_of(c * 384, 384), 384)])
        for to, out in enumerate(outs):

            @pl.when(core == to)
            def _():
                for i in range(3):
                    part = (result[:384, 128 * i : 128 * i + 128] + before[3 * c + i, :384, :]).astype(BF16)
                    out[pl.ds(pl.multiple_of((3 * c + i) * 384, 384), 384), :] = part

            @pl.when(core != to)
            def _():
                for i in range(3):
                    part = (result[384:, 128 * i : 128 * i + 128] + before[3 * c + i, 384:, :]).astype(BF16)
                    out[pl.ds(pl.multiple_of((3 * c + i) * 384, 384), 384), :] = part

        return 0

    lax.fori_loop(0, 6, step, 0)
    for out in outs:
        out[6912:6928, :] = gains[...].astype(BF16)


def widen_kernel(core, mine, other, out):
    half = pl.program_id(0) // 3

    def put(ref):
        for i in range(ref.shape[0]):
            out[:, 128 * i : 128 * i + 128] = ref[i].astype(F32)

    @pl.when(half == core[0])
    def _():
        put(mine)

    @pl.when(half != core[0])
    def _():
        put(other)


def widen(core, mine, other, columns, height, first):
    def place(own):
        def index(i, core):
            low = core[0] == (0 if own else 1)
            part = jnp.where(low, jnp.minimum(i, 2), jnp.maximum(i - 3, 0))
            return (first // columns, part, 0)

        return pl.BlockSpec((columns, height // 3, 128), index)

    return pl.pallas_call(
        widen_kernel,
        out_shape=shape(2 * height, columns * 128, dtype=F32),
        grid_spec=pltpu.PrefetchScalarGridSpec(
            num_scalar_prefetch=1,
            grid=(6,),
            in_specs=[place(True), place(False)],
            out_specs=pl.BlockSpec((height // 3, columns * 128), lambda i, core: (i, 0)),
        ),
        compiler_params=pltpu.CompilerParams(vmem_limit_bytes=20 << 20),
        name="widen",
    )(core, mine.reshape(-1, height, 128), other.reshape(-1, height, 128))


def swap(value, bit):
    return lax.ppermute(value, "batch", [(i, i ^ bit) for i in range(4)])


def exchange(slots):
    return lax.all_to_all(slots, "seq", 0, 0)


def sum_cores(partial):
    mine, other = partial
    return (mine.astype(F32) + swap(other, 1).astype(F32)).astype(BF16)


CHIPS = 64


def across_chips(slots):
    groups = [[s * 4 + z * 2 + c for s in range(SEQ) for z in range(2)] for c in range(2)]
    return lax.all_to_all(slots, ("seq", "batch"), 0, 0, axis_index_groups=groups)


def positions(half, first_row, count):
    at = lax.broadcasted_iota(jnp.int32, (1, count), 1)
    block = at // HALF
    return first_row + block * ROWS + ((half + block) % 2) * HALF + at % HALF


def third_keys(recv, count):
    last = recv[SEQ - 1, ROWS + 64 : SLOT, :].astype(F32)[0:1].astype(jnp.int32)
    row = last + (SEQ - 1) * ROWS
    return jnp.concatenate([row] * (count // 128), axis=1)


def first_keys(at, second, third):
    return jnp.where(at < second, 0, jnp.where(at < third, second, third))


def attend_kernel(info, recv_far, out_low_far, out_f_far, lse_far, kv_t_far, q_t_far, recv, out_low, out_f, lse, kv_t, q_t, sems, top, acc, *, devs):
    tile_rows = devs * HALF
    span = devs * ROWS
    active, half, second = info[0], info[1], info[2]

    @pl.when(active == 1)
    def _():
        parts = [
            Held(recv_far.at[8 * i : 8 * i + 8], recv.at[8 * i : 8 * i + 8], sems.at[i]) for i in range(4)
        ]
        fars = (kv_t_far, q_t_far, out_low_far, out_f_far, lse_far)
        kept = [
            Kept(near, far, sems.at[4 + i])
            for i, (near, far) in enumerate(zip((kv_t, q_t, out_low, out_f, lse), fars))
        ]
        ones = (lax.broadcasted_iota(jnp.int32, (16, ROWS), 0) == 0).astype(BF16)
        for d in range(SEQ):
            parts[d // 8].ready()
            keys = slice(d * ROWS, (d + 1) * ROWS)
            kv_t[0:128, keys] = recv[d, 0:ROWS, :].T
            kv_t[128:144, keys] = ones
            q_t[0:64, d * HALF : (d + 1) * HALF] = recv[d, ROWS : ROWS + 64, :]
        q_t[64:128, :] = jnp.zeros((64, SEQ * HALF), BF16)
        kept[0].flush()
        kept[1].flush()

        third = third_keys(recv, tile_rows)

        def square_top(features):
            wide = features.astype(F32)
            return jnp.max(jnp.sum(wide * wide, axis=0, keepdims=True))

        key_top = jnp.float32(0.0)
        query_top = jnp.float32(0.0)
        for c in range(8):
            key_top = jnp.maximum(key_top, square_top(kv_t[0:64, 1024 * c : 1024 * c + 1024]))
        for c in range(4):
            query_top = jnp.maximum(query_top, square_top(q_t[0:64, 1024 * c : 1024 * c + 1024]))
        small = key_top * query_top < (SMALL / LOG2E) ** 2

        def one_tile(t, shifted):
            start = t * span
            columns = pl.ds(pl.multiple_of(t * tile_rows, tile_rows), tile_rows)
            at = positions(half, start, tile_rows)
            first = first_keys(at, second, third)
            top[...] = jnp.full((1, tile_rows), LOW if shifted else 0.0, F32)
            acc[...] = jnp.zeros((80, tile_rows), F32)
            queries = q_t[:, columns]

            def update(kv, key_rows, left, mask):
                here = slice(left, tile_rows)
                scores = dot(kv, queries[:, here]) * LOG2E
                if not shifted:
                    weights = jnp.exp2(scores)
                    if mask is not None:
                        weights = jnp.where(mask, weights, 0.0)
                    acc[:, here] = acc[:, here] + dot(kv_t[64:144, key_rows], weights.astype(BF16))
                    return
                if mask is not None:
                    scores = jnp.where(mask, scores, LOW)
                old_top = top[:, here]
                new_top = jnp.maximum(old_top, jnp.max(scores, axis=0, keepdims=True))
                weights = jnp.exp2(scores - new_top).astype(BF16)
                shrink = jnp.exp2(old_top - new_top)
                acc[:, here] = acc[:, here] * shrink + dot(kv_t[64:144, key_rows], weights)
                top[:, here] = new_top

            def whole(j, masked):
                key_start = pl.multiple_of(j * 1024, 1024)
                kv = recv[pl.ds(j * 4, 4), 0:ROWS, :].reshape(1024, 128)
                mask = None
                if masked:
                    mask = lax.broadcasted_iota(jnp.int32, (1024, 1), 0) >= second
                update(kv, pl.ds(key_start, 1024), 0, mask)

            @pl.when(t > 0)
            def _():
                whole(0, True)

            def step(j, _):
                whole(j, False)
                return 0

            lax.fori_loop(1, t * (span // 1024), step, 0)
            fresh = first >= start
            top[...] = jnp.where(fresh, LOW if shifted else 0.0, top[...])
            acc[...] = jnp.where(fresh, 0.0, acc[...])
            for i in range(devs // 2):
                left = 256 * i
                key_start = pl.multiple_of(start + 512 * i, 512)
                kv = recv[pl.ds(t * devs + 2 * i, 2), 0:ROWS, :].reshape(512, 128)
                key_at = key_start + lax.broadcasted_iota(jnp.int32, (512, 1), 0)
                allowed = (key_at >= first[:, left:]) & (key_at <= at[:, left:])
                update(kv, pl.ds(key_start, 512), left, allowed)
            total = acc[64:65, :]
            result = acc[0:64, :] / total
            out_f[:, columns] = result
            lse[:, columns] = top[...] + jnp.log2(total)
            low = result.astype(BF16)
            for i in range(devs):
                out_low[t * devs + i] = low[:, i * HALF : (i + 1) * HALF]

        for shifted in (False, True):

            @pl.when(small != shifted)
            def _():
                def tile(t, _):
                    one_tile(t, shifted)
                    return 0

                lax.fori_loop(0, SEQ // devs, tile, 0)

        for one in kept[2:]:
            one.flush()
        for one in kept:
            one.finish()


def attend(info, recv):
    devs = 8
    pairs = 17.8e6
    out_low, *rest = pl.pallas_call(
        functools.partial(attend_kernel, devs=devs),
        out_shape=(
            jax.ShapeDtypeStruct((SEQ, 64, HALF), BF16),
            jax.ShapeDtypeStruct((64, SEQ * HALF), F32),
            jax.ShapeDtypeStruct((1, SEQ * HALF), F32),
            jax.ShapeDtypeStruct((144, SEQ * ROWS), BF16),
            jax.ShapeDtypeStruct((128, SEQ * HALF), BF16),
        ),
        in_specs=[
            pl.BlockSpec(memory_space=pltpu.SMEM),
            pl.BlockSpec(memory_space=pl.ANY),
        ],
        out_specs=tuple(pl.BlockSpec(memory_space=pl.ANY) for _ in range(5)),
        scratch_shapes=[
            pltpu.VMEM((SEQ, SLOT, 128), BF16),
            pltpu.VMEM((SEQ, 64, HALF), BF16),
            pltpu.VMEM((64, SEQ * HALF), F32),
            pltpu.VMEM((1, SEQ * HALF), F32),
            pltpu.VMEM((144, SEQ * ROWS), BF16),
            pltpu.VMEM((128, SEQ * HALF), BF16),
            pltpu.SemaphoreType.DMA((9,)),
            pltpu.VMEM((1, devs * HALF), F32),
            pltpu.VMEM((80, devs * HALF), F32),
        ],
        compiler_params=pltpu.CompilerParams(vmem_limit_bytes=56 << 20),
        cost_estimate=pl.CostEstimate(
            flops=int(pairs * 1024), bytes_accessed=8 << 20, transcendentals=int(pairs)
        ),
        name="attend",
    )(info, recv)
    out_f, lse, kv_t, q_t = rest
    return out_low, recv, kv_t, q_t, out_f, lse


def attend_back_kernel(info, recv_far, kv_t_far, q_t_far, out_f_far, lse_far, grad_out_far, send_far, recv, kv_t, q_t, out_f, lse, grad_out, send, sems, grad_kv, do_t, grad_q, *, devs):
    tile_rows = devs * HALF
    span = devs * ROWS
    active, half, second = info[0], info[1], info[2]

    @pl.when(active == 1)
    def _():
        fars = (grad_out_far, recv_far, q_t_far, out_f_far, lse_far, kv_t_far)
        nears = (grad_out, recv, q_t, out_f, lse, kv_t)
        held = [Held(far, near, sems.at[i]) for i, (far, near) in enumerate(zip(fars, nears))]
        grad_kv[...] = jnp.zeros(grad_kv.shape, F32)
        held[0].ready()
        for d in range(SEQ):
            do_t[64:128, d * HALF : (d + 1) * HALF] = grad_out[d]
        do_t[0:64, :] = jnp.zeros((64, SEQ * HALF), BF16)
        for one in held:
            one.ready()

        third = third_keys(recv, tile_rows)

        def one_tile(t, _):
            start = t * span
            columns = pl.ds(pl.multiple_of(t * tile_rows, tile_rows), tile_rows)
            at = positions(half, start, tile_rows)
            first = first_keys(at, second, third)
            queries = q_t[:, columns]
            grads = do_t[:, columns]
            query_rows = queries.T
            grad_rows = grads.T
            delta = jnp.sum(
                grads[64:128, :].astype(F32) * out_f[:, columns], axis=0, keepdims=True
            )
            own_lse = lse[:, columns]
            far_lse = jnp.where(first >= start, -LOW, own_lse)
            grad_q[...] = jnp.zeros((64, tile_rows), F32)

            def update(kv, key_rows, left, row_lse, mask):
                here = slice(left, tile_rows)
                scores = dot(kv, queries[:, here]) * LOG2E
                probs = jnp.exp2(scores - row_lse[:, here])
                if mask is not None:
                    probs = jnp.where(mask, probs, 0.0)
                grad_probs = dot(kv, grads[:, here])
                grad_scores = (probs * (grad_probs - delta[:, here])).astype(BF16)
                grad_kv[key_rows, :] += dot(grad_scores, query_rows[here, :]) + dot(
                    probs.astype(BF16), grad_rows[here, :]
                )
                grad_q[:, here] += dot(kv_t[0:64, key_rows], grad_scores)

            def whole(j, masked):
                key_start = pl.multiple_of(j * 1024, 1024)
                kv = recv[pl.ds(j * 4, 4), 0:ROWS, :].reshape(1024, 128)
                mask = None
                if masked:
                    mask = lax.broadcasted_iota(jnp.int32, (1024, 1), 0) >= second
                update(kv, pl.ds(key_start, 1024), 0, far_lse, mask)

            @pl.when(t > 0)
            def _():
                whole(0, True)

            def step(j, _):
                whole(j, False)
                return 0

            lax.fori_loop(1, t * (span // 1024), step, 0)
            for i in range(devs // 2):
                left = 256 * i
                key_start = pl.multiple_of(start + 512 * i, 512)
                kv = recv[pl.ds(t * devs + 2 * i, 2), 0:ROWS, :].reshape(512, 128)
                key_at = key_start + lax.broadcasted_iota(jnp.int32, (512, 1), 0)
                allowed = (key_at >= first[:, left:]) & (key_at <= at[:, left:])
                update(kv, pl.ds(key_start, 512), left, own_lse, allowed)
            low = (grad_q[...] * HEAD_DIM**-0.5).astype(BF16)
            for i in range(devs):
                send[t * devs + i, ROWS:, :] = low[:, i * HALF : (i + 1) * HALF]
            return 0

        lax.fori_loop(0, SEQ // devs, one_tile, 0)
        for d in range(SEQ):
            send[d, 0:ROWS, :] = grad_kv[d * ROWS : (d + 1) * ROWS, :].astype(BF16)
        out = Kept(send, send_far, sems.at[6])
        out.finish()


def attend_back(info, recv, kv_t, q_t, out_f, lse, grad_out):
    devs = 4
    pairs = 17.8e6
    return pl.pallas_call(
        functools.partial(attend_back_kernel, devs=devs),
        out_shape=jax.ShapeDtypeStruct((SEQ, ROWS + 64, HALF), BF16),
        in_specs=[pl.BlockSpec(memory_space=pltpu.SMEM)]
        + [pl.BlockSpec(memory_space=pl.ANY)] * 6,
        out_specs=pl.BlockSpec(memory_space=pl.ANY),
        scratch_shapes=[
            pltpu.VMEM((SEQ, SLOT, 128), BF16),
            pltpu.VMEM((144, SEQ * ROWS), BF16),
            pltpu.VMEM((128, SEQ * HALF), BF16),
            pltpu.VMEM((64, SEQ * HALF), F32),
            pltpu.VMEM((1, SEQ * HALF), F32),
            pltpu.VMEM((SEQ, 64, HALF), BF16),
            pltpu.VMEM((SEQ, ROWS + 64, HALF), BF16),
            pltpu.SemaphoreType.DMA((7,)),
            pltpu.VMEM((SEQ * ROWS, 128), F32),
            pltpu.VMEM((128, SEQ * HALF), BF16),
            pltpu.VMEM((64, devs * HALF), F32),
        ],
        compiler_params=pltpu.CompilerParams(vmem_limit_bytes=56 << 20),
        cost_estimate=pl.CostEstimate(
            flops=int(pairs * 1024), bytes_accessed=8 << 20, transcendentals=int(pairs)
        ),
        name="attend_back",
    )(info, recv, kv_t, q_t, out_f, lse, grad_out)


def on_device(
    tokens,
    token_pos,
    token_pass,
    token_count,
    w_qkv,
    w_out,
    w_up,
    w_down,
    gain_attn,
    gain_mlp,
    pass_table,
    cotangent,
):
    here = lax.axis_index("seq")
    offset = token_pos[0] * token_count[0] + token_pass[0]
    first_token = here * ROWS - offset[0]
    last_token = here * ROWS + ROWS - 1 - offset[ROWS - 1]
    second = jnp.where(here == 0, last_token, first_token)
    third = last_token - (SEQ - 1) * ROWS
    third = jnp.where((third < 0) | (third > ROWS), ROWS, third)
    group, place = here // 4, here % 4
    active = (place < 3).astype(jnp.int32)
    core = lax.axis_index("batch") % 2
    info = jnp.stack([active, (3 * group + place) % 2, second, here % 2, third, core])
    passes = token_pass[0][:, None]
    table = jnp.pad(pass_table, ((0, 8 - PASSES), (0, 0)))
    gain_a, gain_m = gain_attn[None], gain_mlp[None]
    stream_one = tokens[0]
    features = pltpu.VMEM((WIDTH, ROWS), BF16)
    acc = pltpu.VMEM((ROWS, WIDTH), F32)
    square = shape(ROWS, WIDTH)
    wide = shape(ROWS, WIDTH, dtype=F32)
    row = shape(1, WIDTH, dtype=F32)
    sent = shape(SEQ, SLOT, 128)
    sent_back = shape(SEQ, 64, 128)

    slots, normed_one = in_vmem(
        enter_kernel, "enter", info, (gain_a,), (stream_one, w_qkv), (sent, square), [], 1e9
    )
    saved_one = attend(info, exchange(slots))
    slots, normed_two, stream_two, att_one, mid_one, midn_one, hidden_one, act_one = in_vmem(
        turn_kernel,
        "turn",
        info,
        (passes, table, gain_a, gain_m),
        (exchange(saved_one[0]), stream_one, w_out, w_up, w_down, w_qkv),
        (sent, square, wide, square, wide, square, shape(ROWS, FF, dtype=F32), shape(ROWS, FF)),
        [features, acc],
        3.6e9,
    )
    saved_two = attend(info, exchange(slots))
    slots, mixed, att_two, midn_two, act_two, dh_two, dy_two, dmid_two, gain_m_two = in_vmem(
        crest_kernel,
        "crest",
        info,
        (gain_m,),
        (exchange(saved_two[0]), stream_two, w_out, w_up, w_down, cotangent[0]),
        (sent_back, square, square, square, shape(ROWS, FF), shape(ROWS, FF), square, wide, row),
        [features, acc, acc, pltpu.VMEM((ROWS, FF), F32), pltpu.VMEM((ROWS, WIDTH), BF16)],
        5e9,
    )
    back = exchange(slots)
    recv = exchange(attend_back(info, *saved_two[1:], back))
    slots, dproj_two, gain_a_two, grad_table, dz_one, dh_one, dy_one, dmid_one, gain_m_one = in_vmem(
        return_kernel,
        "return",
        info,
        (passes, gain_a, gain_m),
        (recv, w_qkv, stream_two, dmid_two, w_down, hidden_one, w_up, mid_one, w_out),
        (
            sent_back,
            shape(ROWS, 3 * WIDTH),
            row,
            shape(8, WIDTH, dtype=F32),
            square,
            shape(ROWS, FF),
            square,
            wide,
            row,
        ),
        [features, acc],
        5e9,
    )
    back = exchange(slots)
    small = jnp.concatenate(
        [grad_table[:PASSES], gain_a_two, gain_m_one + gain_m_two, jnp.zeros((9, WIDTH), F32)]
    )
    early = in_vmem(
        grads_kernel,
        "grads",
        info,
        (small,),
        (dh_one, midn_one, dh_two, midn_two, act_one, dz_one, act_two, cotangent[0], att_one, dy_one, att_two, dy_two),
        (shape(WIDTH, FF), shape(FF, WIDTH), shape(WIDTH + 16, WIDTH)),
        [],
        5.4e10,
    )
    back, early = lax.optimization_barrier((back, early))
    early = lax.psum(early, ("seq", "batch"))
    sent_one = attend_back(info, *saved_one[1:], back)
    recv = exchange(sent_one)
    grad_tokens, dproj_one, gain_a_one = in_vmem(
        leave_kernel,
        "leave",
        info,
        (gain_a,),
        (recv, w_qkv, stream_one, dmid_one),
        (wide, shape(ROWS, 3 * WIDTH), row),
        [features],
        1e9,
    )
    (grad_two,) = in_vmem(
        grad_qkv_kernel,
        "grad_qkv_two",
        info,
        (),
        (normed_two, dproj_two),
        (shape(18, WIDTH, 128, dtype=F32),),
        [],
        9e8,
    )
    late = in_vmem(
        grad_qkv_both_kernel,
        "grad_qkv",
        info,
        (jnp.pad(gain_a_one.reshape(6, 128), ((0, 10), (0, 0))),),
        (normed_one, dproj_one, grad_two),
        (shape(LATE, 128),) * 2,
        [],
        9e8,
    )
    late, early = lax.optimization_barrier((late, early))
    late = across_chips(sum_cores(late).reshape(CHIPS, -1, 128))
    early = tuple(x.astype(F32) for x in early)
    late, early = lax.optimization_barrier((late, early))
    late = jnp.sum(late.astype(F32), axis=0).astype(BF16)
    whole = across_chips(jnp.broadcast_to(late[None], (CHIPS, *late.shape))).reshape(-1, 128)
    late = (whole, swap(whole, 1))
    grad_up, grad_down, grad_out = early
    tail = grad_out[WIDTH : WIDTH + 8]
    gain_a_sum = late[0][6912:6918].reshape(WIDTH).astype(F32)
    return (
        mixed[None],
        grad_tokens[None],
        widen(info[CORE : CORE + 1], *late, 18, 384, 0),
        grad_out[:WIDTH],
        grad_up,
        grad_down,
        tail[PASSES] + gain_a_sum,
        tail[PASSES + 1],
        tail[:PASSES],
    )


def solution(mesh):
    return jax.shard_map(
        on_device,
        mesh=mesh,
        in_specs=(
            P("batch", "seq", None),
            P("batch", "seq"),
            P("batch", "seq"),
            P("batch", "seq"),
            P(),
            P(),
            P(),
            P(),
            P(),
            P(),
            P(),
            P("batch", "seq", None),
        ),
        out_specs=(
            P("batch", "seq", None),
            P("batch", "seq", None),
            P(),
            P(),
            P(),
            P(),
            P(),
            P(),
            P(),
        ),
        check_vma=False,
    )
```

```python
import functools

import jax
import jax.numpy as jnp
from jax import lax
from jax.experimental import pallas as pl
from jax.experimental.pallas import tpu as pltpu
from jax.sharding import PartitionSpec as P

HEADS = 12
HEAD_DIM = 64
PASSES = 5
SEQ = 32
ROWS = 256
HALF = 128
SLOT = ROWS + 64 + 16
WIDTH = 768
FF = 3072
FF_BLOCK = 512
EPS = 1e-5
LOG2E = 1.4426950408889634
LOW = -1e30
SMALL = 60.0
F32 = jnp.float32
BF16 = jnp.bfloat16

WORK = [3 * (e // 4) + e % 4 if e % 4 < 3 else None for e in range(SEQ)]
SLOT_OF = {w: e for e, w in enumerate(WORK) if w is not None}


def dot(left, right):
    return jnp.dot(left, right, preferred_element_type=F32)


def contract_rows(left, right):
    return lax.dot_general(left, right, (((0,), (0,)), ((), ())), preferred_element_type=F32)


def times_transposed(left, right):
    return lax.dot_general(left, right, (((1,), (1,)), ((), ())), preferred_element_type=F32)


def standardise(values):
    centered = values - jnp.mean(values, axis=-1, keepdims=True)
    inverse = lax.rsqrt(jnp.mean(centered * centered, axis=-1, keepdims=True) + EPS)
    return centered * inverse, inverse


def standardise_back(grad, gain, values):
    normal, inverse = standardise(values)
    scaled = grad * gain
    along = jnp.mean(scaled * normal, axis=-1, keepdims=True)
    grad_values = inverse * (scaled - jnp.mean(scaled, axis=-1, keepdims=True) - normal * along)
    return grad_values, jnp.sum(grad * normal, axis=0, keepdims=True)


GELU_A = 0.7978845608028654
GELU_B = 0.044715


def gelu(value):
    return 0.5 * value * (1.0 + jnp.tanh(GELU_A * (value + GELU_B * value * value * value)))


def gelu_slope(value):
    square = value * value
    bent = jnp.tanh(GELU_A * value * (1.0 + GELU_B * square))
    inner = GELU_A * (1.0 + 3.0 * GELU_B * square)
    return 0.5 * (1.0 + bent) + 0.5 * value * (1.0 - bent * bent) * inner


def slot_of(head, block, odd):
    this, other = SLOT_OF[2 * head + block], SLOT_OF[2 * head + 1 - block]
    return jnp.where(odd == 1, other, this)


class Held:
    def __init__(self, source, target, sem):
        self.target = target
        self.copy = pltpu.make_async_copy(source, target, sem)
        self.copy.start()
        self.waited = False

    def ready(self):
        if not self.waited:
            self.copy.wait()
            self.waited = True
        return self.target

    def __getitem__(self, at):
        return self.ready()[at]


class HeldBlocks:
    def __init__(self, source, target, sems, axis):
        self.source, self.target, self.sems, self.axis = source, target, sems, axis
        self.waited = False

    def copy(self, c):
        here = pl.ds(c * FF_BLOCK if isinstance(c, int) else pl.multiple_of(c * FF_BLOCK, FF_BLOCK), FF_BLOCK)
        at = (here, slice(None)) if self.axis == 0 else (slice(None), here)
        return pltpu.make_async_copy(self.source.at[at], self.target.at[at], self.sems.at[c])

    def wait(self, c):
        if not self.waited:
            self.copy(c).wait()

    def ready(self):
        assert self.waited
        return self.target

    def __getitem__(self, at):
        return self.target[at]


class Kept:
    def __init__(self, source, target, sem):
        self.source = source
        self.copy = pltpu.make_async_copy(source, target, sem)
        self.started = False

    def __getitem__(self, at):
        return self.source[at]

    def __setitem__(self, at, value):
        self.source[at] = value

    def flush(self):
        self.copy.start()
        self.started = True

    def finish(self):
        if not self.started:
            self.flush()
        self.copy.wait()


def project(stream, gain, w_qkv, odd, third, slots, normed_out):
    normed = (standardise(stream)[0] * gain).astype(BF16)
    normed_out[...] = normed
    low_lanes = lax.broadcasted_iota(jnp.int32, (ROWS, 128), 1) < 64
    for pair in range(HEADS // 2):
        at = 128 * pair
        queries = dot(normed, w_qkv[:, at : at + 128]) * HEAD_DIM**-0.5
        keys = dot(normed, w_qkv[:, WIDTH + at : WIDTH + at + 128])
        values = dot(normed, w_qkv[:, 2 * WIDTH + at : 2 * WIDTH + at + 128])
        queries_t = queries.T.astype(BF16)
        first = jnp.where(low_lanes, keys, pltpu.roll(values, 64, 1)).astype(BF16)
        second = jnp.where(low_lanes, pltpu.roll(keys, 64, 1), values).astype(BF16)
        for j, both in enumerate((first, second)):
            head = 2 * pair + j
            for block in range(2):
                to = slot_of(head, block, odd)
                slots[to, 0:ROWS, :] = both
                slots[to, ROWS : ROWS + 64, :] = queries_t[
                    64 * j : 64 * j + 64, block * HALF : (block + 1) * HALF
                ]
                slots[to, ROWS + 64 : SLOT, :] = jnp.broadcast_to(third, (16, 128)).astype(BF16)


def gather_heads(recv, odd, row, target):
    for head in range(HEADS):
        for block in range(2):
            target[64 * head : 64 * head + 64, block * HALF : (block + 1) * HALF] = recv[
                slot_of(head, block, odd), row : row + 64, :
            ]


def scatter_heads(features, odd, slots):
    for head in range(HEADS):
        for block in range(2):
            slots[slot_of(head, block, odd)] = features[
                64 * head : 64 * head + 64, block * HALF : (block + 1) * HALF
            ]


def mix(recv, stream, odd, gain, weights, features, acc, att_out, mid_out, normed_out, hidden_out, act_out):
    gather_heads(recv, odd, 0, features)
    attended = features[...].T
    att_out[...] = attended
    mid = stream + dot(attended, weights[0][...])
    mid_out[...] = mid
    normed_out[...] = (standardise(mid)[0] * gain).astype(BF16)
    acc[...] = mid
    up, down = weights[1:]

    def step(c, _):
        here = pl.ds(pl.multiple_of(c * FF_BLOCK, FF_BLOCK), FF_BLOCK)
        up.wait(c)
        down.wait(c)
        hidden = dot(normed_out[...], up[:, here])
        hidden_out[:, here] = hidden
        active = gelu(hidden).astype(BF16)
        act_out[:, here] = active
        acc[...] += dot(active, down[here, :])
        return 0

    lax.fori_loop(0, FF // FF_BLOCK, step, 0)
    up.waited = down.waited = True


def mix_back(grad, odd, gain, mid, hidden, weights, acc, dz_out, dh_out, dy_out, dmid_out, gain_out, slots):
    out, up, down = weights
    dz_out[...] = grad.astype(BF16)
    acc[...] = jnp.zeros(acc.shape, F32)

    def step(c, _):
        here = pl.ds(pl.multiple_of(c * FF_BLOCK, FF_BLOCK), FF_BLOCK)
        up.wait(c)
        down.wait(c)
        grad_act = times_transposed(dz_out[...], down[here, :])
        low = (gelu_slope(hidden[:, here]) * grad_act).astype(BF16)
        dh_out[:, here] = low
        acc[...] += times_transposed(low, up[:, here])
        return 0

    lax.fori_loop(0, FF // FF_BLOCK, step, 0)
    up.waited = down.waited = True
    grad_mid, grad_gain = standardise_back(acc[...], gain, mid[...])
    gain_out[...] = grad_gain
    grad_mid = grad_mid + grad
    dmid_out[...] = grad_mid
    for done in (dh_out, dmid_out, dz_out):
        if isinstance(done, Kept):
            done.flush()
    low = grad_mid.astype(BF16)
    dy_out[...] = low
    scatter_heads(times_transposed(low, out[...]).T.astype(BF16), odd, slots)


def project_back(recv, odd, gain, stream, grad_mid, w_qkv, features, dproj_out, gain_out):
    gather_heads(recv, odd, ROWS, features)
    dproj_out[:, 0:WIDTH] = features[...].T
    low_lanes = lax.broadcasted_iota(jnp.int32, (ROWS, 128), 1) < 64
    for pair in range(HEADS // 2):
        at = 128 * pair
        both = []
        for head in (2 * pair, 2 * pair + 1):
            one, two = recv[SLOT_OF[2 * head], 0:ROWS, :], recv[SLOT_OF[2 * head + 1], 0:ROWS, :]
            both.append(one.astype(F32) + two.astype(F32))
        keys = jnp.where(low_lanes, both[0], pltpu.roll(both[1], 64, 1)).astype(BF16)
        values = jnp.where(low_lanes, pltpu.roll(both[0], 64, 1), both[1]).astype(BF16)
        dproj_out[:, WIDTH + at : WIDTH + at + 128] = keys
        dproj_out[:, 2 * WIDTH + at : 2 * WIDTH + at + 128] = values
    grad_normed = times_transposed(dproj_out[...], w_qkv[...])
    grad_stream, grad_gain = standardise_back(grad_normed, gain, stream[...].astype(F32))
    gain_out[...] = grad_gain
    return grad_stream + grad_mid[...]


def start_of(pos, passes, count, here, at):
    return at - (pos[0, at] * count[0, at] + passes[0, at])


def third_start(start):
    return jnp.where((start < 0) | (start > ROWS), ROWS, start)


def enter_kernel(pos, passes, count, gain_attn, ins, outs):
    tokens, w_qkv = ins
    slots, normed = outs
    here = lax.axis_index("seq")
    third = third_start(start_of(pos, passes, count, here, ROWS - 1))
    project(tokens[...].astype(F32), gain_attn[...], w_qkv, here % 2, third.astype(F32), slots, normed)


def turn_kernel(info, passes, table, gain_attn, gain_mlp, ins, outs, features, acc):
    recv, tokens, w_out, w_up, w_down, w_qkv = ins
    slots, normed, second, att, mid, mid_normed, hidden, act = outs
    odd = info[3]
    mix(recv, tokens[...].astype(F32), odd, gain_mlp[...], (w_out, w_up, w_down), features, acc, att, mid, mid_normed, hidden, act)
    for out in (att, mid, mid_normed, hidden, act):
        out.flush()
    stream = acc[...]
    for row in range(PASSES):
        stream = stream + jnp.where(passes[...] == row, table[row : row + 1, :], 0.0)
    second[...] = stream
    second.flush()
    project(stream, gain_attn[...], w_qkv, odd, info[4].astype(F32), slots, normed)


def crest_kernel(info, gain_mlp, ins, outs, features, acc, mid, hidden, dz):
    recv, stream, w_out, w_up, w_down, cotangent = ins
    slots, mixed, att, mid_normed, act, dh, dy, dmid, gain_out = outs
    odd = info[3]
    gain = gain_mlp[...]
    mix(recv, stream[...], odd, gain, (w_out, w_up, w_down), features, acc, att, mid, mid_normed, hidden, act)
    mixed[...] = acc[...].astype(BF16)
    for out in (att, mid_normed, act, mixed):
        out.flush()
    mix_back(cotangent[...].astype(F32), odd, gain, mid, hidden, (w_out, w_up, w_down), acc, dz, dh, dy, dmid, gain_out, slots)


def return_kernel(info, passes, gain_attn, gain_mlp, gain_m_two, ins, outs, features, acc, dz, dh, dy, gain_m):
    (recv, w_qkv, stream, grad_mid, hidden, w_down, w_up, mid, w_out,
     mid_one, mid_two, dh_two, act_one, act_two, dz_two, att_one, att_two, dy_two) = ins
    slots, dproj, dmid, up_out, down_out, out_out = outs
    odd = info[3]
    small = jnp.zeros((16, WIDTH), F32)
    at = lax.broadcasted_iota(jnp.int32, (16, 1), 0)
    grad = project_back(recv, odd, gain_attn[...], stream, grad_mid, w_qkv, features, dproj, gain_m)
    dproj.flush()
    small = jnp.where(at == PASSES, gain_m[...], small)
    for row in range(PASSES):
        part = jnp.sum(jnp.where(passes[...] == row, grad, 0.0), axis=0, keepdims=True)
        small = jnp.where(at == row, part, small)
    mix_back(grad, odd, gain_mlp[...], mid, hidden.ready(), (w_out, w_up, w_down), acc, dz, dh, dy, dmid, gain_m, slots)
    slots.flush()
    small = jnp.where(at == PASSES + 1, gain_m[...] + gain_m_two[...], small)
    weight_gradients(
        (mid_one, dh, mid_two, dh_two, act_one, dz, act_two, dz_two, att_one, dy, att_two, dy_two),
        small, up_out, down_out, out_out,
    )


def leave_kernel(info, gain_attn, ins, outs, features):
    recv, w_qkv, tokens, grad_mid = ins
    grad_tokens, dproj, gain_out = outs
    grad_tokens[...] = project_back(recv, info[3], gain_attn[...], tokens, grad_mid, w_qkv, features, dproj, gain_out)


def shape(*dims, dtype=BF16):
    return jax.ShapeDtypeStruct(dims, dtype)


def in_vmem(kernel, name, info, small, arrays, outs, scratch, flops, split={}):
    vmem = pl.BlockSpec(memory_space=pltpu.VMEM)
    hbm = pl.BlockSpec(memory_space=pl.ANY)
    ins, count = len(arrays), len(arrays) + len(outs)

    info = info if isinstance(info, tuple) else (info,)

    def body(*refs):
        known, refs = refs[: len(info)], refs[len(info) :]
        few, refs = refs[: len(small)], refs[len(small) :]
        far, near, sems, rest = refs[:count], refs[count : 2 * count], refs[2 * count], refs[2 * count + 1 :]
        held, blocks = [], []
        for i in range(ins):
            if i in split:
                own = sems.at[pl.ds(count + 6 * len(blocks), 6)]
                held.append(HeldBlocks(far[i], near[i], own, split[i]))
                blocks.append(held[-1])
                if len(blocks) == 2:
                    for c in range(6):
                        for one in blocks:
                            one.copy(c).start()
            else:
                held.append(Held(far[i], near[i], sems.at[i]))
        kept = [Kept(near[i], far[i], sems.at[i]) for i in range(ins, count)]
        kernel(*known, *few, held, kept, *rest)
        for one in kept:
            if not one.started:
                one.flush()
        for one in held:
            one.ready()
        for one in kept:
            one.finish()

    return pl.pallas_call(
        body,
        out_shape=tuple(outs),
        in_specs=[pl.BlockSpec(memory_space=pltpu.SMEM)] * len(info) + [vmem] * len(small) + [hbm] * ins,
        out_specs=(hbm,) * len(outs),
        scratch_shapes=[pltpu.VMEM(x.shape, x.dtype) for x in (*arrays, *outs)]
        + [pltpu.SemaphoreType.DMA((count + 12,))]
        + scratch,
        compiler_params=pltpu.CompilerParams(vmem_limit_bytes=62 << 20),
        cost_estimate=pl.CostEstimate(flops=int(flops), bytes_accessed=16 << 20, transcendentals=1 << 20),
        name=name,
    )(*info, *small, *arrays)


LATE = 7168
CORE = 5


def weight_gradients(factors, small, up, down, out):
    mid_one, dh_one, mid_two, dh_two, act_one, dz_one, act_two, dz_two, att_one, dy_one, att_two, dy_two = factors
    for one in (dh_two, act_one, act_two):
        one.ready()

    def left(one, two):
        return jnp.concatenate([one, two], axis=0).T

    mid = left(mid_one[...], mid_two[...])

    def step_up(c, _):
        here = pl.ds(pl.multiple_of(c * 512, 512), 512)
        up[:, here] = dot(mid, jnp.concatenate([dh_one[:, here], dh_two[:, here]], axis=0)).astype(BF16)
        return 0

    lax.fori_loop(0, 6, step_up, 0)
    up.flush()
    dz = jnp.concatenate([dz_one[...], dz_two[...]], axis=0)

    def step_down(c, _):
        here = pl.ds(pl.multiple_of(c * 512, 512), 512)
        down[here, :] = dot(left(act_one[:, here], act_two[:, here]), dz).astype(BF16)
        return 0

    lax.fori_loop(0, 6, step_down, 0)
    down.flush()
    dy = jnp.concatenate([dy_one[...], dy_two[...]], axis=0)
    out[0:WIDTH, :] = dot(left(att_one[...], att_two[...]), dy).astype(BF16)
    out[WIDTH:, :] = small.astype(BF16)


def grad_qkv_kernel(info, ins, outs):
    normed, dproj = ins
    left = normed[...].T
    dproj.ready()

    def step(c, _):
        result = dot(left, dproj[:, pl.ds(pl.multiple_of(c * 384, 384), 384)])
        for i in range(3):
            outs[0][3 * c + i] = result[:, 128 * i : 128 * i + 128]
        return 0

    lax.fori_loop(0, 6, step, 0)


def grad_qkv_both_kernel(info, gains, ins, outs):
    normed, dproj, before = ins
    left = normed[...].T
    dproj.ready(), before.ready()
    core = info[CORE]

    def step(c, _):
        result = dot(left, dproj[:, pl.ds(pl.multiple_of(c * 384, 384), 384)])
        for to, out in enumerate(outs):
            for half in range(2):

                @pl.when((half ^ core) == to)
                def _():
                    for i in range(3):
                        for part in range(3):
                            rows = slice(384 * half + 128 * part, 384 * half + 128 * part + 128)
                            value = result[rows, 128 * i : 128 * i + 128] + before[3 * c + i, rows, :]
                            at = pl.multiple_of(part * 2304 + (3 * c + i) * 128, 128)
                            out[pl.ds(at, 128), :] = value.astype(BF16)

        return 0

    lax.fori_loop(0, 6, step, 0)
    for out in outs:
        out[6912:6928, :] = gains[...].astype(BF16)


def widen_kernel(core, mine, other, out):
    half = pl.program_id(0) // 3

    def put(ref):
        for i in range(18):
            out[:, 128 * i : 128 * i + 128] = ref[128 * i : 128 * i + 128, :].astype(F32)

    @pl.when(half == core[0])
    def _():
        put(mine)

    @pl.when(half != core[0])
    def _():
        put(other)


def widen(core, mine, other):
    def place(own):
        def index(i, core):
            low = core[0] == (0 if own else 1)
            return (jnp.where(low, jnp.minimum(i, 2), jnp.maximum(i - 3, 0)), 0)

        return pl.BlockSpec((2304, 128), index)

    return pl.pallas_call(
        widen_kernel,
        out_shape=shape(WIDTH, 3 * WIDTH, dtype=F32),
        grid_spec=pltpu.PrefetchScalarGridSpec(
            num_scalar_prefetch=1,
            grid=(6,),
            in_specs=[place(True), place(False)],
            out_specs=pl.BlockSpec((128, 3 * WIDTH), lambda i, core: (i, 0)),
        ),
        compiler_params=pltpu.CompilerParams(vmem_limit_bytes=20 << 20),
        name="widen",
    )(core, mine, other)


def swap(value, bit):
    return lax.ppermute(value, "batch", [(i, i ^ bit) for i in range(4)])


def exchange(slots):
    return lax.all_to_all(slots, "seq", 0, 0)


def sum_cores(partial):
    mine, other = partial
    return (mine.astype(F32) + swap(other, 1).astype(F32)).astype(BF16)


CHIPS = 64


def across_chips(slots):
    groups = [[s * 4 + z * 2 + c for s in range(SEQ) for z in range(2)] for c in range(2)]
    return lax.all_to_all(slots, ("seq", "batch"), 0, 0, axis_index_groups=groups)


def positions(half, first_row, count):
    at = lax.broadcasted_iota(jnp.int32, (1, count), 1)
    block = at // HALF
    return first_row + block * ROWS + ((half + block) % 2) * HALF + at % HALF


def third_keys(recv, count):
    last = recv[SEQ - 1, ROWS + 64 : SLOT, :].astype(F32)[0:1].astype(jnp.int32)
    row = last + (SEQ - 1) * ROWS
    return jnp.concatenate([row] * (count // 128), axis=1)


def first_keys(at, second, third):
    return jnp.where(at < second, 0, jnp.where(at < third, second, third))


def attend_kernel(info, recv_far, out_low_far, out_f_far, lse_far, k_t_far, q_t_far, recv, out_low, out_f, lse, kv_t, q_t, sems, acc, *, devs):
    tile_rows = devs * HALF
    span = devs * ROWS
    active, half, second = info[0], info[1], info[2]

    @pl.when(active == 1)
    def _():
        parts = [
            Held(recv_far.at[8 * i : 8 * i + 8], recv.at[8 * i : 8 * i + 8], sems.at[i]) for i in range(4)
        ]
        fars = (k_t_far, q_t_far, out_low_far, out_f_far, lse_far)
        kept = [
            Kept(near, far, sems.at[4 + i])
            for i, (near, far) in enumerate(zip((kv_t.at[0:64], q_t, out_low, out_f, lse), fars))
        ]
        ones = (lax.broadcasted_iota(jnp.int32, (16, ROWS), 0) == 0).astype(BF16)
        for d in range(SEQ):
            parts[d // 8].ready()
            keys = slice(d * ROWS, (d + 1) * ROWS)
            kv_t[0:128, keys] = recv[d, 0:ROWS, :].T
            kv_t[128:144, keys] = ones
            q_t[0:64, d * HALF : (d + 1) * HALF] = recv[d, ROWS : ROWS + 64, :]
        q_t[64:128, :] = jnp.zeros((64, SEQ * HALF), BF16)
        kept[0].flush()
        kept[1].flush()

        third = third_keys(recv, tile_rows)

        def square_top(features):
            wide = features.astype(F32)
            return jnp.max(jnp.sum(wide * wide, axis=0, keepdims=True))

        key_top = jnp.float32(0.0)
        query_top = jnp.float32(0.0)
        for c in range(8):
            key_top = jnp.maximum(key_top, square_top(kv_t[0:64, 1024 * c : 1024 * c + 1024]))
        for c in range(4):
            query_top = jnp.maximum(query_top, square_top(q_t[0:64, 1024 * c : 1024 * c + 1024]))
        small = key_top * query_top < (SMALL / LOG2E) ** 2

        def one_tile(t, _):
            start = t * span
            columns = pl.ds(pl.multiple_of(t * tile_rows, tile_rows), tile_rows)
            at = positions(half, start, tile_rows)
            first = first_keys(at, second, third)
            acc[...] = jnp.zeros((80, tile_rows), F32)
            queries = q_t[:, columns]

            def update(kv, key_rows, left, mask):
                here = slice(left, tile_rows)
                weights = jnp.exp2(dot(kv, queries[:, here]) * LOG2E)
                if mask is not None:
                    weights = jnp.where(mask, weights, 0.0)
                acc[:, here] = acc[:, here] + dot(kv_t[64:144, key_rows], weights.astype(BF16))

            def step(j, _):
                kv = recv[pl.ds(j * 4, 4), 0:ROWS, :].reshape(1024, 128)
                update(kv, pl.ds(pl.multiple_of(j * 1024, 1024), 1024), 0, None)
                return 0

            lax.fori_loop(0, t * (span // 1024), step, 0)
            acc[...] = jnp.where(first >= start, 0.0, acc[...])
            for i in range(devs // 2):
                left = 256 * i
                key_start = pl.multiple_of(start + 512 * i, 512)
                kv = recv[pl.ds(t * devs + 2 * i, 2), 0:ROWS, :].reshape(512, 128)
                key_at = key_start + lax.broadcasted_iota(jnp.int32, (512, 1), 0)
                allowed = (key_at >= first[:, left:]) & (key_at <= at[:, left:])
                update(kv, pl.ds(key_start, 512), left, allowed)
            total = acc[64:65, :]
            result = acc[0:64, :] / total
            out_f[:, columns] = result
            lse[:, columns] = jnp.log2(total)
            low = result.astype(BF16)
            for i in range(devs):
                out_low[t * devs + i] = low[:, i * HALF : (i + 1) * HALF]

            @pl.when(t == 0)
            def _():
                key_at = lax.broadcasted_iota(jnp.int32, (1, ROWS), 1)
                kv_t[64:144, 0:ROWS] = jnp.where(key_at >= second, kv_t[64:144, 0:ROWS], 0.0).astype(BF16)

            return 0

        def one_device(d, _):
            columns = pl.ds(pl.multiple_of(d * HALF, HALF), HALF)
            at = d * ROWS + (half + d) % 2 * HALF + lax.broadcasted_iota(jnp.int32, (1, HALF), 1)
            first = first_keys(at, second, third_keys(recv, HALF))
            queries = q_t[:, columns]

            def step(j, state):
                old_top, old_acc = state
                kv = recv[pl.ds(j * 2, 2), 0:ROWS, :].reshape(512, 128)
                key_at = j * 512 + lax.broadcasted_iota(jnp.int32, (512, 1), 0)
                allowed = (key_at >= first) & (key_at <= at)
                scores = jnp.where(allowed, dot(kv, queries) * LOG2E, LOW)
                new_top = jnp.maximum(old_top, jnp.max(scores, axis=0, keepdims=True))
                weights = jnp.exp2(scores - new_top).astype(BF16)
                keys = pl.ds(pl.multiple_of(j * 512, 512), 512)
                return new_top, old_acc * jnp.exp2(old_top - new_top) + dot(kv_t[64:144, keys], weights)

            state = (jnp.full((1, HALF), LOW, F32), jnp.zeros((80, HALF), F32))
            top, state = lax.fori_loop(0, d // 2 + 1, step, state)
            total = state[64:65, :]
            result = state[0:64, :] / total
            out_f[:, columns] = result
            lse[:, columns] = top + jnp.log2(total)
            out_low[d] = result.astype(BF16)
            return 0

        @pl.when(small)
        def _():
            lax.fori_loop(0, SEQ // devs, one_tile, 0)

        @pl.when(jnp.logical_not(small))
        def _():
            lax.fori_loop(0, SEQ, one_device, 0)

        for one in kept[2:]:
            one.flush()
        for one in kept:
            one.finish()


def attend(info, recv):
    devs = 8
    pairs = 17.8e6
    out_low, *rest = pl.pallas_call(
        functools.partial(attend_kernel, devs=devs),
        out_shape=(
            jax.ShapeDtypeStruct((SEQ, 64, HALF), BF16),
            jax.ShapeDtypeStruct((64, SEQ * HALF), F32),
            jax.ShapeDtypeStruct((1, SEQ * HALF), F32),
            jax.ShapeDtypeStruct((64, SEQ * ROWS), BF16),
            jax.ShapeDtypeStruct((128, SEQ * HALF), BF16),
        ),
        in_specs=[
            pl.BlockSpec(memory_space=pltpu.SMEM),
            pl.BlockSpec(memory_space=pl.ANY),
        ],
        out_specs=tuple(pl.BlockSpec(memory_space=pl.ANY) for _ in range(5)),
        scratch_shapes=[
            pltpu.VMEM((SEQ, SLOT, 128), BF16),
            pltpu.VMEM((SEQ, 64, HALF), BF16),
            pltpu.VMEM((64, SEQ * HALF), F32),
            pltpu.VMEM((1, SEQ * HALF), F32),
            pltpu.VMEM((144, SEQ * ROWS), BF16),
            pltpu.VMEM((128, SEQ * HALF), BF16),
            pltpu.SemaphoreType.DMA((9,)),
            pltpu.VMEM((80, devs * HALF), F32),
        ],
        compiler_params=pltpu.CompilerParams(vmem_limit_bytes=62 << 20),
        cost_estimate=pl.CostEstimate(
            flops=int(pairs * 1024), bytes_accessed=8 << 20, transcendentals=int(pairs)
        ),
        name="attend",
    )(info, recv)
    out_f, lse, kv_t, q_t = rest
    return out_low, recv, kv_t, q_t, out_f, lse


def attend_back_kernel(info, recv_far, kv_t_far, q_t_far, out_f_far, lse_far, grad_out_far, send_far, recv, kv_t, q_t, out_f, lse, grad_out, send, sems, grad_kv, do_t, grad_q, *, devs):
    tile_rows = devs * HALF
    span = devs * ROWS
    active, half, second = info[0], info[1], info[2]

    @pl.when(active == 1)
    def _():
        fars = (grad_out_far, recv_far, q_t_far, out_f_far, lse_far, kv_t_far)
        nears = (grad_out, recv, q_t, out_f, lse, kv_t)
        held = [Held(far, near, sems.at[i]) for i, (far, near) in enumerate(zip(fars, nears))]
        grad_kv[...] = jnp.zeros(grad_kv.shape, F32)
        held[0].ready()
        for d in range(SEQ):
            do_t[64:128, d * HALF : (d + 1) * HALF] = grad_out[d]
        do_t[0:64, :] = jnp.zeros((64, SEQ * HALF), BF16)
        for one in held:
            one.ready()

        third = third_keys(recv, tile_rows)

        def one_tile(t, _):
            start = t * span
            columns = pl.ds(pl.multiple_of(t * tile_rows, tile_rows), tile_rows)
            at = positions(half, start, tile_rows)
            first = first_keys(at, second, third)
            queries = q_t[:, columns]
            grads = do_t[:, columns]
            query_rows = queries.T
            grad_rows = grads.T
            delta = jnp.sum(
                grads[64:128, :].astype(F32) * out_f[:, columns], axis=0, keepdims=True
            )
            own_lse = lse[:, columns]
            far_lse = jnp.where(first >= start, -LOW, own_lse)
            grad_q[...] = jnp.zeros((64, tile_rows), F32)

            def update(kv, key_rows, left, row_lse, mask):
                here = slice(left, tile_rows)
                scores = dot(kv, queries[:, here]) * LOG2E
                probs = jnp.where(mask, jnp.exp2(scores - row_lse[:, here]), 0.0)
                grad_probs = dot(kv, grads[:, here])
                grad_scores = (probs * (grad_probs - delta[:, here])).astype(BF16)
                grad_kv[key_rows, :] += dot(grad_scores, query_rows[here, :]) + dot(
                    probs.astype(BF16), grad_rows[here, :]
                )
                grad_q[:, here] += dot(kv_t[0:64, key_rows], grad_scores)

            def step(j, _):
                kv = recv[pl.ds(j * 4, 4), 0:ROWS, :].reshape(1024, 128)
                key_at = j * 1024 + lax.broadcasted_iota(jnp.int32, (1024, 1), 0)
                update(kv, pl.ds(pl.multiple_of(j * 1024, 1024), 1024), 0, far_lse, key_at >= second)
                return 0

            lax.fori_loop(0, t * (span // 1024), step, 0)
            for i in range(devs // 2):
                left = 256 * i
                key_start = pl.multiple_of(start + 512 * i, 512)
                kv = recv[pl.ds(t * devs + 2 * i, 2), 0:ROWS, :].reshape(512, 128)
                key_at = key_start + lax.broadcasted_iota(jnp.int32, (512, 1), 0)
                allowed = (key_at >= first[:, left:]) & (key_at <= at[:, left:])
                update(kv, pl.ds(key_start, 512), left, own_lse, allowed)
            low = (grad_q[...] * HEAD_DIM**-0.5).astype(BF16)
            for i in range(devs):
                d = t * devs + i
                send[d, ROWS:, :] = low[:, i * HALF : (i + 1) * HALF]
                send[d, 0:ROWS, :] = grad_kv[pl.ds(pl.multiple_of(d * ROWS, ROWS), ROWS), :].astype(BF16)
            sending(t).start()
            return 0

        def sending(t):
            here = pl.ds(t * devs, devs)
            return pltpu.make_async_copy(send.at[here], send_far.at[here], sems.at[6 + t])

        def from_last(i, _):
            return one_tile(SEQ // devs - 1 - i, 0)

        lax.fori_loop(0, SEQ // devs, from_last, 0)
        for t in range(SEQ // devs):
            sending(t).wait()


def attend_back(info, recv, kv_t, q_t, out_f, lse, grad_out):
    devs = 8
    pairs = 17.8e6
    return pl.pallas_call(
        functools.partial(attend_back_kernel, devs=devs),
        out_shape=jax.ShapeDtypeStruct((SEQ, ROWS + 64, HALF), BF16),
        in_specs=[pl.BlockSpec(memory_space=pltpu.SMEM)]
        + [pl.BlockSpec(memory_space=pl.ANY)] * 6,
        out_specs=pl.BlockSpec(memory_space=pl.ANY),
        scratch_shapes=[
            pltpu.VMEM((SEQ, SLOT, 128), BF16),
            pltpu.VMEM((64, SEQ * ROWS), BF16),
            pltpu.VMEM((128, SEQ * HALF), BF16),
            pltpu.VMEM((64, SEQ * HALF), F32),
            pltpu.VMEM((1, SEQ * HALF), F32),
            pltpu.VMEM((SEQ, 64, HALF), BF16),
            pltpu.VMEM((SEQ, ROWS + 64, HALF), BF16),
            pltpu.SemaphoreType.DMA((14,)),
            pltpu.VMEM((SEQ * ROWS, 128), F32),
            pltpu.VMEM((128, SEQ * HALF), BF16),
            pltpu.VMEM((64, devs * HALF), F32),
        ],
        compiler_params=pltpu.CompilerParams(vmem_limit_bytes=62 << 20),
        cost_estimate=pl.CostEstimate(
            flops=int(pairs * 1024), bytes_accessed=8 << 20, transcendentals=int(pairs)
        ),
        name="attend_back",
    )(info, recv, kv_t, q_t, out_f, lse, grad_out)


def on_device(
    tokens,
    token_pos,
    token_pass,
    token_count,
    w_qkv,
    w_out,
    w_up,
    w_down,
    gain_attn,
    gain_mlp,
    pass_table,
    cotangent,
):
    here = lax.axis_index("seq")
    documents = (token_pos, token_pass, token_count)
    edge = jnp.where(here == 0, ROWS - 1, 0)
    second = here * ROWS + start_of(*documents, here, edge)
    third = third_start(start_of(*documents, here, ROWS - 1))
    group, place = here // 4, here % 4
    active = (place < 3).astype(jnp.int32)
    core = lax.axis_index("batch") % 2
    info = jnp.stack([active, (3 * group + place) % 2, second, here % 2, third, core])
    passes = token_pass[0][:, None]
    table = jnp.pad(pass_table, ((0, 8 - PASSES), (0, 0)))
    gain_a, gain_m = gain_attn[None], gain_mlp[None]
    stream_one = tokens[0]
    features = pltpu.VMEM((WIDTH, ROWS), BF16)
    acc = pltpu.VMEM((ROWS, WIDTH), F32)
    square = shape(ROWS, WIDTH)
    wide = shape(ROWS, WIDTH, dtype=F32)
    row = shape(1, WIDTH, dtype=F32)
    sent = shape(SEQ, SLOT, 128)
    sent_back = shape(SEQ, 64, 128)

    slots, normed_one = in_vmem(
        enter_kernel, "enter", documents, (gain_a,), (stream_one, w_qkv), (sent, square), [], 1e9
    )
    saved_one = attend(info, exchange(slots))
    slots, normed_two, stream_two, att_one, mid_one, midn_one, hidden_one, act_one = in_vmem(
        turn_kernel,
        "turn",
        info,
        (passes, table, gain_a, gain_m),
        (exchange(saved_one[0]), stream_one, w_out, w_up, w_down, w_qkv),
        (sent, square, wide, square, wide, square, shape(ROWS, FF, dtype=F32), shape(ROWS, FF)),
        [features, acc],
        3.6e9,
        {3: 1, 4: 0},
    )
    saved_two = attend(info, exchange(slots))
    slots, mixed, att_two, midn_two, act_two, dh_two, dy_two, dmid_two, gain_m_two = in_vmem(
        crest_kernel,
        "crest",
        info,
        (gain_m,),
        (exchange(saved_two[0]), stream_two, w_out, w_up, w_down, cotangent[0]),
        (sent_back, square, square, square, shape(ROWS, FF), shape(ROWS, FF), square, wide, row),
        [features, acc, acc, pltpu.VMEM((ROWS, FF), F32), pltpu.VMEM((ROWS, WIDTH), BF16)],
        5e9,
        {3: 1, 4: 0},
    )
    back = exchange(slots)
    recv = exchange(attend_back(info, *saved_two[1:], back))
    slots, dproj_two, dmid_one, *early = in_vmem(
        return_kernel,
        "return",
        info,
        (passes, gain_a, gain_m, gain_m_two),
        (recv, w_qkv, stream_two, dmid_two, hidden_one, w_down, w_up, mid_one, w_out,
         midn_one, midn_two, dh_two, act_one, act_two, cotangent[0], att_one, att_two, dy_two),
        (sent_back, shape(ROWS, 3 * WIDTH), wide, shape(WIDTH, FF), shape(FF, WIDTH), shape(WIDTH + 16, WIDTH)),
        [features, acc, pltpu.VMEM((ROWS, WIDTH), BF16), pltpu.VMEM((ROWS, FF), BF16),
         pltpu.VMEM((ROWS, WIDTH), BF16), pltpu.VMEM((1, WIDTH), F32)],
        1e10,
        {5: 0, 6: 1},
    )
    back = exchange(slots)
    early = lax.psum(tuple(early), ("seq", "batch"))
    sent_one = attend_back(info, *saved_one[1:], back)
    recv = exchange(sent_one)
    grad_tokens, dproj_one, gain_a_one = in_vmem(
        leave_kernel,
        "leave",
        info,
        (gain_a,),
        (recv, w_qkv, stream_one, dmid_one),
        (wide, shape(ROWS, 3 * WIDTH), row),
        [features],
        1e9,
    )
    (grad_two,) = in_vmem(
        grad_qkv_kernel,
        "grad_qkv_two",
        info,
        (),
        (normed_two, dproj_two),
        (shape(18, WIDTH, 128, dtype=F32),),
        [],
        9e8,
    )
    late = in_vmem(
        grad_qkv_both_kernel,
        "grad_qkv",
        info,
        (jnp.pad(gain_a_one.reshape(6, 128), ((0, 10), (0, 0))),),
        (normed_one, dproj_one, grad_two),
        (shape(LATE, 128),) * 2,
        [],
        9e8,
    )
    late, early = lax.optimization_barrier((late, early))
    late = across_chips(sum_cores(late).reshape(CHIPS, -1, 128))
    tail = early[2][WIDTH:].astype(F32)
    early = (early[0].astype(F32), early[1].astype(F32), early[2][:WIDTH].astype(F32))
    late, early = lax.optimization_barrier((late, early))
    late = jnp.sum(late.astype(F32), axis=0).astype(BF16)
    whole = across_chips(jnp.broadcast_to(late[None], (CHIPS, *late.shape))).reshape(-1, 128)
    late = (whole, swap(whole, 1))
    grad_up, grad_down, grad_out = early
    gain_a_sum = late[0][6912:6918].reshape(WIDTH).astype(F32)
    return (
        mixed[None],
        grad_tokens[None],
        widen(info[CORE : CORE + 1], *late),
        grad_out,
        grad_up,
        grad_down,
        tail[PASSES] + gain_a_sum,
        tail[PASSES + 1],
        tail[:PASSES],
    )


def solution(mesh):
    return jax.shard_map(
        on_device,
        mesh=mesh,
        in_specs=(
            P("batch", "seq", None),
            P("batch", "seq"),
            P("batch", "seq"),
            P("batch", "seq"),
            P(),
            P(),
            P(),
            P(),
            P(),
            P(),
            P(),
            P("batch", "seq", None),
        ),
        out_specs=(
            P("batch", "seq", None),
            P("batch", "seq", None),
            P(),
            P(),
            P(),
            P(),
            P(),
            P(),
            P(),
        ),
        check_vma=False,
    )
```

```python
import functools

import jax
import jax.numpy as jnp
from jax import lax
from jax.experimental import pallas as pl
from jax.experimental.pallas import tpu as pltpu
from jax.sharding import PartitionSpec as P

HEADS = 12
HEAD_DIM = 64
PASSES = 5
SEQ = 32
ROWS = 256
HALF = 128
SLOT = ROWS + 64 + 16
WIDTH = 768
FF = 3072
FF_BLOCK = 1024
EPS = 1e-5
LOG2E = 1.4426950408889634
LOW = -1e30
SMALL = 60.0
F32 = jnp.float32
BF16 = jnp.bfloat16

WORK = [3 * (e // 4) + e % 4 if e % 4 < 3 else None for e in range(SEQ)]
SLOT_OF = {w: e for e, w in enumerate(WORK) if w is not None}


def dot(left, right):
    return jnp.dot(left, right, preferred_element_type=F32)


def contract_rows(left, right):
    return lax.dot_general(left, right, (((0,), (0,)), ((), ())), preferred_element_type=F32)


def times_transposed(left, right):
    return lax.dot_general(left, right, (((1,), (1,)), ((), ())), preferred_element_type=F32)


def standardise(values):
    centered = values - jnp.mean(values, axis=-1, keepdims=True)
    inverse = lax.rsqrt(jnp.mean(centered * centered, axis=-1, keepdims=True) + EPS)
    return centered * inverse, inverse


def standardise_back(grad, gain, values):
    normal, inverse = standardise(values)
    scaled = grad * gain
    along = jnp.mean(scaled * normal, axis=-1, keepdims=True)
    grad_values = inverse * (scaled - jnp.mean(scaled, axis=-1, keepdims=True) - normal * along)
    return grad_values, jnp.sum(grad * normal, axis=0, keepdims=True)


GELU_A = 0.7978845608028654
GELU_B = 0.044715


def gelu(value):
    return 0.5 * value * (1.0 + jnp.tanh(GELU_A * (value + GELU_B * value * value * value)))


def gelu_slope(value):
    square = value * value
    bent = jnp.tanh(GELU_A * value * (1.0 + GELU_B * square))
    inner = GELU_A * (1.0 + 3.0 * GELU_B * square)
    return 0.5 * (1.0 + bent) + 0.5 * value * (1.0 - bent * bent) * inner


def slot_of(head, block, odd):
    this, other = SLOT_OF[2 * head + block], SLOT_OF[2 * head + 1 - block]
    return jnp.where(odd == 1, other, this)


class Held:
    def __init__(self, source, target, sem):
        self.target = target
        self.copy = pltpu.make_async_copy(source, target, sem)
        self.copy.start()
        self.waited = False

    def ready(self):
        if not self.waited:
            self.copy.wait()
            self.waited = True
        return self.target

    def __getitem__(self, at):
        return self.ready()[at]


class HeldBlocks:
    def __init__(self, source, target, sems, axis):
        self.source, self.target, self.sems, self.axis = source, target, sems, axis
        self.waited = False

    def copy(self, c):
        here = pl.ds(c * FF_BLOCK if isinstance(c, int) else pl.multiple_of(c * FF_BLOCK, FF_BLOCK), FF_BLOCK)
        at = (here, slice(None)) if self.axis == 0 else (slice(None), here)
        return pltpu.make_async_copy(self.source.at[at], self.target.at[at], self.sems.at[c])

    def wait(self, c):
        if not self.waited:
            self.copy(c).wait()

    def ready(self):
        assert self.waited
        return self.target

    def __getitem__(self, at):
        return self.target[at]


class Kept:
    def __init__(self, source, target, sem):
        self.source = source
        self.copy = pltpu.make_async_copy(source, target, sem)
        self.started = False

    def __getitem__(self, at):
        return self.source[at]

    def __setitem__(self, at, value):
        self.source[at] = value

    def flush(self):
        self.copy.start()
        self.started = True

    def finish(self):
        if not self.started:
            self.flush()
        self.copy.wait()


class KeptSlots(Kept):
    def __init__(self, source, target, sems):
        self.source = source
        self.copies = [pltpu.make_async_copy(source.at[e], target.at[e], sems.at[w]) for w, e in SLOT_OF.items()]
        self.started = True

    def flush_head(self, head):
        for half in range(2):
            self.copies[2 * head + half].start()

    def finish(self):
        for copy in self.copies:
            copy.wait()


def project(stream, gain, w_qkv, odd, third, slots, normed_out):
    normed = (standardise(stream)[0] * gain).astype(BF16)
    normed_out[...] = normed
    low_lanes = lax.broadcasted_iota(jnp.int32, (ROWS, 128), 1) < 64
    for pair in range(HEADS // 2):
        at = 128 * pair
        queries = dot(normed, w_qkv[:, at : at + 128]) * HEAD_DIM**-0.5
        keys = dot(normed, w_qkv[:, WIDTH + at : WIDTH + at + 128])
        values = dot(normed, w_qkv[:, 2 * WIDTH + at : 2 * WIDTH + at + 128])
        queries_t = queries.T.astype(BF16)
        first = jnp.where(low_lanes, keys, pltpu.roll(values, 64, 1)).astype(BF16)
        second = jnp.where(low_lanes, pltpu.roll(keys, 64, 1), values).astype(BF16)
        for j, both in enumerate((first, second)):
            head = 2 * pair + j
            for block in range(2):
                to = slot_of(head, block, odd)
                slots[to, 0:ROWS, :] = both
                slots[to, ROWS : ROWS + 64, :] = queries_t[
                    64 * j : 64 * j + 64, block * HALF : (block + 1) * HALF
                ]
                slots[to, ROWS + 64 : SLOT, :] = jnp.broadcast_to(third, (16, 128)).astype(BF16)
            slots.flush_head(head)


def gather_heads(recv, odd, row, target):
    for head in range(HEADS):
        for block in range(2):
            target[64 * head : 64 * head + 64, block * HALF : (block + 1) * HALF] = recv[
                slot_of(head, block, odd), row : row + 64, :
            ]


def scatter_heads(features, odd, slots):
    for head in range(HEADS):
        for block in range(2):
            slots[slot_of(head, block, odd)] = features[
                64 * head : 64 * head + 64, block * HALF : (block + 1) * HALF
            ]


def mix(recv, stream, odd, gain, weights, features, acc, att_out, mid_out, normed_out, hidden_out, act_out):
    gather_heads(recv, odd, 0, features)
    attended = features[...].T
    att_out[...] = attended
    mid = stream + dot(attended, weights[0][...])
    mid_out[...] = mid
    normed_out[...] = (standardise(mid)[0] * gain).astype(BF16)
    acc[...] = mid
    up, down = weights[1:]

    def step(c, _):
        here = pl.ds(pl.multiple_of(c * FF_BLOCK, FF_BLOCK), FF_BLOCK)
        up.wait(c)
        down.wait(c)
        hidden = dot(normed_out[...], up[:, here])
        hidden_out[:, here] = hidden
        active = gelu(hidden).astype(BF16)
        act_out[:, here] = active
        acc[...] += dot(active, down[here, :])
        return 0

    lax.fori_loop(0, FF // FF_BLOCK, step, 0)
    up.waited = down.waited = True


def mix_back(grad, odd, gain, mid, hidden, weights, acc, dz_out, dh_out, dy_out, dmid_out, gain_out, slots):
    out, up, down = weights
    dz_out[...] = grad.astype(BF16)
    acc[...] = jnp.zeros(acc.shape, F32)

    def step(c, _):
        here = pl.ds(pl.multiple_of(c * FF_BLOCK, FF_BLOCK), FF_BLOCK)
        up.wait(c)
        down.wait(c)
        grad_act = times_transposed(dz_out[...], down[here, :])
        low = (gelu_slope(hidden[:, here]) * grad_act).astype(BF16)
        dh_out[:, here] = low
        acc[...] += times_transposed(low, up[:, here])
        return 0

    lax.fori_loop(0, FF // FF_BLOCK, step, 0)
    up.waited = down.waited = True
    grad_mid, grad_gain = standardise_back(acc[...], gain, mid[...])
    gain_out[...] = grad_gain
    grad_mid = grad_mid + grad
    dmid_out[...] = grad_mid
    for done in (dh_out, dmid_out, dz_out):
        if isinstance(done, Kept):
            done.flush()
    low = grad_mid.astype(BF16)
    dy_out[...] = low
    scatter_heads(times_transposed(low, out[...]).T.astype(BF16), odd, slots)


def project_back(recv, odd, gain, stream, grad_mid, w_qkv, features, dproj_out, gain_out):
    gather_heads(recv, odd, ROWS, features)
    dproj_out[:, 0:WIDTH] = features[...].T
    low_lanes = lax.broadcasted_iota(jnp.int32, (ROWS, 128), 1) < 64
    for pair in range(HEADS // 2):
        at = 128 * pair
        both = []
        for head in (2 * pair, 2 * pair + 1):
            one, two = recv[SLOT_OF[2 * head], 0:ROWS, :], recv[SLOT_OF[2 * head + 1], 0:ROWS, :]
            both.append(one.astype(F32) + two.astype(F32))
        keys = jnp.where(low_lanes, both[0], pltpu.roll(both[1], 64, 1)).astype(BF16)
        values = jnp.where(low_lanes, pltpu.roll(both[0], 64, 1), both[1]).astype(BF16)
        dproj_out[:, WIDTH + at : WIDTH + at + 128] = keys
        dproj_out[:, 2 * WIDTH + at : 2 * WIDTH + at + 128] = values
    grad_normed = times_transposed(dproj_out[...], w_qkv[...])
    grad_stream, grad_gain = standardise_back(grad_normed, gain, stream[...].astype(F32))
    gain_out[...] = grad_gain
    return grad_stream + grad_mid[...]


def start_of(pos, passes, count, here, at):
    return at - (pos[0, at] * count[0, at] + passes[0, at])


def third_start(start):
    return jnp.where((start < 0) | (start > ROWS), ROWS, start)


def enter_kernel(pos, passes, count, gain_attn, ins, outs):
    tokens, w_qkv = ins
    slots, normed = outs
    here = lax.axis_index("seq")
    third = third_start(start_of(pos, passes, count, here, ROWS - 1))
    project(tokens[...].astype(F32), gain_attn[...].reshape(1, WIDTH), w_qkv, here % 2, third.astype(F32), slots, normed)


def as_column(row):
    return jnp.broadcast_to(row.astype(F32), (8, ROWS)).T[:, 0:1]


def turn_kernel(info, passes, table, gain_attn, gain_mlp, ins, outs, features, acc):
    recv, tokens, w_out, w_up, w_down, w_qkv = ins
    slots, normed, second, att, mid, mid_normed, hidden, act = outs
    odd = info[3]
    mix(recv, tokens[...].astype(F32), odd, gain_mlp[...].reshape(1, WIDTH), (w_out, w_up, w_down), features, acc, att, mid, mid_normed, hidden, act)
    for out in (att, mid, mid_normed, hidden, act):
        out.flush()
    stream = acc[...]
    column = as_column(passes[...])
    for row in range(PASSES):
        stream = stream + jnp.where(column == row, table[row : row + 1, :], 0.0)
    second[...] = stream
    second.flush()
    project(stream, gain_attn[...].reshape(1, WIDTH), w_qkv, odd, info[4].astype(F32), slots, normed)


def crest_kernel(info, gain_mlp, ins, outs, features, acc, mid, hidden, dz):
    recv, stream, w_out, w_up, w_down, cotangent = ins
    slots, mixed, att, mid_normed, act, dh, dy, dmid, gain_out = outs
    odd = info[3]
    gain = gain_mlp[...].reshape(1, WIDTH)
    mix(recv, stream[...], odd, gain, (w_out, w_up, w_down), features, acc, att, mid, mid_normed, hidden, act)
    mixed[...] = acc[...].astype(BF16)
    for out in (att, mid_normed, act, mixed):
        out.flush()
    mix_back(cotangent[...].astype(F32), odd, gain, mid, hidden, (w_out, w_up, w_down), acc, dz, dh, dy, dmid, gain_out, slots)


def return_kernel(info, passes, gain_attn, gain_mlp, gain_m_two, ins, outs, features, acc, dz, dh, dy, gain_m):
    (recv, w_qkv, stream, grad_mid, hidden, w_down, w_up, mid, w_out,
     mid_one, mid_two, dh_two, act_one, act_two, dz_two, att_one, att_two, dy_two) = ins
    slots, dproj, dmid, up_out, down_out, out_out = outs
    odd = info[3]
    small = jnp.zeros((16, WIDTH), F32)
    at = lax.broadcasted_iota(jnp.int32, (16, 1), 0)
    grad = project_back(recv, odd, gain_attn[...].reshape(1, WIDTH), stream, grad_mid, w_qkv, features, dproj, gain_m)
    dproj.flush()
    small = jnp.where(at == PASSES, gain_m[...], small)
    column = as_column(passes[...])
    for row in range(PASSES):
        part = jnp.sum(jnp.where(column == row, grad, 0.0), axis=0, keepdims=True)
        small = jnp.where(at == row, part, small)
    mix_back(grad, odd, gain_mlp[...].reshape(1, WIDTH), mid, hidden.ready(), (w_out, w_up, w_down), acc, dz, dh, dy, dmid, gain_m, slots)
    slots.flush()
    small = jnp.where(at == PASSES + 1, gain_m[...] + gain_m_two[...], small)
    weight_gradients(
        (mid_one, dh, mid_two, dh_two, act_one, dz, act_two, dz_two, att_one, dy, att_two, dy_two),
        small, up_out, down_out, out_out,
    )


def leave_kernel(info, gain_attn, ins, outs, features):
    recv, w_qkv, tokens, grad_mid = ins
    grad_tokens, dproj, gain_out = outs
    grad_tokens[...] = project_back(recv, info[3], gain_attn[...].reshape(1, WIDTH), tokens, grad_mid, w_qkv, features, dproj, gain_out)


def shape(*dims, dtype=BF16):
    return jax.ShapeDtypeStruct(dims, dtype)


def in_vmem(kernel, name, info, small, arrays, outs, scratch, flops, split={}):
    vmem = pl.BlockSpec(memory_space=pltpu.VMEM)
    hbm = pl.BlockSpec(memory_space=pl.ANY)
    ins, count = len(arrays), len(arrays) + len(outs)

    info = info if isinstance(info, tuple) else (info,)

    def body(*refs):
        known, refs = refs[: len(info)], refs[len(info) :]
        few, refs = refs[: len(small)], refs[len(small) :]
        far, near, sems, rest = refs[:count], refs[count : 2 * count], refs[2 * count], refs[2 * count + 1 :]
        held, blocks = [], []
        for i in range(ins):
            if i in split:
                own = sems.at[pl.ds(count + 6 * len(blocks), 6)]
                held.append(HeldBlocks(far[i], near[i], own, split[i]))
                blocks.append(held[-1])
                if len(blocks) == 2:
                    for c in range(FF // FF_BLOCK):
                        for one in blocks:
                            one.copy(c).start()
            else:
                held.append(Held(far[i], near[i], sems.at[i]))
        kept = [Kept(near[i], far[i], sems.at[i]) for i in range(ins, count)]
        if outs[0].shape == (SEQ, SLOT, 128):
            kept[0] = KeptSlots(near[ins], far[ins], sems.at[pl.ds(count + 12, 24)])
        kernel(*known, *few, held, kept, *rest)
        for one in kept:
            if not one.started:
                one.flush()
        for one in held:
            one.ready()
        for one in kept:
            one.finish()

    return pl.pallas_call(
        body,
        out_shape=tuple(outs),
        in_specs=[pl.BlockSpec(memory_space=pltpu.SMEM)] * len(info) + [vmem] * len(small) + [hbm] * ins,
        out_specs=(hbm,) * len(outs),
        scratch_shapes=[pltpu.VMEM(x.shape, x.dtype) for x in (*arrays, *outs)]
        + [pltpu.SemaphoreType.DMA((count + 36,))]
        + scratch,
        compiler_params=pltpu.CompilerParams(vmem_limit_bytes=62 << 20),
        cost_estimate=pl.CostEstimate(flops=int(flops), bytes_accessed=16 << 20, transcendentals=1 << 20),
        name=name,
    )(*info, *small, *arrays)


LATE = 7168
CORE = 5


def weight_gradients(factors, small, up, down, out):
    mid_one, dh_one, mid_two, dh_two, act_one, dz_one, act_two, dz_two, att_one, dy_one, att_two, dy_two = factors
    for one in (dh_two, act_one, act_two):
        one.ready()

    def left(one, two):
        return jnp.concatenate([one, two], axis=0).T

    mid = left(mid_one[...], mid_two[...])

    def step_up(c, _):
        here = pl.ds(pl.multiple_of(c * 512, 512), 512)
        up[:, here] = dot(mid, jnp.concatenate([dh_one[:, here], dh_two[:, here]], axis=0)).astype(BF16)
        return 0

    lax.fori_loop(0, 6, step_up, 0)
    up.flush()
    dz = jnp.concatenate([dz_one[...], dz_two[...]], axis=0)

    def step_down(c, _):
        here = pl.ds(pl.multiple_of(c * 512, 512), 512)
        down[here, :] = dot(left(act_one[:, here], act_two[:, here]), dz).astype(BF16)
        return 0

    lax.fori_loop(0, 6, step_down, 0)
    down.flush()
    dy = jnp.concatenate([dy_one[...], dy_two[...]], axis=0)
    out[0:WIDTH, :] = dot(left(att_one[...], att_two[...]), dy).astype(BF16)
    out[WIDTH:, :] = small.astype(BF16)


def grad_qkv_kernel(info, ins, outs):
    normed, dproj = ins
    left = normed[...].T
    dproj.ready()

    def step(c, _):
        result = dot(left, dproj[:, pl.ds(pl.multiple_of(c * 384, 384), 384)])
        for i in range(3):
            outs[0][3 * c + i] = result[:, 128 * i : 128 * i + 128]
        return 0

    lax.fori_loop(0, 6, step, 0)


def grad_qkv_both_kernel(info, gains, ins, outs):
    normed, dproj, before = ins
    left = normed[...].T
    dproj.ready(), before.ready()
    core = info[CORE]

    def step(c, _):
        result = dot(left, dproj[:, pl.ds(pl.multiple_of(c * 384, 384), 384)])
        for to, out in enumerate(outs):
            for half in range(2):

                @pl.when((half ^ core) == to)
                def _():
                    for i in range(3):
                        for part in range(3):
                            rows = slice(384 * half + 128 * part, 384 * half + 128 * part + 128)
                            value = result[rows, 128 * i : 128 * i + 128] + before[3 * c + i, rows, :]
                            at = pl.multiple_of(part * 2304 + (3 * c + i) * 128, 128)
                            out[pl.ds(at, 128), :] = value.astype(BF16)

        return 0

    lax.fori_loop(0, 6, step, 0)
    for out in outs:
        out[6912:6928, :] = gains[...].astype(BF16)


def widen_kernel(core, mine, other, out):
    half = pl.program_id(0) // 3

    def put(ref):
        for i in range(18):
            out[:, 128 * i : 128 * i + 128] = ref[128 * i : 128 * i + 128, :].astype(F32)

    @pl.when(half == core[0])
    def _():
        put(mine)

    @pl.when(half != core[0])
    def _():
        put(other)


def widen(core, mine, other):
    def place(own):
        def index(i, core):
            low = core[0] == (0 if own else 1)
            return (jnp.where(low, jnp.minimum(i, 2), jnp.maximum(i - 3, 0)), 0)

        return pl.BlockSpec((2304, 128), index)

    return pl.pallas_call(
        widen_kernel,
        out_shape=shape(WIDTH, 3 * WIDTH, dtype=F32),
        grid_spec=pltpu.PrefetchScalarGridSpec(
            num_scalar_prefetch=1,
            grid=(6,),
            in_specs=[place(True), place(False)],
            out_specs=pl.BlockSpec((128, 3 * WIDTH), lambda i, core: (i, 0)),
        ),
        compiler_params=pltpu.CompilerParams(vmem_limit_bytes=20 << 20),
        name="widen",
    )(core, mine, other)


def swap(value, bit):
    return lax.ppermute(value, "batch", [(i, i ^ bit) for i in range(4)])


def exchange(slots):
    return lax.all_to_all(slots, "seq", 0, 0)


def sum_cores(partial):
    mine, other = partial
    return (mine.astype(F32) + swap(other, 1).astype(F32)).astype(BF16)


CHIPS = 64


def across_chips(slots):
    groups = [[s * 4 + z * 2 + c for s in range(SEQ) for z in range(2)] for c in range(2)]
    return lax.all_to_all(slots, ("seq", "batch"), 0, 0, axis_index_groups=groups)


def positions(half, first_row, count):
    at = lax.broadcasted_iota(jnp.int32, (1, count), 1)
    block = at // HALF
    return first_row + block * ROWS + ((half + block) % 2) * HALF + at % HALF


def third_keys(recv, count):
    last = recv[SEQ - 1, ROWS + 64 : SLOT, :].astype(F32)[0:1].astype(jnp.int32)
    row = last + (SEQ - 1) * ROWS
    return jnp.concatenate([row] * (count // 128), axis=1)


def first_keys(at, second, third):
    return jnp.where(at < second, 0, jnp.where(at < third, second, third))


def attend_kernel(info, recv_far, out_low_far, out_f_far, lse_far, k_t_far, q_t_far, recv, out_low, out_f, lse, kv_t, q_t, sems, acc, *, devs):
    tile_rows = devs * HALF
    span = devs * ROWS
    active, half, second = info[0], info[1], info[2]

    @pl.when(active == 1)
    def _():
        parts = [
            Held(recv_far.at[8 * i : 8 * i + 8], recv.at[8 * i : 8 * i + 8], sems.at[i]) for i in range(4)
        ]
        fars = (k_t_far, q_t_far, out_low_far, out_f_far, lse_far)
        kept = [
            Kept(near, far, sems.at[4 + i])
            for i, (near, far) in enumerate(zip((kv_t.at[0:64], q_t, out_low, out_f, lse), fars))
        ]
        ones = (lax.broadcasted_iota(jnp.int32, (16, ROWS), 0) == 0).astype(BF16)
        for d in range(SEQ):
            parts[d // 8].ready()
            keys = slice(d * ROWS, (d + 1) * ROWS)
            kv_t[0:128, keys] = recv[d, 0:ROWS, :].T
            kv_t[128:144, keys] = ones
            q_t[0:64, d * HALF : (d + 1) * HALF] = recv[d, ROWS : ROWS + 64, :]
        q_t[64:128, :] = jnp.zeros((64, SEQ * HALF), BF16)
        kept[0].flush()
        kept[1].flush()

        third = third_keys(recv, tile_rows)

        def square_top(features):
            wide = features.astype(F32)
            return jnp.max(jnp.sum(wide * wide, axis=0, keepdims=True))

        key_top = jnp.float32(0.0)
        query_top = jnp.float32(0.0)
        for c in range(8):
            key_top = jnp.maximum(key_top, square_top(kv_t[0:64, 1024 * c : 1024 * c + 1024]))
        for c in range(4):
            query_top = jnp.maximum(query_top, square_top(q_t[0:64, 1024 * c : 1024 * c + 1024]))
        small = key_top * query_top < (SMALL / LOG2E) ** 2

        def one_tile(t, _):
            start = t * span
            columns = pl.ds(pl.multiple_of(t * tile_rows, tile_rows), tile_rows)
            at = positions(half, start, tile_rows)
            first = first_keys(at, second, third)
            acc[...] = jnp.zeros((80, tile_rows), F32)
            queries = q_t[:, columns]

            def update(kv, key_rows, left, mask):
                here = slice(left, tile_rows)
                weights = jnp.exp2(dot(kv, queries[:, here]) * LOG2E)
                if mask is not None:
                    weights = jnp.where(mask, weights, 0.0)
                acc[:, here] = acc[:, here] + dot(kv_t[64:144, key_rows], weights.astype(BF16))

            def step(j, _):
                kv = recv[pl.ds(j * 4, 4), 0:ROWS, :].reshape(1024, 128)
                update(kv, pl.ds(pl.multiple_of(j * 1024, 1024), 1024), 0, None)
                return 0

            lax.fori_loop(0, t * (span // 1024), step, 0)
            acc[...] = jnp.where(first >= start, 0.0, acc[...])
            for i in range(devs // 2):
                left = 256 * i
                key_start = pl.multiple_of(start + 512 * i, 512)
                kv = recv[pl.ds(t * devs + 2 * i, 2), 0:ROWS, :].reshape(512, 128)
                key_at = key_start + lax.broadcasted_iota(jnp.int32, (512, 1), 0)
                allowed = (key_at >= first[:, left:]) & (key_at <= at[:, left:])
                update(kv, pl.ds(key_start, 512), left, allowed)
            total = acc[64:65, :]
            result = acc[0:64, :] / total
            out_f[:, columns] = result
            lse[:, columns] = jnp.log2(total)
            low = result.astype(BF16)
            for i in range(devs):
                out_low[t * devs + i] = low[:, i * HALF : (i + 1) * HALF]

            @pl.when(t == 0)
            def _():
                key_at = lax.broadcasted_iota(jnp.int32, (1, ROWS), 1)
                kv_t[64:144, 0:ROWS] = jnp.where(key_at >= second, kv_t[64:144, 0:ROWS], 0.0).astype(BF16)

            return 0

        def one_device(d, _):
            columns = pl.ds(pl.multiple_of(d * HALF, HALF), HALF)
            at = d * ROWS + (half + d) % 2 * HALF + lax.broadcasted_iota(jnp.int32, (1, HALF), 1)
            first = first_keys(at, second, third_keys(recv, HALF))
            queries = q_t[:, columns]

            def step(j, state):
                old_top, old_acc = state
                kv = recv[pl.ds(j * 2, 2), 0:ROWS, :].reshape(512, 128)
                key_at = j * 512 + lax.broadcasted_iota(jnp.int32, (512, 1), 0)
                allowed = (key_at >= first) & (key_at <= at)
                scores = jnp.where(allowed, dot(kv, queries) * LOG2E, LOW)
                new_top = jnp.maximum(old_top, jnp.max(scores, axis=0, keepdims=True))
                weights = jnp.exp2(scores - new_top).astype(BF16)
                keys = pl.ds(pl.multiple_of(j * 512, 512), 512)
                return new_top, old_acc * jnp.exp2(old_top - new_top) + dot(kv_t[64:144, keys], weights)

            state = (jnp.full((1, HALF), LOW, F32), jnp.zeros((80, HALF), F32))
            top, state = lax.fori_loop(0, d // 2 + 1, step, state)
            total = state[64:65, :]
            result = state[0:64, :] / total
            out_f[:, columns] = result
            lse[:, columns] = top + jnp.log2(total)
            out_low[d] = result.astype(BF16)
            return 0

        @pl.when(small)
        def _():
            lax.fori_loop(0, SEQ // devs, one_tile, 0)

        @pl.when(jnp.logical_not(small))
        def _():
            lax.fori_loop(0, SEQ, one_device, 0)

        for one in kept[2:]:
            one.flush()
        for one in kept:
            one.finish()


def attend(info, recv):
    devs = 8
    pairs = 17.8e6
    out_low, *rest = pl.pallas_call(
        functools.partial(attend_kernel, devs=devs),
        out_shape=(
            jax.ShapeDtypeStruct((SEQ, 64, HALF), BF16),
            jax.ShapeDtypeStruct((64, SEQ * HALF), F32),
            jax.ShapeDtypeStruct((1, SEQ * HALF), F32),
            jax.ShapeDtypeStruct((64, SEQ * ROWS), BF16),
            jax.ShapeDtypeStruct((128, SEQ * HALF), BF16),
        ),
        in_specs=[
            pl.BlockSpec(memory_space=pltpu.SMEM),
            pl.BlockSpec(memory_space=pl.ANY),
        ],
        out_specs=tuple(pl.BlockSpec(memory_space=pl.ANY) for _ in range(5)),
        scratch_shapes=[
            pltpu.VMEM((SEQ, SLOT, 128), BF16),
            pltpu.VMEM((SEQ, 64, HALF), BF16),
            pltpu.VMEM((64, SEQ * HALF), F32),
            pltpu.VMEM((1, SEQ * HALF), F32),
            pltpu.VMEM((144, SEQ * ROWS), BF16),
            pltpu.VMEM((128, SEQ * HALF), BF16),
            pltpu.SemaphoreType.DMA((9,)),
            pltpu.VMEM((80, devs * HALF), F32),
        ],
        compiler_params=pltpu.CompilerParams(vmem_limit_bytes=62 << 20),
        cost_estimate=pl.CostEstimate(
            flops=int(pairs * 1024), bytes_accessed=8 << 20, transcendentals=int(pairs)
        ),
        name="attend",
    )(info, recv)
    out_f, lse, kv_t, q_t = rest
    return out_low, recv, kv_t, q_t, out_f, lse


def attend_back_kernel(info, recv_far, kv_t_far, q_t_far, out_f_far, lse_far, grad_out_far, send_far, recv, kv_t, q_t, out_f, lse, grad_out, send, sems, grad_kv, do_t, grad_q, *, devs):
    tile_rows = devs * HALF
    span = devs * ROWS
    active, half, second = info[0], info[1], info[2]

    @pl.when(active == 1)
    def _():
        fars = (grad_out_far, recv_far, q_t_far, out_f_far, lse_far, kv_t_far)
        nears = (grad_out, recv, q_t, out_f, lse, kv_t)
        held = [Held(far, near, sems.at[i]) for i, (far, near) in enumerate(zip(fars, nears))]
        grad_kv[...] = jnp.zeros(grad_kv.shape, F32)
        held[0].ready()
        for d in range(SEQ):
            do_t[64:128, d * HALF : (d + 1) * HALF] = grad_out[d]
        do_t[0:64, :] = jnp.zeros((64, SEQ * HALF), BF16)
        for one in held:
            one.ready()

        third = third_keys(recv, tile_rows)

        def one_tile(t, _):
            start = t * span
            columns = pl.ds(pl.multiple_of(t * tile_rows, tile_rows), tile_rows)
            at = positions(half, start, tile_rows)
            first = first_keys(at, second, third)
            queries = q_t[:, columns]
            grads = do_t[:, columns]
            query_rows = queries.T
            grad_rows = grads.T
            delta = jnp.sum(
                grads[64:128, :].astype(F32) * out_f[:, columns], axis=0, keepdims=True
            )
            own_lse = lse[:, columns]
            far_lse = jnp.where(first >= start, -LOW, own_lse)
            grad_q[...] = jnp.zeros((64, tile_rows), F32)

            def update(kv, key_rows, left, row_lse, mask):
                here = slice(left, tile_rows)
                scores = dot(kv, queries[:, here]) * LOG2E
                probs = jnp.where(mask, jnp.exp2(scores - row_lse[:, here]), 0.0)
                grad_probs = dot(kv, grads[:, here])
                grad_scores = (probs * (grad_probs - delta[:, here])).astype(BF16)
                grad_kv[key_rows, :] += dot(grad_scores, query_rows[here, :]) + dot(
                    probs.astype(BF16), grad_rows[here, :]
                )
                grad_q[:, here] += dot(kv_t[0:64, key_rows], grad_scores)

            def step(j, _):
                kv = recv[pl.ds(j * 4, 4), 0:ROWS, :].reshape(1024, 128)
                key_at = j * 1024 + lax.broadcasted_iota(jnp.int32, (1024, 1), 0)
                update(kv, pl.ds(pl.multiple_of(j * 1024, 1024), 1024), 0, far_lse, key_at >= second)
                return 0

            lax.fori_loop(0, t * (span // 1024), step, 0)
            for i in range(devs // 2):
                left = 256 * i
                key_start = pl.multiple_of(start + 512 * i, 512)
                kv = recv[pl.ds(t * devs + 2 * i, 2), 0:ROWS, :].reshape(512, 128)
                key_at = key_start + lax.broadcasted_iota(jnp.int32, (512, 1), 0)
                allowed = (key_at >= first[:, left:]) & (key_at <= at[:, left:])
                update(kv, pl.ds(key_start, 512), left, own_lse, allowed)
            low = (grad_q[...] * HEAD_DIM**-0.5).astype(BF16)
            for i in range(devs):
                d = t * devs + i
                send[d, ROWS:, :] = low[:, i * HALF : (i + 1) * HALF]
                send[d, 0:ROWS, :] = grad_kv[pl.ds(pl.multiple_of(d * ROWS, ROWS), ROWS), :].astype(BF16)
            sending(t).start()
            return 0

        def sending(t):
            here = pl.ds(t * devs, devs)
            return pltpu.make_async_copy(send.at[here], send_far.at[here], sems.at[6 + t])

        def from_last(i, _):
            return one_tile(SEQ // devs - 1 - i, 0)

        lax.fori_loop(0, SEQ // devs, from_last, 0)
        for t in range(SEQ // devs):
            sending(t).wait()


def attend_back(info, recv, kv_t, q_t, out_f, lse, grad_out):
    devs = 8
    pairs = 17.8e6
    return pl.pallas_call(
        functools.partial(attend_back_kernel, devs=devs),
        out_shape=jax.ShapeDtypeStruct((SEQ, ROWS + 64, HALF), BF16),
        in_specs=[pl.BlockSpec(memory_space=pltpu.SMEM)]
        + [pl.BlockSpec(memory_space=pl.ANY)] * 6,
        out_specs=pl.BlockSpec(memory_space=pl.ANY),
        scratch_shapes=[
            pltpu.VMEM((SEQ, SLOT, 128), BF16),
            pltpu.VMEM((64, SEQ * ROWS), BF16),
            pltpu.VMEM((128, SEQ * HALF), BF16),
            pltpu.VMEM((64, SEQ * HALF), F32),
            pltpu.VMEM((1, SEQ * HALF), F32),
            pltpu.VMEM((SEQ, 64, HALF), BF16),
            pltpu.VMEM((SEQ, ROWS + 64, HALF), BF16),
            pltpu.SemaphoreType.DMA((14,)),
            pltpu.VMEM((SEQ * ROWS, 128), F32),
            pltpu.VMEM((128, SEQ * HALF), BF16),
            pltpu.VMEM((64, devs * HALF), F32),
        ],
        compiler_params=pltpu.CompilerParams(vmem_limit_bytes=62 << 20),
        cost_estimate=pl.CostEstimate(
            flops=int(pairs * 1024), bytes_accessed=8 << 20, transcendentals=int(pairs)
        ),
        name="attend_back",
    )(info, recv, kv_t, q_t, out_f, lse, grad_out)


def on_device(
    tokens,
    token_pos,
    token_pass,
    token_count,
    w_qkv,
    w_out,
    w_up,
    w_down,
    gain_attn,
    gain_mlp,
    pass_table,
    cotangent,
):
    here = lax.axis_index("seq")
    documents = (token_pos, token_pass, token_count)
    edge = jnp.where(here == 0, ROWS - 1, 0)
    second = here * ROWS + start_of(*documents, here, edge)
    third = third_start(start_of(*documents, here, ROWS - 1))
    group, place = here // 4, here % 4
    active = (place < 3).astype(jnp.int32)
    core = lax.axis_index("batch") % 2
    info = jnp.stack([active, (3 * group + place) % 2, second, here % 2, third, core])
    passes = token_pass
    table = jnp.pad(pass_table, ((0, 8 - PASSES), (0, 0)))
    gain_a, gain_m = gain_attn, gain_mlp
    stream_one = tokens[0]
    features = pltpu.VMEM((WIDTH, ROWS), BF16)
    acc = pltpu.VMEM((ROWS, WIDTH), F32)
    square = shape(ROWS, WIDTH)
    wide = shape(ROWS, WIDTH, dtype=F32)
    row = shape(1, WIDTH, dtype=F32)
    sent = shape(SEQ, SLOT, 128)
    sent_back = shape(SEQ, 64, 128)

    slots, normed_one = in_vmem(
        enter_kernel, "enter", documents, (gain_a,), (stream_one, w_qkv), (sent, square), [], 1e9
    )
    recv = exchange(slots)
    recv, passes, table, gain_m = lax.optimization_barrier((recv, passes, table, gain_m))
    saved_one = attend(info, recv)
    slots, normed_two, stream_two, att_one, mid_one, midn_one, hidden_one, act_one = in_vmem(
        turn_kernel,
        "turn",
        info,
        (passes, table, gain_a, gain_m),
        (exchange(saved_one[0]), stream_one, w_out, w_up, w_down, w_qkv),
        (sent, square, wide, square, wide, square, shape(ROWS, FF, dtype=F32), shape(ROWS, FF)),
        [features, acc],
        3.6e9,
        {3: 1, 4: 0},
    )
    saved_two = attend(info, exchange(slots))
    slots, mixed, att_two, midn_two, act_two, dh_two, dy_two, dmid_two, gain_m_two = in_vmem(
        crest_kernel,
        "crest",
        info,
        (gain_m,),
        (exchange(saved_two[0]), stream_two, w_out, w_up, w_down, cotangent[0]),
        (sent_back, square, square, square, shape(ROWS, FF), shape(ROWS, FF), square, wide, row),
        [features, acc, acc, pltpu.VMEM((ROWS, FF), F32), pltpu.VMEM((ROWS, WIDTH), BF16)],
        5e9,
        {3: 1, 4: 0},
    )
    back = exchange(slots)
    recv = exchange(attend_back(info, *saved_two[1:], back))
    slots, dproj_two, dmid_one, *early = in_vmem(
        return_kernel,
        "return",
        info,
        (passes, gain_a, gain_m, gain_m_two),
        (recv, w_qkv, stream_two, dmid_two, hidden_one, w_down, w_up, mid_one, w_out,
         midn_one, midn_two, dh_two, act_one, act_two, cotangent[0], att_one, att_two, dy_two),
        (sent_back, shape(ROWS, 3 * WIDTH), wide, shape(WIDTH, FF), shape(FF, WIDTH), shape(WIDTH + 16, WIDTH)),
        [features, acc, pltpu.VMEM((ROWS, WIDTH), BF16), pltpu.VMEM((ROWS, FF), BF16),
         pltpu.VMEM((ROWS, WIDTH), BF16), pltpu.VMEM((1, WIDTH), F32)],
        1e10,
        {5: 0, 6: 1},
    )
    back = exchange(slots)
    early = lax.psum(tuple(early), ("seq", "batch"))
    sent_one = attend_back(info, *saved_one[1:], back)
    recv = exchange(sent_one)
    grad_tokens, dproj_one, gain_a_one = in_vmem(
        leave_kernel,
        "leave",
        info,
        (gain_a,),
        (recv, w_qkv, stream_one, dmid_one),
        (wide, shape(ROWS, 3 * WIDTH), row),
        [features],
        1e9,
    )
    (grad_two,) = in_vmem(
        grad_qkv_kernel,
        "grad_qkv_two",
        info,
        (),
        (normed_two, dproj_two),
        (shape(18, WIDTH, 128, dtype=F32),),
        [],
        9e8,
    )
    late = in_vmem(
        grad_qkv_both_kernel,
        "grad_qkv",
        info,
        (jnp.pad(gain_a_one.reshape(6, 128), ((0, 10), (0, 0))),),
        (normed_one, dproj_one, grad_two),
        (shape(LATE, 128),) * 2,
        [],
        9e8,
    )
    late, early = lax.optimization_barrier((late, early))
    late = across_chips(sum_cores(late).reshape(CHIPS, -1, 128))
    tail = early[2][WIDTH:].astype(F32)
    early = (early[0].astype(F32), early[1].astype(F32), early[2][:WIDTH].astype(F32))
    late, early = lax.optimization_barrier((late, early))
    late = jnp.sum(late.astype(F32), axis=0).astype(BF16)
    whole = across_chips(jnp.broadcast_to(late[None], (CHIPS, *late.shape))).reshape(-1, 128)
    late = (whole, swap(whole, 1))
    grad_up, grad_down, grad_out = early
    gain_a_sum = late[0][6912:6918].reshape(WIDTH).astype(F32)
    return (
        mixed[None],
        grad_tokens[None],
        widen(info[CORE : CORE + 1], *late),
        grad_out,
        grad_up,
        grad_down,
        tail[PASSES] + gain_a_sum,
        tail[PASSES + 1],
        tail[:PASSES],
    )


def solution(mesh):
    return jax.shard_map(
        on_device,
        mesh=mesh,
        in_specs=(
            P("batch", "seq", None),
            P("batch", "seq"),
            P("batch", "seq"),
            P("batch", "seq"),
            P(),
            P(),
            P(),
            P(),
            P(),
            P(),
            P(),
            P("batch", "seq", None),
        ),
        out_specs=(
            P("batch", "seq", None),
            P("batch", "seq", None),
            P(),
            P(),
            P(),
            P(),
            P(),
            P(),
            P(),
        ),
        check_vma=False,
    )
```

```python
import functools

import jax
import jax.numpy as jnp
from jax import lax
from jax.experimental import pallas as pl
from jax.experimental.pallas import tpu as pltpu
from jax.sharding import PartitionSpec as P

HEADS = 12
HEAD_DIM = 64
PASSES = 5
SEQ = 32
ROWS = 256
HALF = 128
SLOT = ROWS + 64 + 16
WIDTH = 768
FF = 3072
FF_BLOCK = 1024
EPS = 1e-5
LOG2E = 1.4426950408889634
LOW = -1e30
SMALL = 60.0
F32 = jnp.float32
BF16 = jnp.bfloat16

WORK = [3 * (e // 4) + e % 4 if e % 4 < 3 else None for e in range(SEQ)]
SLOT_OF = {w: e for e, w in enumerate(WORK) if w is not None}


def dot(left, right):
    return jnp.dot(left, right, preferred_element_type=F32)


def contract_rows(left, right):
    return lax.dot_general(left, right, (((0,), (0,)), ((), ())), preferred_element_type=F32)


def times_transposed(left, right):
    return lax.dot_general(left, right, (((1,), (1,)), ((), ())), preferred_element_type=F32)


def standardise(values):
    centered = values - jnp.mean(values, axis=-1, keepdims=True)
    inverse = lax.rsqrt(jnp.mean(centered * centered, axis=-1, keepdims=True) + EPS)
    return centered * inverse, inverse


def standardise_back(grad, gain, values):
    normal, inverse = standardise(values)
    scaled = grad * gain
    along = jnp.mean(scaled * normal, axis=-1, keepdims=True)
    grad_values = inverse * (scaled - jnp.mean(scaled, axis=-1, keepdims=True) - normal * along)
    return grad_values, jnp.sum(grad * normal, axis=0, keepdims=True)


GELU_A = 0.7978845608028654
GELU_B = 0.044715


def gelu(value):
    return 0.5 * value * (1.0 + jnp.tanh(GELU_A * (value + GELU_B * value * value * value)))


def gelu_slope(value):
    square = value * value
    bent = jnp.tanh(GELU_A * value * (1.0 + GELU_B * square))
    inner = GELU_A * (1.0 + 3.0 * GELU_B * square)
    return 0.5 * (1.0 + bent) + 0.5 * value * (1.0 - bent * bent) * inner


def slot_of(head, block, odd):
    this, other = SLOT_OF[2 * head + block], SLOT_OF[2 * head + 1 - block]
    return jnp.where(odd == 1, other, this)


class Held:
    def __init__(self, source, target, sem):
        self.target = target
        self.copy = pltpu.make_async_copy(source, target, sem)
        self.copy.start()
        self.waited = False

    def ready(self):
        if not self.waited:
            self.copy.wait()
            self.waited = True
        return self.target

    def __getitem__(self, at):
        return self.ready()[at]


class HeldBlocks:
    def __init__(self, source, target, sems, axis):
        self.source, self.target, self.sems, self.axis = source, target, sems, axis
        self.waited = False

    def copy(self, c):
        here = pl.ds(c * FF_BLOCK if isinstance(c, int) else pl.multiple_of(c * FF_BLOCK, FF_BLOCK), FF_BLOCK)
        at = (here, slice(None)) if self.axis == 0 else (slice(None), here)
        return pltpu.make_async_copy(self.source.at[at], self.target.at[at], self.sems.at[c])

    def wait(self, c):
        if not self.waited:
            self.copy(c).wait()

    def ready(self):
        assert self.waited
        return self.target

    def __getitem__(self, at):
        return self.target[at]


class Kept:
    def __init__(self, source, target, sem):
        self.source = source
        self.copy = pltpu.make_async_copy(source, target, sem)
        self.started = False

    def __getitem__(self, at):
        return self.source[at]

    def __setitem__(self, at, value):
        self.source[at] = value

    def flush(self):
        self.copy.start()
        self.started = True

    def finish(self):
        if not self.started:
            self.flush()
        self.copy.wait()


class KeptBlocks(Kept):
    def __init__(self, source, target, sems):
        self.source, self.target, self.sems = source, target, sems
        self.started = True

    def copy_of(self, c):
        here = pl.ds(c * 512 if isinstance(c, int) else pl.multiple_of(c * 512, 512), 512)
        return pltpu.make_async_copy(self.source.at[here], self.target.at[here], self.sems.at[c])

    def finish(self):
        for c in range(FF // 512):
            self.copy_of(c).wait()


class KeptSlots(Kept):
    def __init__(self, source, target, sems):
        self.source = source
        self.copies = [pltpu.make_async_copy(source.at[e], target.at[e], sems.at[w]) for w, e in SLOT_OF.items()]
        self.started = True

    def flush_head(self, head):
        for half in range(2):
            self.copies[2 * head + half].start()

    def finish(self):
        for copy in self.copies:
            copy.wait()


def project(stream, gain, w_qkv, odd, third, slots, normed_out):
    normed = (standardise(stream)[0] * gain).astype(BF16)
    normed_out[...] = normed
    low_lanes = lax.broadcasted_iota(jnp.int32, (ROWS, 128), 1) < 64
    for pair in range(HEADS // 2):
        at = 128 * pair
        queries = dot(normed, w_qkv[:, at : at + 128]) * HEAD_DIM**-0.5
        keys = dot(normed, w_qkv[:, WIDTH + at : WIDTH + at + 128])
        values = dot(normed, w_qkv[:, 2 * WIDTH + at : 2 * WIDTH + at + 128])
        queries_t = queries.T.astype(BF16)
        first = jnp.where(low_lanes, keys, pltpu.roll(values, 64, 1)).astype(BF16)
        second = jnp.where(low_lanes, pltpu.roll(keys, 64, 1), values).astype(BF16)
        for j, both in enumerate((first, second)):
            head = 2 * pair + j
            for block in range(2):
                to = slot_of(head, block, odd)
                slots[to, 0:ROWS, :] = both
                slots[to, ROWS : ROWS + 64, :] = queries_t[
                    64 * j : 64 * j + 64, block * HALF : (block + 1) * HALF
                ]
                slots[to, ROWS + 64 : SLOT, :] = jnp.broadcast_to(third, (16, 128)).astype(BF16)
            slots.flush_head(head)


def gather_heads(recv, odd, row, target):
    for head in range(HEADS):
        for block in range(2):
            target[64 * head : 64 * head + 64, block * HALF : (block + 1) * HALF] = recv[
                slot_of(head, block, odd), row : row + 64, :
            ]


def scatter_heads(features, odd, slots):
    for head in range(HEADS):
        for block in range(2):
            slots[slot_of(head, block, odd)] = features[
                64 * head : 64 * head + 64, block * HALF : (block + 1) * HALF
            ]


def mix(recv, stream, odd, gain, weights, features, acc, att_out, mid_out, normed_out, hidden_out, act_out):
    gather_heads(recv, odd, 0, features)
    attended = features[...].T
    att_out[...] = attended
    mid = stream + dot(attended, weights[0][...])
    mid_out[...] = mid
    normed_out[...] = (standardise(mid)[0] * gain).astype(BF16)
    acc[...] = mid
    up, down = weights[1:]

    def step(c, _):
        here = pl.ds(pl.multiple_of(c * FF_BLOCK, FF_BLOCK), FF_BLOCK)
        up.wait(c)
        down.wait(c)
        hidden = dot(normed_out[...], up[:, here])
        hidden_out[:, here] = hidden
        active = gelu(hidden).astype(BF16)
        act_out[:, here] = active
        acc[...] += dot(active, down[here, :])
        return 0

    lax.fori_loop(0, FF // FF_BLOCK, step, 0)
    up.waited = down.waited = True


def mix_back(grad, odd, gain, mid, hidden, weights, acc, dz_out, dh_out, dy_out, dmid_out, gain_out, slots):
    out, up, down = weights
    dz_out[...] = grad.astype(BF16)
    acc[...] = jnp.zeros(acc.shape, F32)

    def step(c, _):
        here = pl.ds(pl.multiple_of(c * FF_BLOCK, FF_BLOCK), FF_BLOCK)
        up.wait(c)
        down.wait(c)
        grad_act = times_transposed(dz_out[...], down[here, :])
        low = (gelu_slope(hidden[:, here]) * grad_act).astype(BF16)
        dh_out[:, here] = low
        acc[...] += times_transposed(low, up[:, here])
        return 0

    lax.fori_loop(0, FF // FF_BLOCK, step, 0)
    up.waited = down.waited = True
    grad_mid, grad_gain = standardise_back(acc[...], gain, mid[...])
    gain_out[...] = grad_gain
    grad_mid = grad_mid + grad
    dmid_out[...] = grad_mid
    for done in (dh_out, dmid_out, dz_out):
        if isinstance(done, Kept):
            done.flush()
    low = grad_mid.astype(BF16)
    dy_out[...] = low
    scatter_heads(times_transposed(low, out[...]).T.astype(BF16), odd, slots)


def project_back(recv, odd, gain, stream, grad_mid, w_qkv, features, dproj_out, gain_out):
    gather_heads(recv, odd, ROWS, features)
    dproj_out[:, 0:WIDTH] = features[...].T
    low_lanes = lax.broadcasted_iota(jnp.int32, (ROWS, 128), 1) < 64
    for pair in range(HEADS // 2):
        at = 128 * pair
        both = []
        for head in (2 * pair, 2 * pair + 1):
            one, two = recv[SLOT_OF[2 * head], 0:ROWS, :], recv[SLOT_OF[2 * head + 1], 0:ROWS, :]
            both.append(one.astype(F32) + two.astype(F32))
        keys = jnp.where(low_lanes, both[0], pltpu.roll(both[1], 64, 1)).astype(BF16)
        values = jnp.where(low_lanes, pltpu.roll(both[0], 64, 1), both[1]).astype(BF16)
        dproj_out[:, WIDTH + at : WIDTH + at + 128] = keys
        dproj_out[:, 2 * WIDTH + at : 2 * WIDTH + at + 128] = values
    grad_normed = times_transposed(dproj_out[...], w_qkv[...])
    grad_stream, grad_gain = standardise_back(grad_normed, gain, stream[...].astype(F32))
    gain_out[...] = grad_gain
    return grad_stream + grad_mid[...]


def start_of(pos, passes, count, here, at):
    return at - (pos[0, at] * count[0, at] + passes[0, at])


def third_start(start):
    return jnp.where((start < 0) | (start > ROWS), ROWS, start)


def enter_kernel(pos, passes, count, gain_attn, ins, outs):
    tokens, w_qkv = ins
    slots, normed = outs
    here = lax.axis_index("seq")
    third = third_start(start_of(pos, passes, count, here, ROWS - 1))
    project(tokens[...].astype(F32), gain_attn[...].reshape(1, WIDTH), w_qkv, here % 2, third.astype(F32), slots, normed)


def as_column(row):
    return jnp.broadcast_to(row.astype(F32), (8, ROWS)).T[:, 0:1]


def turn_kernel(info, passes, table, gain_attn, gain_mlp, ins, outs, features, acc):
    recv, tokens, w_out, w_up, w_down, w_qkv = ins
    slots, normed, second, att, mid, mid_normed, hidden, act = outs
    odd = info[3]
    mix(recv, tokens[...].astype(F32), odd, gain_mlp[...].reshape(1, WIDTH), (w_out, w_up, w_down), features, acc, att, mid, mid_normed, hidden, act)
    for out in (att, mid, mid_normed, hidden, act):
        out.flush()
    stream = acc[...]
    column = as_column(passes[...])
    for row in range(PASSES):
        stream = stream + jnp.where(column == row, table[row : row + 1, :], 0.0)
    second[...] = stream
    second.flush()
    project(stream, gain_attn[...].reshape(1, WIDTH), w_qkv, odd, info[4].astype(F32), slots, normed)


def crest_kernel(info, gain_mlp, ins, outs, features, acc, mid, hidden, dz):
    recv, stream, w_out, w_up, w_down, cotangent = ins
    slots, mixed, att, mid_normed, act, dh, dy, dmid, gain_out = outs
    odd = info[3]
    gain = gain_mlp[...].reshape(1, WIDTH)
    mix(recv, stream[...], odd, gain, (w_out, w_up, w_down), features, acc, att, mid, mid_normed, hidden, act)
    mixed[...] = acc[...].astype(BF16)
    for out in (att, mid_normed, act, mixed):
        out.flush()
    mix_back(cotangent[...].astype(F32), odd, gain, mid, hidden, (w_out, w_up, w_down), acc, dz, dh, dy, dmid, gain_out, slots)


def return_kernel(info, passes, gain_attn, gain_mlp, gain_m_two, ins, outs, features, acc, dz, dh, dy, gain_m):
    (recv, w_qkv, stream, grad_mid, hidden, w_down, w_up, mid, w_out,
     mid_one, mid_two, dh_two, act_one, act_two, dz_two, att_one, att_two, dy_two) = ins
    slots, dproj, dmid, up_out, down_out, out_out = outs
    odd = info[3]
    small = jnp.zeros((16, WIDTH), F32)
    at = lax.broadcasted_iota(jnp.int32, (16, 1), 0)
    grad = project_back(recv, odd, gain_attn[...].reshape(1, WIDTH), stream, grad_mid, w_qkv, features, dproj, gain_m)
    dproj.flush()
    small = jnp.where(at == PASSES, gain_m[...], small)
    column = as_column(passes[...])
    for row in range(PASSES):
        part = jnp.sum(jnp.where(column == row, grad, 0.0), axis=0, keepdims=True)
        small = jnp.where(at == row, part, small)
    mix_back(grad, odd, gain_mlp[...].reshape(1, WIDTH), mid, hidden.ready(), (w_out, w_up, w_down), acc, dz, dh, dy, dmid, gain_m, slots)
    slots.flush()
    small = jnp.where(at == PASSES + 1, gain_m[...] + gain_m_two[...], small)
    weight_gradients(
        (mid_one, dh, mid_two, dh_two, act_one, dz, act_two, dz_two, att_one, dy, att_two, dy_two),
        small, up_out, down_out, out_out,
    )


def leave_kernel(info, gain_attn, ins, outs, features):
    recv, w_qkv, tokens, grad_mid = ins
    grad_tokens, dproj, gain_out = outs
    grad_tokens[...] = project_back(recv, info[3], gain_attn[...].reshape(1, WIDTH), tokens, grad_mid, w_qkv, features, dproj, gain_out)


def shape(*dims, dtype=BF16):
    return jax.ShapeDtypeStruct(dims, dtype)


def in_vmem(kernel, name, info, small, arrays, outs, scratch, flops, split={}):
    vmem = pl.BlockSpec(memory_space=pltpu.VMEM)
    hbm = pl.BlockSpec(memory_space=pl.ANY)
    ins, count = len(arrays), len(arrays) + len(outs)

    info = info if isinstance(info, tuple) else (info,)

    def body(*refs):
        known, refs = refs[: len(info)], refs[len(info) :]
        few, refs = refs[: len(small)], refs[len(small) :]
        far, near, sems, rest = refs[:count], refs[count : 2 * count], refs[2 * count], refs[2 * count + 1 :]
        held, blocks = [], []
        for i in range(ins):
            if i in split:
                own = sems.at[pl.ds(count + 6 * len(blocks), 6)]
                held.append(HeldBlocks(far[i], near[i], own, split[i]))
                blocks.append(held[-1])
                if len(blocks) == 2:
                    for c in range(FF // FF_BLOCK):
                        for one in blocks:
                            one.copy(c).start()
            else:
                held.append(Held(far[i], near[i], sems.at[i]))
        kept = [Kept(near[i], far[i], sems.at[i]) for i in range(ins, count)]
        if outs[0].shape == (SEQ, SLOT, 128):
            kept[0] = KeptSlots(near[ins], far[ins], sems.at[pl.ds(count + 12, 24)])
        for i, out in enumerate(outs):
            if out.shape == (FF, WIDTH):
                kept[i] = KeptBlocks(near[ins + i], far[ins + i], sems.at[pl.ds(count + 12, 6)])
        kernel(*known, *few, held, kept, *rest)
        for one in kept:
            if not one.started:
                one.flush()
        for one in held:
            one.ready()
        for one in kept:
            one.finish()

    return pl.pallas_call(
        body,
        out_shape=tuple(outs),
        in_specs=[pl.BlockSpec(memory_space=pltpu.SMEM)] * len(info) + [vmem] * len(small) + [hbm] * ins,
        out_specs=(hbm,) * len(outs),
        scratch_shapes=[pltpu.VMEM(x.shape, x.dtype) for x in (*arrays, *outs)]
        + [pltpu.SemaphoreType.DMA((count + 36,))]
        + scratch,
        compiler_params=pltpu.CompilerParams(vmem_limit_bytes=62 << 20),
        cost_estimate=pl.CostEstimate(flops=int(flops), bytes_accessed=16 << 20, transcendentals=1 << 20),
        name=name,
    )(*info, *small, *arrays)


LATE = 7168
CORE = 5


def weight_gradients(factors, small, up, down, out):
    mid_one, dh_one, mid_two, dh_two, act_one, dz_one, act_two, dz_two, att_one, dy_one, att_two, dy_two = factors
    for one in (dh_two, act_one, act_two):
        one.ready()

    def left(one, two):
        return jnp.concatenate([one, two], axis=0).T

    mid = left(mid_one[...], mid_two[...])

    def step_up(c, _):
        here = pl.ds(pl.multiple_of(c * 512, 512), 512)
        up[:, here] = dot(mid, jnp.concatenate([dh_one[:, here], dh_two[:, here]], axis=0)).astype(BF16)
        return 0

    lax.fori_loop(0, 6, step_up, 0)
    up.flush()
    dy = jnp.concatenate([dy_one[...], dy_two[...]], axis=0)
    out[0:WIDTH, :] = dot(left(att_one[...], att_two[...]), dy).astype(BF16)
    out[WIDTH:, :] = small.astype(BF16)
    out.flush()
    dz = jnp.concatenate([dz_one[...], dz_two[...]], axis=0)

    def step_down(c, _):
        here = pl.ds(pl.multiple_of(c * 512, 512), 512)
        down[here, :] = dot(left(act_one[:, here], act_two[:, here]), dz).astype(BF16)
        down.copy_of(c).start()
        return 0

    lax.fori_loop(0, 6, step_down, 0)


def grad_qkv_kernel(info, ins, outs):
    normed, dproj = ins
    left = normed[...].T
    dproj.ready()

    def step(c, _):
        result = dot(left, dproj[:, pl.ds(pl.multiple_of(c * 384, 384), 384)])
        for i in range(3):
            outs[0][3 * c + i] = result[:, 128 * i : 128 * i + 128]
        return 0

    lax.fori_loop(0, 6, step, 0)


def grad_qkv_both_kernel(info, gains, ins, outs):
    normed, dproj, before = ins
    left = normed[...].T
    dproj.ready(), before.ready()
    core = info[CORE]

    def step(c, _):
        result = dot(left, dproj[:, pl.ds(pl.multiple_of(c * 384, 384), 384)])
        for to, out in enumerate(outs):
            for half in range(2):

                @pl.when((half ^ core) == to)
                def _():
                    for i in range(3):
                        for part in range(3):
                            rows = slice(384 * half + 128 * part, 384 * half + 128 * part + 128)
                            value = result[rows, 128 * i : 128 * i + 128] + before[3 * c + i, rows, :]
                            at = pl.multiple_of(part * 2304 + (3 * c + i) * 128, 128)
                            out[pl.ds(at, 128), :] = value.astype(BF16)

        return 0

    lax.fori_loop(0, 6, step, 0)
    for out in outs:
        out[6912:6928, :] = gains[...].astype(BF16)


def widen_kernel(core, mine, other, out):
    half = pl.program_id(0) // 3

    def put(ref):
        for i in range(18):
            out[:, 128 * i : 128 * i + 128] = ref[128 * i : 128 * i + 128, :].astype(F32)

    @pl.when(half == core[0])
    def _():
        put(mine)

    @pl.when(half != core[0])
    def _():
        put(other)


def widen(core, mine, other):
    def place(own):
        def index(i, core):
            low = core[0] == (0 if own else 1)
            return (jnp.where(low, jnp.minimum(i, 2), jnp.maximum(i - 3, 0)), 0)

        return pl.BlockSpec((2304, 128), index)

    return pl.pallas_call(
        widen_kernel,
        out_shape=shape(WIDTH, 3 * WIDTH, dtype=F32),
        grid_spec=pltpu.PrefetchScalarGridSpec(
            num_scalar_prefetch=1,
            grid=(6,),
            in_specs=[place(True), place(False)],
            out_specs=pl.BlockSpec((128, 3 * WIDTH), lambda i, core: (i, 0)),
        ),
        compiler_params=pltpu.CompilerParams(vmem_limit_bytes=20 << 20),
        name="widen",
    )(core, mine, other)


def swap(value, bit):
    return lax.ppermute(value, "batch", [(i, i ^ bit) for i in range(4)])


def exchange(slots):
    return lax.all_to_all(slots, "seq", 0, 0)


def sum_cores(partial):
    mine, other = partial
    return (mine.astype(F32) + swap(other, 1).astype(F32)).astype(BF16)


CHIPS = 64


def across_chips(slots):
    groups = [[s * 4 + z * 2 + c for s in range(SEQ) for z in range(2)] for c in range(2)]
    return lax.all_to_all(slots, ("seq", "batch"), 0, 0, axis_index_groups=groups)


def positions(half, first_row, count):
    at = lax.broadcasted_iota(jnp.int32, (1, count), 1)
    block = at // HALF
    return first_row + block * ROWS + ((half + block) % 2) * HALF + at % HALF


def third_keys(recv, count):
    last = recv[SEQ - 1, ROWS + 64 : SLOT, :].astype(F32)[0:1].astype(jnp.int32)
    row = last + (SEQ - 1) * ROWS
    return jnp.concatenate([row] * (count // 128), axis=1)


def first_keys(at, second, third):
    return jnp.where(at < second, 0, jnp.where(at < third, second, third))


def attend_kernel(info, recv_far, out_low_far, out_f_far, lse_far, k_t_far, q_t_far, recv, out_low, out_f, lse, kv_t, q_t, sems, acc, *, devs):
    tile_rows = devs * HALF
    span = devs * ROWS
    active, half, second = info[0], info[1], info[2]

    @pl.when(active == 1)
    def _():
        parts = [
            Held(recv_far.at[8 * i : 8 * i + 8], recv.at[8 * i : 8 * i + 8], sems.at[i]) for i in range(4)
        ]
        fars = (k_t_far, q_t_far, out_low_far, out_f_far, lse_far)
        kept = [
            Kept(near, far, sems.at[4 + i])
            for i, (near, far) in enumerate(zip((kv_t.at[0:64], q_t, out_low, out_f, lse), fars))
        ]
        ones = (lax.broadcasted_iota(jnp.int32, (16, ROWS), 0) == 0).astype(BF16)
        for d in range(SEQ):
            parts[d // 8].ready()
            keys = slice(d * ROWS, (d + 1) * ROWS)
            kv_t[0:128, keys] = recv[d, 0:ROWS, :].T
            kv_t[128:144, keys] = ones
            q_t[0:64, d * HALF : (d + 1) * HALF] = recv[d, ROWS : ROWS + 64, :]
        q_t[64:128, :] = jnp.zeros((64, SEQ * HALF), BF16)
        kept[0].flush()
        kept[1].flush()

        third = third_keys(recv, tile_rows)

        def square_top(features):
            wide = features.astype(F32)
            return jnp.max(jnp.sum(wide * wide, axis=0, keepdims=True))

        key_top = jnp.float32(0.0)
        query_top = jnp.float32(0.0)
        for c in range(8):
            key_top = jnp.maximum(key_top, square_top(kv_t[0:64, 1024 * c : 1024 * c + 1024]))
        for c in range(4):
            query_top = jnp.maximum(query_top, square_top(q_t[0:64, 1024 * c : 1024 * c + 1024]))
        small = key_top * query_top < (SMALL / LOG2E) ** 2

        def one_tile(t, _):
            start = t * span
            columns = pl.ds(pl.multiple_of(t * tile_rows, tile_rows), tile_rows)
            at = positions(half, start, tile_rows)
            first = first_keys(at, second, third)
            acc[...] = jnp.zeros((80, tile_rows), F32)
            queries = q_t[:, columns]

            def update(kv, key_rows, left, mask):
                here = slice(left, tile_rows)
                weights = jnp.exp2(dot(kv, queries[:, here]) * LOG2E)
                if mask is not None:
                    weights = jnp.where(mask, weights, 0.0)
                acc[:, here] = acc[:, here] + dot(kv_t[64:144, key_rows], weights.astype(BF16))

            def step(j, _):
                def scores(c, k):
                    kv = recv[pl.ds(j * 8 + k * 2, 2), 0:ROWS, :].reshape(512, 128)
                    return dot(kv, queries[:, c : c + 1024])

                pieces = [(c, k) for c in range(0, tile_rows, 1024) for k in range(4)]
                ahead = scores(*pieces[0])
                for n, (c, k) in enumerate(pieces):
                    now, ahead = ahead, scores(*pieces[n + 1]) if n + 1 < len(pieces) else None
                    keys = pl.ds(pl.multiple_of(j * 2048 + k * 512, 512), 512)
                    part = dot(kv_t[64:144, keys], jnp.exp2(now * LOG2E).astype(BF16))
                    total = part if k == 0 else total + part
                    if k == 3:
                        acc[:, c : c + 1024] += total
                return 0

            lax.fori_loop(0, t, step, 0)
            acc[...] = jnp.where(first >= start, 0.0, acc[...])
            for i in range(devs // 2):
                left = 256 * i
                key_start = pl.multiple_of(start + 512 * i, 512)
                kv = recv[pl.ds(t * devs + 2 * i, 2), 0:ROWS, :].reshape(512, 128)
                key_at = key_start + lax.broadcasted_iota(jnp.int32, (512, 1), 0)
                allowed = (key_at >= first[:, left:]) & (key_at <= at[:, left:])
                update(kv, pl.ds(key_start, 512), left, allowed)
            total = acc[64:65, :]
            result = acc[0:64, :] / total
            out_f[:, columns] = result
            lse[:, columns] = jnp.log2(total)
            low = result.astype(BF16)
            for i in range(devs):
                out_low[t * devs + i] = low[:, i * HALF : (i + 1) * HALF]

            @pl.when(t == 0)
            def _():
                key_at = lax.broadcasted_iota(jnp.int32, (1, ROWS), 1)
                kv_t[64:144, 0:ROWS] = jnp.where(key_at >= second, kv_t[64:144, 0:ROWS], 0.0).astype(BF16)

            return 0

        def one_device(d, _):
            columns = pl.ds(pl.multiple_of(d * HALF, HALF), HALF)
            at = d * ROWS + (half + d) % 2 * HALF + lax.broadcasted_iota(jnp.int32, (1, HALF), 1)
            first = first_keys(at, second, third_keys(recv, HALF))
            queries = q_t[:, columns]

            def step(j, state):
                old_top, old_acc = state
                kv = recv[pl.ds(j * 2, 2), 0:ROWS, :].reshape(512, 128)
                key_at = j * 512 + lax.broadcasted_iota(jnp.int32, (512, 1), 0)
                allowed = (key_at >= first) & (key_at <= at)
                scores = jnp.where(allowed, dot(kv, queries) * LOG2E, LOW)
                new_top = jnp.maximum(old_top, jnp.max(scores, axis=0, keepdims=True))
                weights = jnp.exp2(scores - new_top).astype(BF16)
                keys = pl.ds(pl.multiple_of(j * 512, 512), 512)
                return new_top, old_acc * jnp.exp2(old_top - new_top) + dot(kv_t[64:144, keys], weights)

            state = (jnp.full((1, HALF), LOW, F32), jnp.zeros((80, HALF), F32))
            top, state = lax.fori_loop(0, d // 2 + 1, step, state)
            total = state[64:65, :]
            result = state[0:64, :] / total
            out_f[:, columns] = result
            lse[:, columns] = top + jnp.log2(total)
            out_low[d] = result.astype(BF16)
            return 0

        @pl.when(small)
        def _():
            lax.fori_loop(0, SEQ // devs, one_tile, 0)

        @pl.when(jnp.logical_not(small))
        def _():
            lax.fori_loop(0, SEQ, one_device, 0)

        for one in kept[2:]:
            one.flush()
        for one in kept:
            one.finish()


def attend(info, recv):
    devs = 8
    pairs = 17.8e6
    out_low, *rest = pl.pallas_call(
        functools.partial(attend_kernel, devs=devs),
        out_shape=(
            jax.ShapeDtypeStruct((SEQ, 64, HALF), BF16),
            jax.ShapeDtypeStruct((64, SEQ * HALF), F32),
            jax.ShapeDtypeStruct((1, SEQ * HALF), F32),
            jax.ShapeDtypeStruct((64, SEQ * ROWS), BF16),
            jax.ShapeDtypeStruct((128, SEQ * HALF), BF16),
        ),
        in_specs=[
            pl.BlockSpec(memory_space=pltpu.SMEM),
            pl.BlockSpec(memory_space=pl.ANY),
        ],
        out_specs=tuple(pl.BlockSpec(memory_space=pl.ANY) for _ in range(5)),
        scratch_shapes=[
            pltpu.VMEM((SEQ, SLOT, 128), BF16),
            pltpu.VMEM((SEQ, 64, HALF), BF16),
            pltpu.VMEM((64, SEQ * HALF), F32),
            pltpu.VMEM((1, SEQ * HALF), F32),
            pltpu.VMEM((144, SEQ * ROWS), BF16),
            pltpu.VMEM((128, SEQ * HALF), BF16),
            pltpu.SemaphoreType.DMA((9,)),
            pltpu.VMEM((80, devs * HALF), F32),
        ],
        compiler_params=pltpu.CompilerParams(vmem_limit_bytes=62 << 20),
        cost_estimate=pl.CostEstimate(
            flops=int(pairs * 1024), bytes_accessed=8 << 20, transcendentals=int(pairs)
        ),
        name="attend",
    )(info, recv)
    out_f, lse, kv_t, q_t = rest
    return out_low, recv, kv_t, q_t, out_f, lse


def attend_back_kernel(info, recv_far, kv_t_far, q_t_far, out_f_far, lse_far, grad_out_far, send_far, recv, kv_t, q_t, out_f, lse, grad_out, send, sems, grad_kv, do_t, grad_q, *, devs):
    tile_rows = devs * HALF
    span = devs * ROWS
    active, half, second = info[0], info[1], info[2]

    @pl.when(active == 1)
    def _():
        fars = (grad_out_far, recv_far, q_t_far, out_f_far, lse_far, kv_t_far)
        nears = (grad_out, recv, q_t, out_f, lse, kv_t)
        held = [Held(far, near, sems.at[i]) for i, (far, near) in enumerate(zip(fars, nears))]
        grad_kv[...] = jnp.zeros(grad_kv.shape, F32)
        held[0].ready()
        for d in range(SEQ):
            do_t[64:128, d * HALF : (d + 1) * HALF] = grad_out[d]
        do_t[0:64, :] = jnp.zeros((64, SEQ * HALF), BF16)
        for one in held:
            one.ready()

        third = third_keys(recv, tile_rows)

        def one_tile(t, _):
            start = t * span
            columns = pl.ds(pl.multiple_of(t * tile_rows, tile_rows), tile_rows)
            at = positions(half, start, tile_rows)
            first = first_keys(at, second, third)
            queries = q_t[:, columns]
            grads = do_t[:, columns]
            query_rows = queries.T
            grad_rows = grads.T
            delta = jnp.sum(
                grads[64:128, :].astype(F32) * out_f[:, columns], axis=0, keepdims=True
            )
            own_lse = lse[:, columns]
            far_lse = jnp.where(first >= start, -LOW, own_lse)
            grad_q[...] = jnp.zeros((64, tile_rows), F32)

            def update(kv, key_rows, left, row_lse, mask):
                here = slice(left, tile_rows)
                scores = dot(kv, queries[:, here]) * LOG2E
                probs = jnp.where(mask, jnp.exp2(scores - row_lse[:, here]), 0.0)
                grad_probs = dot(kv, grads[:, here])
                grad_scores = (probs * (grad_probs - delta[:, here])).astype(BF16)
                grad_kv[key_rows, :] += dot(grad_scores, query_rows[here, :]) + dot(
                    probs.astype(BF16), grad_rows[here, :]
                )
                grad_q[:, here] += dot(kv_t[0:64, key_rows], grad_scores)

            def step(j, _):
                kv = recv[pl.ds(j * 4, 4), 0:ROWS, :].reshape(1024, 128)
                key_at = j * 1024 + lax.broadcasted_iota(jnp.int32, (1024, 1), 0)
                update(kv, pl.ds(pl.multiple_of(j * 1024, 1024), 1024), 0, far_lse, key_at >= second)
                return 0

            lax.fori_loop(0, t * (span // 1024), step, 0)
            for i in range(devs // 2):
                left = 256 * i
                key_start = pl.multiple_of(start + 512 * i, 512)
                kv = recv[pl.ds(t * devs + 2 * i, 2), 0:ROWS, :].reshape(512, 128)
                key_at = key_start + lax.broadcasted_iota(jnp.int32, (512, 1), 0)
                allowed = (key_at >= first[:, left:]) & (key_at <= at[:, left:])
                update(kv, pl.ds(key_start, 512), left, own_lse, allowed)
            low = (grad_q[...] * HEAD_DIM**-0.5).astype(BF16)
            for i in range(devs):
                d = t * devs + i
                send[d, ROWS:, :] = low[:, i * HALF : (i + 1) * HALF]
                send[d, 0:ROWS, :] = grad_kv[pl.ds(pl.multiple_of(d * ROWS, ROWS), ROWS), :].astype(BF16)
            sending(t).start()
            return 0

        def sending(t):
            here = pl.ds(t * devs, devs)
            return pltpu.make_async_copy(send.at[here], send_far.at[here], sems.at[6 + t])

        def from_last(i, _):
            return one_tile(SEQ // devs - 1 - i, 0)

        lax.fori_loop(0, SEQ // devs, from_last, 0)
        for t in range(SEQ // devs):
            sending(t).wait()


def attend_back(info, recv, kv_t, q_t, out_f, lse, grad_out):
    devs = 8
    pairs = 17.8e6
    return pl.pallas_call(
        functools.partial(attend_back_kernel, devs=devs),
        out_shape=jax.ShapeDtypeStruct((SEQ, ROWS + 64, HALF), BF16),
        in_specs=[pl.BlockSpec(memory_space=pltpu.SMEM)]
        + [pl.BlockSpec(memory_space=pl.ANY)] * 6,
        out_specs=pl.BlockSpec(memory_space=pl.ANY),
        scratch_shapes=[
            pltpu.VMEM((SEQ, SLOT, 128), BF16),
            pltpu.VMEM((64, SEQ * ROWS), BF16),
            pltpu.VMEM((128, SEQ * HALF), BF16),
            pltpu.VMEM((64, SEQ * HALF), F32),
            pltpu.VMEM((1, SEQ * HALF), F32),
            pltpu.VMEM((SEQ, 64, HALF), BF16),
            pltpu.VMEM((SEQ, ROWS + 64, HALF), BF16),
            pltpu.SemaphoreType.DMA((14,)),
            pltpu.VMEM((SEQ * ROWS, 128), F32),
            pltpu.VMEM((128, SEQ * HALF), BF16),
            pltpu.VMEM((64, devs * HALF), F32),
        ],
        compiler_params=pltpu.CompilerParams(vmem_limit_bytes=62 << 20),
        cost_estimate=pl.CostEstimate(
            flops=int(pairs * 1024), bytes_accessed=8 << 20, transcendentals=int(pairs)
        ),
        name="attend_back",
    )(info, recv, kv_t, q_t, out_f, lse, grad_out)


def on_device(
    tokens,
    token_pos,
    token_pass,
    token_count,
    w_qkv,
    w_out,
    w_up,
    w_down,
    gain_attn,
    gain_mlp,
    pass_table,
    cotangent,
):
    here = lax.axis_index("seq")
    documents = (token_pos, token_pass, token_count)
    edge = jnp.where(here == 0, ROWS - 1, 0)
    second = here * ROWS + start_of(*documents, here, edge)
    third = third_start(start_of(*documents, here, ROWS - 1))
    group, place = here // 4, here % 4
    active = (place < 3).astype(jnp.int32)
    core = lax.axis_index("batch") % 2
    info = jnp.stack([active, (3 * group + place) % 2, second, here % 2, third, core])
    passes = token_pass
    table = jnp.pad(pass_table, ((0, 8 - PASSES), (0, 0)))
    gain_a, gain_m = gain_attn, gain_mlp
    stream_one = tokens[0]
    features = pltpu.VMEM((WIDTH, ROWS), BF16)
    acc = pltpu.VMEM((ROWS, WIDTH), F32)
    square = shape(ROWS, WIDTH)
    wide = shape(ROWS, WIDTH, dtype=F32)
    row = shape(1, WIDTH, dtype=F32)
    sent = shape(SEQ, SLOT, 128)
    sent_back = shape(SEQ, 64, 128)

    slots, normed_one = in_vmem(
        enter_kernel, "enter", documents, (gain_a,), (stream_one, w_qkv), (sent, square), [], 1e9
    )
    recv = exchange(slots)
    recv, passes, table, gain_m = lax.optimization_barrier((recv, passes, table, gain_m))
    saved_one = attend(info, recv)
    slots, normed_two, stream_two, att_one, mid_one, midn_one, hidden_one, act_one = in_vmem(
        turn_kernel,
        "turn",
        info,
        (passes, table, gain_a, gain_m),
        (exchange(saved_one[0]), stream_one, w_out, w_up, w_down, w_qkv),
        (sent, square, wide, square, wide, square, shape(ROWS, FF, dtype=F32), shape(ROWS, FF)),
        [features, acc],
        3.6e9,
        {3: 1, 4: 0},
    )
    saved_two = attend(info, exchange(slots))
    slots, mixed, att_two, midn_two, act_two, dh_two, dy_two, dmid_two, gain_m_two = in_vmem(
        crest_kernel,
        "crest",
        info,
        (gain_m,),
        (exchange(saved_two[0]), stream_two, w_out, w_up, w_down, cotangent[0]),
        (sent_back, square, square, square, shape(ROWS, FF), shape(ROWS, FF), square, wide, row),
        [features, acc, acc, pltpu.VMEM((ROWS, FF), F32), pltpu.VMEM((ROWS, WIDTH), BF16)],
        5e9,
        {3: 1, 4: 0},
    )
    back = exchange(slots)
    recv = exchange(attend_back(info, *saved_two[1:], back))
    slots, dproj_two, dmid_one, *early = in_vmem(
        return_kernel,
        "return",
        info,
        (passes, gain_a, gain_m, gain_m_two),
        (recv, w_qkv, stream_two, dmid_two, hidden_one, w_down, w_up, mid_one, w_out,
         midn_one, midn_two, dh_two, act_one, act_two, cotangent[0], att_one, att_two, dy_two),
        (sent_back, shape(ROWS, 3 * WIDTH), wide, shape(WIDTH, FF), shape(FF, WIDTH), shape(WIDTH + 16, WIDTH)),
        [features, acc, pltpu.VMEM((ROWS, WIDTH), BF16), pltpu.VMEM((ROWS, FF), BF16),
         pltpu.VMEM((ROWS, WIDTH), BF16), pltpu.VMEM((1, WIDTH), F32)],
        1e10,
        {5: 0, 6: 1},
    )
    back = exchange(slots)
    early = lax.psum(tuple(early), ("seq", "batch"))
    sent_one = attend_back(info, *saved_one[1:], back)
    recv = exchange(sent_one)
    grad_tokens, dproj_one, gain_a_one = in_vmem(
        leave_kernel,
        "leave",
        info,
        (gain_a,),
        (recv, w_qkv, stream_one, dmid_one),
        (wide, shape(ROWS, 3 * WIDTH), row),
        [features],
        1e9,
    )
    (grad_two,) = in_vmem(
        grad_qkv_kernel,
        "grad_qkv_two",
        info,
        (),
        (normed_two, dproj_two),
        (shape(18, WIDTH, 128, dtype=F32),),
        [],
        9e8,
    )
    late = in_vmem(
        grad_qkv_both_kernel,
        "grad_qkv",
        info,
        (jnp.pad(gain_a_one.reshape(6, 128), ((0, 10), (0, 0))),),
        (normed_one, dproj_one, grad_two),
        (shape(LATE, 128),) * 2,
        [],
        9e8,
    )
    late, early = lax.optimization_barrier((late, early))
    late = across_chips(sum_cores(late).reshape(CHIPS, -1, 128))
    tail = early[2][WIDTH:].astype(F32)
    early = (early[0].astype(F32), early[1].astype(F32), early[2][:WIDTH].astype(F32))
    late, early = lax.optimization_barrier((late, early))
    late = jnp.sum(late.astype(F32), axis=0).astype(BF16)
    whole = across_chips(jnp.broadcast_to(late[None], (CHIPS, *late.shape))).reshape(-1, 128)
    late = (whole, swap(whole, 1))
    grad_up, grad_down, grad_out = early
    gain_a_sum = late[0][6912:6918].reshape(WIDTH).astype(F32)
    return (
        mixed[None],
        grad_tokens[None],
        widen(info[CORE : CORE + 1], *late),
        grad_out,
        grad_up,
        grad_down,
        tail[PASSES] + gain_a_sum,
        tail[PASSES + 1],
        tail[:PASSES],
    )


def solution(mesh):
    return jax.shard_map(
        on_device,
        mesh=mesh,
        in_specs=(
            P("batch", "seq", None),
            P("batch", "seq"),
            P("batch", "seq"),
            P("batch", "seq"),
            P(),
            P(),
            P(),
            P(),
            P(),
            P(),
            P(),
            P("batch", "seq", None),
        ),
        out_specs=(
            P("batch", "seq", None),
            P("batch", "seq", None),
            P(),
            P(),
            P(),
            P(),
            P(),
            P(),
            P(),
        ),
        check_vma=False,
    )
```

```python
import functools

import jax
import jax.numpy as jnp
from jax import lax
from jax.experimental import pallas as pl
from jax.experimental.pallas import tpu as pltpu
from jax.sharding import PartitionSpec as P

HEADS = 12
HEAD_DIM = 64
PASSES = 5
SEQ = 32
ROWS = 256
HALF = 128
SLOT = ROWS + 64 + 16
WIDTH = 768
FF = 3072
FF_BLOCK = 1024
EPS = 1e-5
LOG2E = 1.4426950408889634
LOW = -1e30
SMALL = 60.0
F32 = jnp.float32
BF16 = jnp.bfloat16

WORK = [3 * (e // 4) + e % 4 if e % 4 < 3 else None for e in range(SEQ)]
SLOT_OF = {w: e for e, w in enumerate(WORK) if w is not None}


def dot(left, right):
    return jnp.dot(left, right, preferred_element_type=F32)


def contract_rows(left, right):
    return lax.dot_general(left, right, (((0,), (0,)), ((), ())), preferred_element_type=F32)


def times_transposed(left, right):
    return lax.dot_general(left, right, (((1,), (1,)), ((), ())), preferred_element_type=F32)


def standardise(values):
    centered = values - jnp.mean(values, axis=-1, keepdims=True)
    inverse = lax.rsqrt(jnp.mean(centered * centered, axis=-1, keepdims=True) + EPS)
    return centered * inverse, inverse


def standardise_back(grad, gain, values):
    normal, inverse = standardise(values)
    scaled = grad * gain
    along = jnp.mean(scaled * normal, axis=-1, keepdims=True)
    grad_values = inverse * (scaled - jnp.mean(scaled, axis=-1, keepdims=True) - normal * along)
    return grad_values, jnp.sum(grad * normal, axis=0, keepdims=True)


GELU_A = 0.7978845608028654
GELU_B = 0.044715


def gelu(value):
    return 0.5 * value * (1.0 + jnp.tanh(GELU_A * (value + GELU_B * value * value * value)))


def gelu_slope(value):
    square = value * value
    bent = jnp.tanh(GELU_A * value * (1.0 + GELU_B * square))
    inner = GELU_A * (1.0 + 3.0 * GELU_B * square)
    return 0.5 * (1.0 + bent) + 0.5 * value * (1.0 - bent * bent) * inner


def slot_of(head, block, odd):
    this, other = SLOT_OF[2 * head + block], SLOT_OF[2 * head + 1 - block]
    return jnp.where(odd == 1, other, this)


class Held:
    def __init__(self, source, target, sem):
        self.target = target
        self.copy = pltpu.make_async_copy(source, target, sem)
        self.copy.start()
        self.waited = False

    def ready(self):
        if not self.waited:
            self.copy.wait()
            self.waited = True
        return self.target

    def __getitem__(self, at):
        return self.ready()[at]


class HeldBlocks:
    def __init__(self, source, target, sems, axis):
        self.source, self.target, self.sems, self.axis = source, target, sems, axis
        self.waited = False

    def copy(self, c):
        here = pl.ds(c * FF_BLOCK if isinstance(c, int) else pl.multiple_of(c * FF_BLOCK, FF_BLOCK), FF_BLOCK)
        at = (here, slice(None)) if self.axis == 0 else (slice(None), here)
        return pltpu.make_async_copy(self.source.at[at], self.target.at[at], self.sems.at[c])

    def wait(self, c):
        if not self.waited:
            self.copy(c).wait()

    def ready(self):
        assert self.waited
        return self.target

    def __getitem__(self, at):
        return self.target[at]


class Kept:
    def __init__(self, source, target, sem):
        self.source = source
        self.copy = pltpu.make_async_copy(source, target, sem)
        self.started = False

    def __getitem__(self, at):
        return self.source[at]

    def __setitem__(self, at, value):
        self.source[at] = value

    def flush(self):
        self.copy.start()
        self.started = True

    def finish(self):
        if not self.started:
            self.flush()
        self.copy.wait()


class KeptBlocks(Kept):
    def __init__(self, source, target, sems):
        self.source, self.target, self.sems = source, target, sems
        self.started = True

    def copy_of(self, c):
        here = pl.ds(c * 512 if isinstance(c, int) else pl.multiple_of(c * 512, 512), 512)
        return pltpu.make_async_copy(self.source.at[here], self.target.at[here], self.sems.at[c])

    def finish(self):
        for c in range(FF // 512):
            self.copy_of(c).wait()


class KeptSlots(Kept):
    def __init__(self, source, target, sems):
        self.source = source
        self.copies = [pltpu.make_async_copy(source.at[e], target.at[e], sems.at[w]) for w, e in SLOT_OF.items()]
        self.started = True

    def flush_head(self, head):
        for half in range(2):
            self.copies[2 * head + half].start()

    def finish(self):
        for copy in self.copies:
            copy.wait()


def project(stream, gain, w_qkv, odd, third, slots, normed_out):
    normed = (standardise(stream)[0] * gain).astype(BF16)
    normed_out[...] = normed
    normed_out.flush()
    low_lanes = lax.broadcasted_iota(jnp.int32, (ROWS, 128), 1) < 64
    for pair in range(HEADS // 2):
        at = 128 * pair
        queries = dot(normed, w_qkv[:, at : at + 128]) * HEAD_DIM**-0.5
        keys = dot(normed, w_qkv[:, WIDTH + at : WIDTH + at + 128])
        values = dot(normed, w_qkv[:, 2 * WIDTH + at : 2 * WIDTH + at + 128])
        queries_t = queries.T.astype(BF16)
        first = jnp.where(low_lanes, keys, pltpu.roll(values, 64, 1)).astype(BF16)
        second = jnp.where(low_lanes, pltpu.roll(keys, 64, 1), values).astype(BF16)
        for j, both in enumerate((first, second)):
            head = 2 * pair + j
            for block in range(2):
                to = slot_of(head, block, odd)
                slots[to, 0:ROWS, :] = both
                slots[to, ROWS : ROWS + 64, :] = queries_t[
                    64 * j : 64 * j + 64, block * HALF : (block + 1) * HALF
                ]
                slots[to, ROWS + 64 : SLOT, :] = jnp.broadcast_to(third, (16, 128)).astype(BF16)
            slots.flush_head(head)


def gather_heads(recv, odd, row, target):
    for head in range(HEADS):
        for block in range(2):
            target[64 * head : 64 * head + 64, block * HALF : (block + 1) * HALF] = recv[
                slot_of(head, block, odd), row : row + 64, :
            ]


def scatter_heads(features, odd, slots):
    for head in range(HEADS):
        for block in range(2):
            slots[slot_of(head, block, odd)] = features[
                64 * head : 64 * head + 64, block * HALF : (block + 1) * HALF
            ]


def mix(recv, stream, odd, gain, weights, features, acc, att_out, mid_out, normed_out, hidden_out, act_out):
    gather_heads(recv, odd, 0, features)
    attended = features[...].T
    att_out[...] = attended
    mid = stream + dot(attended, weights[0][...])
    mid_out[...] = mid
    normed_out[...] = (standardise(mid)[0] * gain).astype(BF16)
    acc[...] = mid
    up, down = weights[1:]

    def step(c, _):
        here = pl.ds(pl.multiple_of(c * FF_BLOCK, FF_BLOCK), FF_BLOCK)
        up.wait(c)
        down.wait(c)
        hidden = dot(normed_out[...], up[:, here])
        hidden_out[:, here] = hidden
        active = gelu(hidden).astype(BF16)
        act_out[:, here] = active
        acc[...] += dot(active, down[here, :])
        return 0

    lax.fori_loop(0, FF // FF_BLOCK, step, 0)
    up.waited = down.waited = True


def mix_back(grad, odd, gain, mid, hidden, weights, acc, dz_out, dh_out, dy_out, dmid_out, gain_out, slots):
    out, up, down = weights
    dz_out[...] = grad.astype(BF16)
    acc[...] = jnp.zeros(acc.shape, F32)

    def step(c, _):
        here = pl.ds(pl.multiple_of(c * FF_BLOCK, FF_BLOCK), FF_BLOCK)
        up.wait(c)
        down.wait(c)
        grad_act = times_transposed(dz_out[...], down[here, :])
        low = (gelu_slope(hidden[:, here]) * grad_act).astype(BF16)
        dh_out[:, here] = low
        acc[...] += times_transposed(low, up[:, here])
        return 0

    lax.fori_loop(0, FF // FF_BLOCK, step, 0)
    up.waited = down.waited = True
    grad_mid, grad_gain = standardise_back(acc[...], gain, mid[...])
    gain_out[...] = grad_gain
    grad_mid = grad_mid + grad
    dmid_out[...] = grad_mid
    for done in (dh_out, dmid_out, dz_out):
        if isinstance(done, Kept):
            done.flush()
    low = grad_mid.astype(BF16)
    dy_out[...] = low
    if isinstance(dy_out, Kept):
        dy_out.flush()
    scatter_heads(times_transposed(low, out[...]).T.astype(BF16), odd, slots)


def project_back(recv, odd, gain, stream, grad_mid, w_qkv, features, dproj_out, gain_out):
    gather_heads(recv, odd, ROWS, features)
    dproj_out[:, 0:WIDTH] = features[...].T
    low_lanes = lax.broadcasted_iota(jnp.int32, (ROWS, 128), 1) < 64
    for pair in range(HEADS // 2):
        at = 128 * pair
        both = []
        for head in (2 * pair, 2 * pair + 1):
            one, two = recv[SLOT_OF[2 * head], 0:ROWS, :], recv[SLOT_OF[2 * head + 1], 0:ROWS, :]
            both.append(one.astype(F32) + two.astype(F32))
        keys = jnp.where(low_lanes, both[0], pltpu.roll(both[1], 64, 1)).astype(BF16)
        values = jnp.where(low_lanes, pltpu.roll(both[0], 64, 1), both[1]).astype(BF16)
        dproj_out[:, WIDTH + at : WIDTH + at + 128] = keys
        dproj_out[:, 2 * WIDTH + at : 2 * WIDTH + at + 128] = values
    grad_normed = times_transposed(dproj_out[...], w_qkv[...])
    grad_stream, grad_gain = standardise_back(grad_normed, gain, stream[...].astype(F32))
    gain_out[...] = grad_gain
    return grad_stream + grad_mid[...]


def start_of(pos, passes, count, here, at):
    return at - (pos[0, at] * count[0, at] + passes[0, at])


def third_start(start):
    return jnp.where((start < 0) | (start > ROWS), ROWS, start)


def enter_kernel(pos, passes, count, gain_attn, ins, outs):
    tokens, w_qkv = ins
    slots, normed = outs
    here = lax.axis_index("seq")
    third = third_start(start_of(pos, passes, count, here, ROWS - 1))
    project(tokens[...].astype(F32), gain_attn[...].reshape(1, WIDTH), w_qkv, here % 2, third.astype(F32), slots, normed)


def as_column(row):
    return jnp.broadcast_to(row.astype(F32), (8, ROWS)).T[:, 0:1]


def turn_kernel(info, passes, table, gain_attn, gain_mlp, ins, outs, features, acc):
    recv, tokens, w_out, w_up, w_down, w_qkv = ins
    slots, normed, second, att, mid, mid_normed, hidden, act = outs
    odd = info[3]
    mix(recv, tokens[...].astype(F32), odd, gain_mlp[...].reshape(1, WIDTH), (w_out, w_up, w_down), features, acc, att, mid, mid_normed, hidden, act)
    for out in (att, mid, mid_normed, hidden, act):
        out.flush()
    stream = acc[...]
    column = as_column(passes[...])
    for row in range(PASSES):
        stream = stream + jnp.where(column == row, table[row : row + 1, :], 0.0)
    second[...] = stream
    second.flush()
    project(stream, gain_attn[...].reshape(1, WIDTH), w_qkv, odd, info[4].astype(F32), slots, normed)


def crest_kernel(info, gain_mlp, ins, outs, features, acc, mid, hidden, dz):
    recv, stream, w_out, w_up, w_down, cotangent = ins
    slots, mixed, att, mid_normed, act, dh, dy, dmid, gain_out = outs
    odd = info[3]
    gain = gain_mlp[...].reshape(1, WIDTH)
    mix(recv, stream[...], odd, gain, (w_out, w_up, w_down), features, acc, att, mid, mid_normed, hidden, act)
    mixed[...] = acc[...].astype(BF16)
    for out in (att, mid_normed, act, mixed):
        out.flush()
    mix_back(cotangent[...].astype(F32), odd, gain, mid, hidden, (w_out, w_up, w_down), acc, dz, dh, dy, dmid, gain_out, slots)


def return_kernel(info, passes, gain_attn, gain_mlp, gain_m_two, ins, outs, features, acc, dz, dh, dy, gain_m):
    (recv, w_qkv, stream, grad_mid, hidden, w_down, w_up, mid, w_out,
     mid_one, mid_two, dh_two, act_one, act_two, dz_two, att_one, att_two, dy_two) = ins
    slots, dproj, dmid, up_out, down_out, out_out = outs
    odd = info[3]
    small = jnp.zeros((16, WIDTH), F32)
    at = lax.broadcasted_iota(jnp.int32, (16, 1), 0)
    grad = project_back(recv, odd, gain_attn[...].reshape(1, WIDTH), stream, grad_mid, w_qkv, features, dproj, gain_m)
    dproj.flush()
    small = jnp.where(at == PASSES, gain_m[...], small)
    column = as_column(passes[...])
    for row in range(PASSES):
        part = jnp.sum(jnp.where(column == row, grad, 0.0), axis=0, keepdims=True)
        small = jnp.where(at == row, part, small)
    mix_back(grad, odd, gain_mlp[...].reshape(1, WIDTH), mid, hidden.ready(), (w_out, w_up, w_down), acc, dz, dh, dy, dmid, gain_m, slots)
    slots.flush()
    small = jnp.where(at == PASSES + 1, gain_m[...] + gain_m_two[...], small)
    weight_gradients(
        (mid_one, dh, mid_two, dh_two, act_one, dz, act_two, dz_two, att_one, dy, att_two, dy_two),
        small, up_out, down_out, out_out,
    )


def leave_kernel(info, gain_attn, ins, outs, features):
    recv, w_qkv, tokens, grad_mid = ins
    grad_tokens, dproj, gain_out = outs
    grad_tokens[...] = project_back(recv, info[3], gain_attn[...].reshape(1, WIDTH), tokens, grad_mid, w_qkv, features, dproj, gain_out)


def shape(*dims, dtype=BF16):
    return jax.ShapeDtypeStruct(dims, dtype)


def in_vmem(kernel, name, info, small, arrays, outs, scratch, flops, split={}):
    vmem = pl.BlockSpec(memory_space=pltpu.VMEM)
    hbm = pl.BlockSpec(memory_space=pl.ANY)
    ins, count = len(arrays), len(arrays) + len(outs)

    info = info if isinstance(info, tuple) else (info,)

    def body(*refs):
        known, refs = refs[: len(info)], refs[len(info) :]
        few, refs = refs[: len(small)], refs[len(small) :]
        far, near, sems, rest = refs[:count], refs[count : 2 * count], refs[2 * count], refs[2 * count + 1 :]
        held, blocks = [], []
        for i in range(ins):
            if i in split:
                own = sems.at[pl.ds(count + 6 * len(blocks), 6)]
                held.append(HeldBlocks(far[i], near[i], own, split[i]))
                blocks.append(held[-1])
                if len(blocks) == 2:
                    for c in range(FF // FF_BLOCK):
                        for one in blocks:
                            one.copy(c).start()
            else:
                held.append(Held(far[i], near[i], sems.at[i]))
        kept = [Kept(near[i], far[i], sems.at[i]) for i in range(ins, count)]
        if outs[0].shape == (SEQ, SLOT, 128):
            kept[0] = KeptSlots(near[ins], far[ins], sems.at[pl.ds(count + 12, 24)])
        for i, out in enumerate(outs):
            if out.shape == (FF, WIDTH):
                kept[i] = KeptBlocks(near[ins + i], far[ins + i], sems.at[pl.ds(count + 12, 6)])
        kernel(*known, *few, held, kept, *rest)
        for one in kept:
            if not one.started:
                one.flush()
        for one in held:
            one.ready()
        for one in kept:
            one.finish()

    return pl.pallas_call(
        body,
        out_shape=tuple(outs),
        in_specs=[pl.BlockSpec(memory_space=pltpu.SMEM)] * len(info) + [vmem] * len(small) + [hbm] * ins,
        out_specs=(hbm,) * len(outs),
        scratch_shapes=[pltpu.VMEM(x.shape, x.dtype) for x in (*arrays, *outs)]
        + [pltpu.SemaphoreType.DMA((count + 36,))]
        + scratch,
        compiler_params=pltpu.CompilerParams(vmem_limit_bytes=62 << 20),
        cost_estimate=pl.CostEstimate(flops=int(flops), bytes_accessed=16 << 20, transcendentals=1 << 20),
        name=name,
    )(*info, *small, *arrays)


LATE = 7168
CORE = 5


def weight_gradients(factors, small, up, down, out):
    mid_one, dh_one, mid_two, dh_two, act_one, dz_one, act_two, dz_two, att_one, dy_one, att_two, dy_two = factors
    for one in (dh_two, act_one, act_two):
        one.ready()

    def left(one, two):
        return jnp.concatenate([one, two], axis=0).T

    mid = left(mid_one[...], mid_two[...])

    def step_up(c, _):
        here = pl.ds(pl.multiple_of(c * 512, 512), 512)
        up[:, here] = dot(mid, jnp.concatenate([dh_one[:, here], dh_two[:, here]], axis=0)).astype(BF16)
        return 0

    lax.fori_loop(0, 6, step_up, 0)
    up.flush()
    dy = jnp.concatenate([dy_one[...], dy_two[...]], axis=0)
    out[0:WIDTH, :] = dot(left(att_one[...], att_two[...]), dy).astype(BF16)
    out[WIDTH:, :] = small.astype(BF16)
    out.flush()
    dz = jnp.concatenate([dz_one[...], dz_two[...]], axis=0)

    def step_down(c, _):
        here = pl.ds(pl.multiple_of(c * 512, 512), 512)
        down[here, :] = dot(left(act_one[:, here], act_two[:, here]), dz).astype(BF16)
        down.copy_of(c).start()
        return 0

    lax.fori_loop(0, 6, step_down, 0)


def grad_qkv_kernel(info, ins, outs):
    normed, dproj = ins
    left = normed[...].T
    dproj.ready()

    def step(c, _):
        result = dot(left, dproj[:, pl.ds(pl.multiple_of(c * 384, 384), 384)])
        for i in range(3):
            outs[0][3 * c + i] = result[:, 128 * i : 128 * i + 128]
        return 0

    lax.fori_loop(0, 6, step, 0)


def grad_qkv_both_kernel(info, gains, ins, outs):
    normed, dproj, before = ins
    left = normed[...].T
    dproj.ready(), before.ready()
    core = info[CORE]

    def step(c, _):
        result = dot(left, dproj[:, pl.ds(pl.multiple_of(c * 384, 384), 384)])
        for to, out in enumerate(outs):
            for half in range(2):

                @pl.when((half ^ core) == to)
                def _():
                    for i in range(3):
                        for part in range(3):
                            rows = slice(384 * half + 128 * part, 384 * half + 128 * part + 128)
                            value = result[rows, 128 * i : 128 * i + 128] + before[3 * c + i, rows, :]
                            at = pl.multiple_of(part * 2304 + (3 * c + i) * 128, 128)
                            out[pl.ds(at, 128), :] = value.astype(BF16)

        return 0

    lax.fori_loop(0, 6, step, 0)
    for out in outs:
        out[6912:6928, :] = gains[...].astype(BF16)


def widen_kernel(core, mine, other, out):
    half = pl.program_id(0) // 3

    def put(ref):
        for i in range(18):
            out[:, 128 * i : 128 * i + 128] = ref[128 * i : 128 * i + 128, :].astype(F32)

    @pl.when(half == core[0])
    def _():
        put(mine)

    @pl.when(half != core[0])
    def _():
        put(other)


def widen(core, mine, other):
    def place(own):
        def index(i, core):
            low = core[0] == (0 if own else 1)
            return (jnp.where(low, jnp.minimum(i, 2), jnp.maximum(i - 3, 0)), 0)

        return pl.BlockSpec((2304, 128), index)

    return pl.pallas_call(
        widen_kernel,
        out_shape=shape(WIDTH, 3 * WIDTH, dtype=F32),
        grid_spec=pltpu.PrefetchScalarGridSpec(
            num_scalar_prefetch=1,
            grid=(6,),
            in_specs=[place(True), place(False)],
            out_specs=pl.BlockSpec((128, 3 * WIDTH), lambda i, core: (i, 0)),
        ),
        compiler_params=pltpu.CompilerParams(vmem_limit_bytes=20 << 20),
        name="widen",
    )(core, mine, other)


def swap(value, bit):
    return lax.ppermute(value, "batch", [(i, i ^ bit) for i in range(4)])


def exchange(slots):
    return lax.all_to_all(slots, "seq", 0, 0)


def sum_cores(partial):
    mine, other = partial
    return (mine.astype(F32) + swap(other, 1).astype(F32)).astype(BF16)


CHIPS = 64


def across_chips(slots):
    groups = [[s * 4 + z * 2 + c for s in range(SEQ) for z in range(2)] for c in range(2)]
    return lax.all_to_all(slots, ("seq", "batch"), 0, 0, axis_index_groups=groups)


def positions(half, first_row, count):
    at = lax.broadcasted_iota(jnp.int32, (1, count), 1)
    block = at // HALF
    return first_row + block * ROWS + ((half + block) % 2) * HALF + at % HALF


def third_keys(recv, count):
    last = recv[SEQ - 1, ROWS + 64 : SLOT, :].astype(F32)[0:1].astype(jnp.int32)
    row = last + (SEQ - 1) * ROWS
    return jnp.concatenate([row] * (count // 128), axis=1)


def first_keys(at, second, third):
    return jnp.where(at < second, 0, jnp.where(at < third, second, third))


def attend_kernel(info, recv_far, out_low_far, out_f_far, lse_far, k_t_far, q_t_far, recv, out_low, out_f, lse, kv_t, q_t, sems, acc, *, devs):
    tile_rows = devs * HALF
    span = devs * ROWS
    active, half, second = info[0], info[1], info[2]

    @pl.when(active == 1)
    def _():
        parts = [
            Held(recv_far.at[8 * i : 8 * i + 8], recv.at[8 * i : 8 * i + 8], sems.at[i]) for i in range(4)
        ]
        fars = (k_t_far, q_t_far, out_low_far, out_f_far, lse_far)
        kept = [
            Kept(near, far, sems.at[4 + i])
            for i, (near, far) in enumerate(zip((kv_t.at[0:64], q_t, out_low, out_f, lse), fars))
        ]
        ones = (lax.broadcasted_iota(jnp.int32, (16, ROWS), 0) == 0).astype(BF16)
        for d in range(SEQ):
            parts[d // 8].ready()
            keys = slice(d * ROWS, (d + 1) * ROWS)
            kv_t[0:128, keys] = recv[d, 0:ROWS, :].T
            kv_t[128:144, keys] = ones
            q_t[0:64, d * HALF : (d + 1) * HALF] = recv[d, ROWS : ROWS + 64, :]
        q_t[64:128, :] = jnp.zeros((64, SEQ * HALF), BF16)
        kept[0].flush()
        kept[1].flush()

        third = third_keys(recv, tile_rows)

        def square_top(features):
            wide = features.astype(F32)
            return jnp.max(jnp.sum(wide * wide, axis=0, keepdims=True))

        key_top = jnp.float32(0.0)
        query_top = jnp.float32(0.0)
        for c in range(8):
            key_top = jnp.maximum(key_top, square_top(kv_t[0:64, 1024 * c : 1024 * c + 1024]))
        for c in range(4):
            query_top = jnp.maximum(query_top, square_top(q_t[0:64, 1024 * c : 1024 * c + 1024]))
        small = key_top * query_top < (SMALL / LOG2E) ** 2

        def one_tile(t, _):
            start = t * span
            columns = pl.ds(pl.multiple_of(t * tile_rows, tile_rows), tile_rows)
            at = positions(half, start, tile_rows)
            first = first_keys(at, second, third)
            acc[...] = jnp.zeros((80, tile_rows), F32)
            queries = q_t[:, columns]

            def update(kv, key_rows, left, mask):
                here = slice(left, tile_rows)
                weights = jnp.exp2(dot(kv, queries[:, here]) * LOG2E)
                if mask is not None:
                    weights = jnp.where(mask, weights, 0.0)
                acc[:, here] = acc[:, here] + dot(kv_t[64:144, key_rows], weights.astype(BF16))

            def step(j, _):
                def scores(c, k):
                    kv = recv[pl.ds(j * 8 + k * 2, 2), 0:ROWS, :].reshape(512, 128)
                    return dot(kv, queries[:, c : c + 1024])

                pieces = [(c, k) for c in range(0, tile_rows, 1024) for k in range(4)]
                ahead = scores(*pieces[0])
                for n, (c, k) in enumerate(pieces):
                    now, ahead = ahead, scores(*pieces[n + 1]) if n + 1 < len(pieces) else None
                    keys = pl.ds(pl.multiple_of(j * 2048 + k * 512, 512), 512)
                    part = dot(kv_t[64:144, keys], jnp.exp2(now * LOG2E).astype(BF16))
                    total = part if k == 0 else total + part
                    if k == 3:
                        acc[:, c : c + 1024] += total
                return 0

            lax.fori_loop(0, t, step, 0)
            acc[...] = jnp.where(first >= start, 0.0, acc[...])
            for i in range(devs // 2):
                left = 256 * i
                key_start = pl.multiple_of(start + 512 * i, 512)
                kv = recv[pl.ds(t * devs + 2 * i, 2), 0:ROWS, :].reshape(512, 128)
                key_at = key_start + lax.broadcasted_iota(jnp.int32, (512, 1), 0)
                allowed = (key_at >= first[:, left:]) & (key_at <= at[:, left:])
                update(kv, pl.ds(key_start, 512), left, allowed)
            total = acc[64:65, :]
            result = acc[0:64, :] / total
            out_f[:, columns] = result
            lse[:, columns] = jnp.log2(total)
            low = result.astype(BF16)
            for i in range(devs):
                out_low[t * devs + i] = low[:, i * HALF : (i + 1) * HALF]

            @pl.when(t == 0)
            def _():
                key_at = lax.broadcasted_iota(jnp.int32, (1, ROWS), 1)
                kv_t[64:144, 0:ROWS] = jnp.where(key_at >= second, kv_t[64:144, 0:ROWS], 0.0).astype(BF16)

            return 0

        def one_device(d, _):
            columns = pl.ds(pl.multiple_of(d * HALF, HALF), HALF)
            at = d * ROWS + (half + d) % 2 * HALF + lax.broadcasted_iota(jnp.int32, (1, HALF), 1)
            first = first_keys(at, second, third_keys(recv, HALF))
            queries = q_t[:, columns]

            def step(j, state):
                old_top, old_acc = state
                kv = recv[pl.ds(j * 2, 2), 0:ROWS, :].reshape(512, 128)
                key_at = j * 512 + lax.broadcasted_iota(jnp.int32, (512, 1), 0)
                allowed = (key_at >= first) & (key_at <= at)
                scores = jnp.where(allowed, dot(kv, queries) * LOG2E, LOW)
                new_top = jnp.maximum(old_top, jnp.max(scores, axis=0, keepdims=True))
                weights = jnp.exp2(scores - new_top).astype(BF16)
                keys = pl.ds(pl.multiple_of(j * 512, 512), 512)
                return new_top, old_acc * jnp.exp2(old_top - new_top) + dot(kv_t[64:144, keys], weights)

            state = (jnp.full((1, HALF), LOW, F32), jnp.zeros((80, HALF), F32))
            top, state = lax.fori_loop(0, d // 2 + 1, step, state)
            total = state[64:65, :]
            result = state[0:64, :] / total
            out_f[:, columns] = result
            lse[:, columns] = top + jnp.log2(total)
            out_low[d] = result.astype(BF16)
            return 0

        @pl.when(small)
        def _():
            lax.fori_loop(0, SEQ // devs, one_tile, 0)

        @pl.when(jnp.logical_not(small))
        def _():
            lax.fori_loop(0, SEQ, one_device, 0)

        for one in kept[2:]:
            one.flush()
        for one in kept:
            one.finish()


def attend(info, recv):
    devs = 8
    pairs = 17.8e6
    out_low, *rest = pl.pallas_call(
        functools.partial(attend_kernel, devs=devs),
        out_shape=(
            jax.ShapeDtypeStruct((SEQ, 64, HALF), BF16),
            jax.ShapeDtypeStruct((64, SEQ * HALF), F32),
            jax.ShapeDtypeStruct((1, SEQ * HALF), F32),
            jax.ShapeDtypeStruct((64, SEQ * ROWS), BF16),
            jax.ShapeDtypeStruct((128, SEQ * HALF), BF16),
        ),
        in_specs=[
            pl.BlockSpec(memory_space=pltpu.SMEM),
            pl.BlockSpec(memory_space=pl.ANY),
        ],
        out_specs=tuple(pl.BlockSpec(memory_space=pl.ANY) for _ in range(5)),
        scratch_shapes=[
            pltpu.VMEM((SEQ, SLOT, 128), BF16),
            pltpu.VMEM((SEQ, 64, HALF), BF16),
            pltpu.VMEM((64, SEQ * HALF), F32),
            pltpu.VMEM((1, SEQ * HALF), F32),
            pltpu.VMEM((144, SEQ * ROWS), BF16),
            pltpu.VMEM((128, SEQ * HALF), BF16),
            pltpu.SemaphoreType.DMA((9,)),
            pltpu.VMEM((80, devs * HALF), F32),
        ],
        compiler_params=pltpu.CompilerParams(vmem_limit_bytes=62 << 20),
        cost_estimate=pl.CostEstimate(
            flops=int(pairs * 1024), bytes_accessed=8 << 20, transcendentals=int(pairs)
        ),
        name="attend",
    )(info, recv)
    out_f, lse, kv_t, q_t = rest
    return out_low, recv, kv_t, q_t, out_f, lse


def attend_back_kernel(info, recv_far, kv_t_far, q_t_far, out_f_far, lse_far, grad_out_far, send_far, recv, kv_t, q_t, out_f, lse, grad_out, send, sems, grad_kv, do_t, grad_q, *, devs):
    tile_rows = devs * HALF
    span = devs * ROWS
    active, half, second = info[0], info[1], info[2]

    @pl.when(active == 1)
    def _():
        fars = (grad_out_far, recv_far, q_t_far, out_f_far, lse_far, kv_t_far)
        nears = (grad_out, recv, q_t, out_f, lse, kv_t)
        held = [Held(far, near, sems.at[i]) for i, (far, near) in enumerate(zip(fars, nears))]
        grad_kv[...] = jnp.zeros(grad_kv.shape, F32)
        held[0].ready()
        for d in range(SEQ):
            do_t[64:128, d * HALF : (d + 1) * HALF] = grad_out[d]
        do_t[0:64, :] = jnp.zeros((64, SEQ * HALF), BF16)
        for one in held:
            one.ready()

        third = third_keys(recv, tile_rows)

        def one_tile(t, _):
            start = t * span
            columns = pl.ds(pl.multiple_of(t * tile_rows, tile_rows), tile_rows)
            at = positions(half, start, tile_rows)
            first = first_keys(at, second, third)
            queries = q_t[:, columns]
            grads = do_t[:, columns]
            query_rows = queries.T
            grad_rows = grads.T
            delta = jnp.sum(
                grads[64:128, :].astype(F32) * out_f[:, columns], axis=0, keepdims=True
            )
            own_lse = lse[:, columns]
            far_lse = jnp.where(first >= start, -LOW, own_lse)
            grad_q[...] = jnp.zeros((64, tile_rows), F32)

            def update(kv, key_rows, left, row_lse, mask):
                here = slice(left, tile_rows)
                scores = dot(kv, queries[:, here]) * LOG2E
                probs = jnp.where(mask, jnp.exp2(scores - row_lse[:, here]), 0.0)
                grad_probs = dot(kv, grads[:, here])
                grad_scores = (probs * (grad_probs - delta[:, here])).astype(BF16)
                grad_kv[key_rows, :] += dot(grad_scores, query_rows[here, :]) + dot(
                    probs.astype(BF16), grad_rows[here, :]
                )
                grad_q[:, here] += dot(kv_t[0:64, key_rows], grad_scores)

            def step(j, _):
                kv = recv[pl.ds(j * 4, 4), 0:ROWS, :].reshape(1024, 128)
                key_at = j * 1024 + lax.broadcasted_iota(jnp.int32, (1024, 1), 0)
                update(kv, pl.ds(pl.multiple_of(j * 1024, 1024), 1024), 0, far_lse, key_at >= second)
                return 0

            lax.fori_loop(0, t * (span // 1024), step, 0)
            for i in range(devs // 2):
                left = 256 * i
                key_start = pl.multiple_of(start + 512 * i, 512)
                kv = recv[pl.ds(t * devs + 2 * i, 2), 0:ROWS, :].reshape(512, 128)
                key_at = key_start + lax.broadcasted_iota(jnp.int32, (512, 1), 0)
                allowed = (key_at >= first[:, left:]) & (key_at <= at[:, left:])
                update(kv, pl.ds(key_start, 512), left, own_lse, allowed)
            low = (grad_q[...] * HEAD_DIM**-0.5).astype(BF16)
            for i in range(devs):
                d = t * devs + i
                send[d, ROWS:, :] = low[:, i * HALF : (i + 1) * HALF]
                send[d, 0:ROWS, :] = grad_kv[pl.ds(pl.multiple_of(d * ROWS, ROWS), ROWS), :].astype(BF16)
            sending(t).start()
            return 0

        def sending(t):
            here = pl.ds(t * devs, devs)
            return pltpu.make_async_copy(send.at[here], send_far.at[here], sems.at[6 + t])

        def from_last(i, _):
            return one_tile(SEQ // devs - 1 - i, 0)

        lax.fori_loop(0, SEQ // devs, from_last, 0)
        for t in range(SEQ // devs):
            sending(t).wait()


def attend_back(info, recv, kv_t, q_t, out_f, lse, grad_out):
    devs = 8
    pairs = 17.8e6
    return pl.pallas_call(
        functools.partial(attend_back_kernel, devs=devs),
        out_shape=jax.ShapeDtypeStruct((SEQ, ROWS + 64, HALF), BF16),
        in_specs=[pl.BlockSpec(memory_space=pltpu.SMEM)]
        + [pl.BlockSpec(memory_space=pl.ANY)] * 6,
        out_specs=pl.BlockSpec(memory_space=pl.ANY),
        scratch_shapes=[
            pltpu.VMEM((SEQ, SLOT, 128), BF16),
            pltpu.VMEM((64, SEQ * ROWS), BF16),
            pltpu.VMEM((128, SEQ * HALF), BF16),
            pltpu.VMEM((64, SEQ * HALF), F32),
            pltpu.VMEM((1, SEQ * HALF), F32),
            pltpu.VMEM((SEQ, 64, HALF), BF16),
            pltpu.VMEM((SEQ, ROWS + 64, HALF), BF16),
            pltpu.SemaphoreType.DMA((14,)),
            pltpu.VMEM((SEQ * ROWS, 128), F32),
            pltpu.VMEM((128, SEQ * HALF), BF16),
            pltpu.VMEM((64, devs * HALF), F32),
        ],
        compiler_params=pltpu.CompilerParams(vmem_limit_bytes=62 << 20),
        cost_estimate=pl.CostEstimate(
            flops=int(pairs * 1024), bytes_accessed=8 << 20, transcendentals=int(pairs)
        ),
        name="attend_back",
    )(info, recv, kv_t, q_t, out_f, lse, grad_out)


def on_device(
    tokens,
    token_pos,
    token_pass,
    token_count,
    w_qkv,
    w_out,
    w_up,
    w_down,
    gain_attn,
    gain_mlp,
    pass_table,
    cotangent,
):
    here = lax.axis_index("seq")
    documents = (token_pos, token_pass, token_count)
    edge = jnp.where(here == 0, ROWS - 1, 0)
    second = here * ROWS + start_of(*documents, here, edge)
    third = third_start(start_of(*documents, here, ROWS - 1))
    group, place = here // 4, here % 4
    active = (place < 3).astype(jnp.int32)
    core = lax.axis_index("batch") % 2
    info = jnp.stack([active, (3 * group + place) % 2, second, here % 2, third, core])
    passes = token_pass
    table = jnp.pad(pass_table, ((0, 8 - PASSES), (0, 0)))
    gain_a, gain_m = gain_attn, gain_mlp
    stream_one = tokens[0]
    features = pltpu.VMEM((WIDTH, ROWS), BF16)
    acc = pltpu.VMEM((ROWS, WIDTH), F32)
    square = shape(ROWS, WIDTH)
    wide = shape(ROWS, WIDTH, dtype=F32)
    row = shape(1, WIDTH, dtype=F32)
    sent = shape(SEQ, SLOT, 128)
    sent_back = shape(SEQ, 64, 128)

    slots, normed_one = in_vmem(
        enter_kernel, "enter", documents, (gain_a,), (stream_one, w_qkv), (sent, square), [], 1e9
    )
    recv = exchange(slots)
    recv, passes, table, gain_m = lax.optimization_barrier((recv, passes, table, gain_m))
    saved_one = attend(info, recv)
    slots, normed_two, stream_two, att_one, mid_one, midn_one, hidden_one, act_one = in_vmem(
        turn_kernel,
        "turn",
        info,
        (passes, table, gain_a, gain_m),
        (exchange(saved_one[0]), stream_one, w_out, w_up, w_down, w_qkv),
        (sent, square, wide, square, wide, square, shape(ROWS, FF, dtype=F32), shape(ROWS, FF)),
        [features, acc],
        3.6e9,
        {3: 1, 4: 0},
    )
    saved_two = attend(info, exchange(slots))
    slots, mixed, att_two, midn_two, act_two, dh_two, dy_two, dmid_two, gain_m_two = in_vmem(
        crest_kernel,
        "crest",
        info,
        (gain_m,),
        (exchange(saved_two[0]), stream_two, w_out, w_up, w_down, cotangent[0]),
        (sent_back, square, square, square, shape(ROWS, FF), shape(ROWS, FF), square, wide, row),
        [features, acc, acc, pltpu.VMEM((ROWS, FF), F32), pltpu.VMEM((ROWS, WIDTH), BF16)],
        5e9,
        {3: 1, 4: 0},
    )
    back = exchange(slots)
    recv = exchange(attend_back(info, *saved_two[1:], back))
    slots, dproj_two, dmid_one, *early = in_vmem(
        return_kernel,
        "return",
        info,
        (passes, gain_a, gain_m, gain_m_two),
        (recv, w_qkv, stream_two, dmid_two, hidden_one, w_down, w_up, mid_one, w_out,
         midn_one, midn_two, dh_two, act_one, act_two, cotangent[0], att_one, att_two, dy_two),
        (sent_back, shape(ROWS, 3 * WIDTH), wide, shape(WIDTH, FF), shape(FF, WIDTH), shape(WIDTH + 16, WIDTH)),
        [features, acc, pltpu.VMEM((ROWS, WIDTH), BF16), pltpu.VMEM((ROWS, FF), BF16),
         pltpu.VMEM((ROWS, WIDTH), BF16), pltpu.VMEM((1, WIDTH), F32)],
        1e10,
        {5: 0, 6: 1},
    )
    back = exchange(slots)
    early = lax.psum(tuple(early), ("seq", "batch"))
    sent_one = attend_back(info, *saved_one[1:], back)
    recv = exchange(sent_one)
    grad_tokens, dproj_one, gain_a_one = in_vmem(
        leave_kernel,
        "leave",
        info,
        (gain_a,),
        (recv, w_qkv, stream_one, dmid_one),
        (wide, shape(ROWS, 3 * WIDTH), row),
        [features],
        1e9,
    )
    (grad_two,) = in_vmem(
        grad_qkv_kernel,
        "grad_qkv_two",
        info,
        (),
        (normed_two, dproj_two),
        (shape(18, WIDTH, 128, dtype=F32),),
        [],
        9e8,
    )
    late = in_vmem(
        grad_qkv_both_kernel,
        "grad_qkv",
        info,
        (jnp.pad(gain_a_one.reshape(6, 128), ((0, 10), (0, 0))),),
        (normed_one, dproj_one, grad_two),
        (shape(LATE, 128),) * 2,
        [],
        9e8,
    )
    late, early = lax.optimization_barrier((late, early))
    late = across_chips(sum_cores(late).reshape(CHIPS, -1, 128))
    tail = early[2][WIDTH:].astype(F32)
    early = (early[0].astype(F32), early[1].astype(F32), early[2][:WIDTH].astype(F32))
    late, early = lax.optimization_barrier((late, early))
    late = jnp.sum(late.astype(F32), axis=0).astype(BF16)
    whole = across_chips(jnp.broadcast_to(late[None], (CHIPS, *late.shape))).reshape(-1, 128)
    late = (whole, swap(whole, 1))
    grad_up, grad_down, grad_out = early
    gain_a_sum = late[0][6912:6918].reshape(WIDTH).astype(F32)
    return (
        mixed[None],
        grad_tokens[None],
        widen(info[CORE : CORE + 1], *late),
        grad_out,
        grad_up,
        grad_down,
        tail[PASSES] + gain_a_sum,
        tail[PASSES + 1],
        tail[:PASSES],
    )


def solution(mesh):
    return jax.shard_map(
        on_device,
        mesh=mesh,
        in_specs=(
            P("batch", "seq", None),
            P("batch", "seq"),
            P("batch", "seq"),
            P("batch", "seq"),
            P(),
            P(),
            P(),
            P(),
            P(),
            P(),
            P(),
            P("batch", "seq", None),
        ),
        out_specs=(
            P("batch", "seq", None),
            P("batch", "seq", None),
            P(),
            P(),
            P(),
            P(),
            P(),
            P(),
            P(),
        ),
        check_vma=False,
    )
```
